128 devices in a mesh: tm: 32 (over y, z, core), batch: 4 (over x).
Axes of the slice: x: 4, y: 4, z: 4, core: 2. Of those that a mesh axis runs over, the one named last changes fastest.
Arguments:
- frames: float32 [4, 64, 131072], P('batch', None, 'tm'), may hold values from -6 to 6
- clip_start: int32 [4, 131072], P('batch', 'tm'), may hold values from 0 to 131071, as said below
- code_ids: int32 [4, 65536], P('batch', 'tm'), may hold values from 0 to 2047
- cotangent: float32 [4, 64, 131072], P('batch', None, 'tm'), may hold values from -6 to 6
- enc_conv: float32 [4, 3, 64, 64], replicated, may hold values from -0.4375 to 0.4375
- enc_conv_bias: float32 [4, 64], replicated, may hold values from -2 to 2
- enc_proj: float32 [4, 64, 64], replicated, may hold values from -0.75 to 0.75
- enc_proj_bias: float32 [4, 64], replicated, may hold values from -2 to 2
- downscale_weight: float32 [4, 64, 64], replicated, may hold values from -0.375 to 0.375
- downscale_bias: float32 [64], replicated, may hold values from -2 to 2
- codebook: float32 [2048, 64], replicated, may hold values from -6 to 6
- up_weight: float32 [4, 64, 64], replicated, may hold values from -0.5 to 0.5
- up_bias: float32 [64], replicated, may hold values from -2 to 2
- dec_conv: float32 [4, 3, 64, 64], replicated, may hold values from -0.4375 to 0.4375
- dec_conv_bias: float32 [4, 64], replicated, may hold values from -2 to 2
- dec_proj: float32 [4, 64, 64], replicated, may hold values from -0.75 to 0.75
- dec_proj_bias: float32 [4, 64], replicated, may hold values from -2 to 2
Outputs:
- rebuilt: float32 [4, 64, 131072], P('batch', None, 'tm')
- frames_grad: float32 [4, 64, 131072], P('batch', None, 'tm')
- enc_conv_grad: float32 [4, 3, 64, 64], replicated
- enc_conv_bias_grad: float32 [4, 64], replicated
- enc_proj_grad: float32 [4, 64, 64], replicated
- enc_proj_bias_grad: float32 [4, 64], replicated
- down_grad: float32 [4, 64, 64], replicated
- down_bias_grad: float32 [64], replicated
- codebook_grad: float32 [2048, 64], replicated
- up_grad: float32 [4, 64, 64], replicated
- up_bias_grad: float32 [64], replicated
- dec_conv_grad: float32 [4, 3, 64, 64], replicated
- dec_conv_bias_grad: float32 [4, 64], replicated
- dec_proj_grad: float32 [4, 64, 64], replicated
- dec_proj_bias_grad: float32 [4, 64], replicated
The draws below stay inside these ranges and needn't reach their ends.
Inputs may be any that keep to these rules, and one draw needn't show every extreme that they name: clip_start[w, t] is the first frame, within window w, of the clip that holds frame t: it is at most t and does not fall along t; the last frame of every window starts a clip of its own.
All inputs are finite; a program needn't handle non-finite values.
Results may differ from the reference program's by a relative error of at most 0.0003.
Values sent between devices are 32-bit elements; how exact they have to be, the bound alone decides.
No kernel may reach another device: no remote copies, remote signals or barrier semaphores. Data moves between devices by JAX's collectives and lax.ppermute only.
A program may use at most 256 MiB of HBM per device.

```python
import jax
import jax.numpy as jnp
from jax import lax

WIDTH = 64
CODES = 2048
BLOCKS = 4
FR_DEV = 4096
WINDOWS = 4
WIN_LEN = 131072
LATENT = 65536


def draw_clip_start(key, part):
    key = jax.random.fold_in(key, 7)
    key_list = jax.random.split(key, 7)
    position = jnp.arange(WIN_LEN, dtype=jnp.int32)[None, :]
    opening = jax.random.randint(key_list[0], (WINDOWS, 1), 1, FR_DEV)
    closing = jax.random.randint(key_list[1], (WINDOWS, 1), WIN_LEN - FR_DEV + 1, WIN_LEN)
    outer_breaks = jax.random.randint(key_list[2], (WINDOWS, WIN_LEN), 0, 48) == 0
    inside = (position > opening) & (position < closing)
    spanning = outer_breaks & ~inside | (position == opening) | (position == closing)
    spread_breaks = jax.random.randint(key_list[3], (WINDOWS, WIN_LEN), 0, FR_DEV) == 0
    devices = WIN_LEN // FR_DEV
    edge_reach = jax.random.randint(key_list[4], (WINDOWS, devices), 1, 28)
    edge_side = jax.random.randint(key_list[5], (WINDOWS, devices), 0, 2) * 2 - 1
    edge_pos = jnp.arange(devices, dtype=jnp.int32)[None, :] * FR_DEV + edge_side * edge_reach
    edge_pos = jnp.clip(edge_pos, 0, WIN_LEN - 1).astype(jnp.int32)
    window_rows = jnp.broadcast_to(jnp.arange(WINDOWS, dtype=jnp.int32)[:, None], edge_pos.shape)
    edge_breaks = jnp.zeros((WINDOWS, WIN_LEN), dtype=bool).at[window_rows, edge_pos].set(True)
    scattered = spread_breaks | edge_breaks
    span_window = jax.random.randint(key_list[6], (), 0, WINDOWS)
    is_span = (jnp.arange(WINDOWS, dtype=jnp.int32) == span_window)[:, None]
    breaks = jnp.where(is_span, spanning, scattered) | (position == 0) | (position == WIN_LEN - 1)
    starts = jnp.where(breaks, position, 0)
    return lax.cummax(starts, axis=1).astype(jnp.int32)


def place_ends(array, own_key, least, top_value):
    longest = array.shape.index(max(array.shape))
    spots = []
    for shift in (0, 1):
        where = [jax.random.randint(jax.random.fold_in(own_key, axis), (), 0, length) for axis, length in enumerate(array.shape)]
        where[longest] = (where[longest] + shift) % array.shape[longest]
        spots.append(tuple(where))
    return array.at[spots[0]].set(least).at[spots[1]].set(top_value)


def block_scale(key, shape, shards, least, top_value):
    level, own = 1.0, jax.random.fold_in(key, 6)
    for dim, blocks in shards:
        heights = jnp.exp(jax.random.uniform(jax.random.fold_in(own, dim), (blocks,), jnp.float32, least / len(shards), top_value / len(shards)))
        level = level * jnp.repeat(heights, shape[dim] // blocks).reshape([-1 if axis == dim else 1 for axis in range(len(shape))])
    return level


def normal_values(rng, dims, scale, bound, cuts=(), kind=jnp.bfloat16):
    entries = scale * jax.random.normal(rng, dims, jnp.float32)
    if cuts:
        entries = entries * block_scale(rng, dims, cuts, -0.22, 0.18)
    return jnp.clip(entries, -bound, bound).astype(kind)


def setup_inputs(seed: int = 0) -> dict:
    key_of = jax.random.split(jax.random.key(seed), 18)
    frames = normal_values(key_of[0], (WINDOWS, WIDTH, WIN_LEN), 1.0, 6.0, ((0, 4), (2, 32)), jnp.float32)
    clip_start = draw_clip_start(jax.random.fold_in(key_of[17], 71), 0)
    code_ids = place_ends(jax.random.randint(key_of[2], (WINDOWS, LATENT), 0, CODES), jax.random.fold_in(key_of[2], 1), 0, CODES - 1).astype(jnp.int32)
    cotangent = normal_values(key_of[3], (WINDOWS, WIDTH, WIN_LEN), 1.0, 6.0, ((0, 4), (2, 32)), jnp.float32)
    enc_conv = normal_values(key_of[4], (BLOCKS, 3, WIDTH, WIDTH), (3 * WIDTH) ** -0.5, 0.4375, (), jnp.float32)
    enc_conv_bias = normal_values(key_of[5], (BLOCKS, WIDTH), 0.3, 2.0, (), jnp.float32)
    enc_proj = normal_values(key_of[6], (BLOCKS, WIDTH, WIDTH), WIDTH ** -0.5, 0.75, (), jnp.float32)
    enc_proj_bias = normal_values(key_of[7], (BLOCKS, WIDTH), 0.3, 2.0, (), jnp.float32)
    downscale_weight = normal_values(key_of[8], (4, WIDTH, WIDTH), (4 * WIDTH) ** -0.5, 0.375, (), jnp.float32)
    downscale_bias = normal_values(key_of[9], (WIDTH,), 0.3, 2.0, (), jnp.float32)
    codebook = normal_values(key_of[10], (CODES, WIDTH), 1.0, 6.0, (), jnp.float32)
    up_weight = normal_values(key_of[11], (4, WIDTH, WIDTH), (2 * WIDTH) ** -0.5, 0.5, (), jnp.float32)
    up_bias = normal_values(key_of[12], (WIDTH,), 0.3, 2.0, (), jnp.float32)
    dec_conv = normal_values(key_of[13], (BLOCKS, 3, WIDTH, WIDTH), (3 * WIDTH) ** -0.5, 0.4375, (), jnp.float32)
    dec_conv_bias = normal_values(key_of[14], (BLOCKS, WIDTH), 0.3, 2.0, (), jnp.float32)
    dec_proj = normal_values(key_of[15], (BLOCKS, WIDTH, WIDTH), WIDTH ** -0.5, 0.75, (), jnp.float32)
    dec_proj_bias = normal_values(key_of[16], (BLOCKS, WIDTH), 0.3, 2.0, (), jnp.float32)
    return dict(frames=frames, clip_start=clip_start, code_ids=code_ids, cotangent=cotangent, enc_conv=enc_conv, enc_conv_bias=enc_conv_bias, enc_proj=enc_proj, enc_proj_bias=enc_proj_bias, downscale_weight=downscale_weight, downscale_bias=downscale_bias, codebook=codebook, up_weight=up_weight, up_bias=up_bias, dec_conv=dec_conv, dec_conv_bias=dec_conv_bias, dec_proj=dec_proj, dec_proj_bias=dec_proj_bias)


COMMIT = 0.02
DILATIONS = (1, 3, 9, 27)

@jax.custom_vjp
def low(v):
    return lax.optimization_barrier(v.astype(jnp.bfloat16)).astype(jnp.float32)

@jax.custom_vjp
def low_back(v):
    return v

def low_keep(v):
    return (low(v), None)

def low_pass(kept, grad):
    return (grad,)

def back_keep(v):
    return (v, None)

def back_low(kept, grad):
    return (low(grad),)
low.defvjp(low_keep, low_pass)
low_back.defvjp(back_keep, back_low)

def matmul(weight, value_entries):
    return jnp.dot(weight, value_entries, precision=lax.Precision.HIGHEST)

def shifted(value_entries, offset, fill):
    length = value_entries.shape[-1]
    reach = abs(offset)
    padded = jnp.pad(value_entries, [(0, 0)] * (value_entries.ndim - 1) + [(reach, reach)], constant_values=fill)
    return lax.slice_in_dim(padded, reach + offset, reach + offset + length, axis=value_entries.ndim - 1)

def conv_dilated(value_entries, filter_weight, bias_vector, packed_clip_row, dilation):
    result = bias_vector[:, None] + jnp.zeros_like(value_entries)
    for k in range(3):
        offset = (k - 1) * dilation
        inside = (shifted(packed_clip_row, offset, -1) == packed_clip_row).astype(value_entries.dtype)
        result = result + matmul(filter_weight[k], shifted(value_entries, offset, 0.0)) * inside[None, :]
    return result

def res_stack(value_entries, conv, conv_bias, proj, proj_bias, packed_clip_row, dilations):
    for section, dilation in enumerate(dilations):
        hidden = conv_dilated(jax.nn.gelu(value_entries), conv[section], conv_bias[section], packed_clip_row, dilation)
        value_entries = value_entries + matmul(proj[section], jax.nn.gelu(hidden)) + proj_bias[section][:, None]
    return value_entries

def strided_reduce(value_entries, filter_weight, bias_vector, packed_clip_row):
    length = value_entries.shape[-1]
    padded = jnp.pad(value_entries, ((0, 0), (1, 2)))
    clip_pad = jnp.pad(packed_clip_row, (1, 2), constant_values=-1)
    centre = packed_clip_row[0::2]
    result = bias_vector[:, None] + jnp.zeros((value_entries.shape[0], length // 2), value_entries.dtype)
    for k in range(4):
        inside = (clip_pad[k:k + length:2] == centre).astype(value_entries.dtype)
        result = result + matmul(filter_weight[k], padded[:, k:k + length:2]) * inside[None, :]
    return result

def upsample(latent, filter_weight, bias_vector, packed_clip_row):
    length = packed_clip_row.shape[0]
    clip_pad = jnp.pad(packed_clip_row, (1, 2), constant_values=-1)
    centre = packed_clip_row[0::2]
    summed = jnp.zeros((latent.shape[0], length + 3), latent.dtype)
    for k in range(4):
        inside = (clip_pad[k:k + length:2] == centre).astype(latent.dtype)
        summed = summed.at[:, k:k + length:2].add(matmul(filter_weight[k], latent) * inside[None, :])
    return summed[:, 1:length + 1] + bias_vector[:, None]

def encode(weights, frames_win, packed_clip_row):
    enc_conv, enc_conv_bias, enc_proj, enc_proj_bias, downscale_weight, downscale_bias = weights[:6]
    encoder_output = res_stack(frames_win, enc_conv, enc_conv_bias, enc_proj, enc_proj_bias, packed_clip_row, DILATIONS)
    return strided_reduce(encoder_output, downscale_weight, downscale_bias, packed_clip_row)

def window_pass(params, frames_win, packed_clip_row, code_row, cot_win):
    fixed_latent = encode(params, frames_win, packed_clip_row)
    fixed_code = jnp.transpose(params[6][code_row])

    def forward(weights, frames_in):
        latent = encode(weights, frames_in, packed_clip_row)
        quantized = fixed_code + (latent - fixed_latent)
        upsampled = upsample(quantized, weights[7], weights[8], packed_clip_row)
        rebuilt = res_stack(upsampled, weights[9], weights[10], weights[11], weights[12], packed_clip_row, DILATIONS[::-1])
        picked = jnp.transpose(weights[6][code_row])
        code_gap = fixed_latent - picked
        commit_gap = latent - fixed_code
        penalty = jnp.sum(code_gap * code_gap) + COMMIT * jnp.sum(commit_gap * commit_gap)
        return (rebuilt, penalty)
    (rebuilt, penalty), pullback = jax.vjp(forward, params, frames_win)
    weight_grads, frames_grad = pullback((cot_win, jnp.ones_like(penalty)))
    return (rebuilt, frames_grad, weight_grads)

def reference(frames, clip_start, code_ids, cotangent, enc_conv, enc_conv_bias, enc_proj, enc_proj_bias, downscale_weight, downscale_bias, codebook, up_weight, up_bias, dec_conv, dec_conv_bias, dec_proj, dec_proj_bias):
    params = (enc_conv, enc_conv_bias, enc_proj, enc_proj_bias, downscale_weight, downscale_bias, codebook, up_weight, up_bias, dec_conv, dec_conv_bias, dec_proj, dec_proj_bias)

    def step_fn(running, window):
        frames_win, packed_clip_row, code_row, cot_win = window
        rebuilt, frames_grad, grads = window_pass(params, frames_win, packed_clip_row, code_row, cot_win)
        return (jax.tree.map(jnp.add, running, grads), (rebuilt, frames_grad))
    zeroed = jax.tree.map(jnp.zeros_like, params)
    totals, (rebuilt, frames_grad) = lax.scan(step_fn, zeroed, (frames, clip_start, code_ids, cotangent))
    return (rebuilt, frames_grad, totals[0], totals[1], totals[2], totals[3], totals[4], totals[5], totals[6], totals[7], totals[8], totals[9], totals[10], totals[11], totals[12])
```

```python
import functools

import jax
import jax.numpy as jnp
from jax import lax
from jax.experimental import pallas as pl
from jax.experimental.pallas import tpu as pltpu
from jax.sharding import PartitionSpec as P

COMMIT = 0.02
DILATIONS = (1, 3, 9, 27)
BF = jnp.bfloat16
F32 = jnp.float32
CH = 64
CODES = 2048
CORE = 4096
HALO = 128
EXT = CORE + 2 * HALO
HCORE = CORE // 2
HEXT = EXT // 2
STEP = 512
G0 = 0.7978845608028654
G1 = G0 * 0.044715
MB = 2**20
GRAD_PROJ = 384
GRAD_PAIR = 512
GRAD_BIAS = 640
GRAD_ROWS = 704


def dot(a, b):
    return jnp.dot(a, b, preferred_element_type=F32)


def dot_nt(a, b):
    return lax.dot_general(a, b, (((1,), (1,)), ((), ())), preferred_element_type=F32)


def split(v):
    hi = v.astype(BF)
    return hi, (v - hi.astype(F32)).astype(BF)


def gelu_both(v):
    s = v * v
    t = jnp.tanh(v * (G0 + G1 * s))
    cdf = 0.5 + 0.5 * t
    slope = cdf + (0.5 * v) * (1.0 - t * t) * (G0 + (3.0 * G1) * s)
    return v * cdf, slope


def tile_rows(rows, times):
    return jnp.concatenate([rows] * times, axis=0)


def aligned(start):
    return start if isinstance(start, int) else pl.multiple_of(start, 128)


def lanes(ref, start, size, rows=slice(None)):
    return ref[rows, pl.ds(aligned(start), size)]


def wrap(start, length):
    return start % length if isinstance(start, int) else lax.rem(start + length, length)


def from_left(ref, rows, start, size, offset, length):
    win = jnp.concatenate(
        [lanes(ref, wrap(start - 128, length), 128, rows), lanes(ref, start, size, rows)], axis=1
    )
    return pltpu.roll(win, offset, 1)[:, 128:]


def from_right(ref, rows, start, size, offset, length):
    win = jnp.concatenate(
        [lanes(ref, start, size, rows), lanes(ref, wrap(start + size, length), 128, rows)], axis=1
    )
    return pltpu.roll(win, size + 128 - offset, 1)[:, :size]


def sweep(fn, step=STEP):
    def body(i, carry):
        fn(i * step, step, True)
        return carry

    lax.fori_loop(0, CORE // step, body, 0)
    fn(CORE, 2 * HALO, False)


def half_sweep(fn, step=STEP // 2):
    def body(i, carry):
        fn(i * step, step, True)
        return carry

    lax.fori_loop(0, HCORE // step, body, 0)
    fn(HCORE, HALO, False)


def lane_fold(v):
    out = v[:, :128]
    for i in range(1, v.shape[1] // 128):
        out = out + v[:, i * 128 : (i + 1) * 128]
    return out


def selector():
    row = lax.broadcasted_iota(jnp.int32, (256, 256), 0)
    col = lax.broadcasted_iota(jnp.int32, (256, 256), 1)
    source = jnp.where(col < 128, 2 * col, 2 * (col - 128) + 1)
    return jnp.where(row == source, 1.0, 0.0).astype(BF)


def prep_kernel(
    ec, ecb, ep, epb, dw, db, cb, uw, ub, dc, dcb, dp, dpb,
    wf, wb, pf, pb, dg, ds_, ug, us, cbt, bias,
):
    def forms(w):
        hi, lo = split(w)
        return jnp.concatenate([hi, hi, lo], axis=1)

    def stacked(w):
        hi, lo = split(w)
        return jnp.concatenate([hi, lo], axis=0)

    def column(row):
        return jnp.broadcast_to(row, (128, CH)).T

    for n, (conv, cbias, proj, pbias) in enumerate(((ec, ecb, ep, epb), (dc, dcb, dp, dpb))):
        for b in range(4):
            at = 4 * n + b
            wf[at] = forms(conv[b].reshape(3 * CH, CH))
            wb[at] = stacked(jnp.concatenate([conv[b, k].T for k in range(3)], axis=1))
            pf[at] = forms(proj[b])
            pb[at] = forms(proj[b].T)
            bias[2 * at] = column(cbias[b : b + 1, :])
            bias[2 * at + 1] = column(pbias[b : b + 1, :])
    bias[16] = column(db[...])
    bias[17] = column(ub[...])
    dg[...] = stacked(jnp.concatenate([dw[k] for k in range(4)], axis=1))
    ds_[...] = forms(jnp.concatenate([dw[k].T for k in range(4)], axis=0))
    ug[...] = stacked(jnp.concatenate([uw[k].T for k in range(4)], axis=1))
    us[...] = forms(jnp.concatenate([uw[k] for k in range(4)], axis=0))
    cbt[...] = stacked(cb[...].T)


def stack_forward(x_ref, z_refs, blocks, dils, wf, pf, bias, mf, keep, last):
    def enter(value, start, size, b):
        act, slope = gelu_both(value)
        hi, lo = split(act)
        a_ref, gx_ref, _, _ = keep(b)
        a_ref[:CH, pl.ds(aligned(start), size)] = hi
        a_ref[CH:, pl.ds(aligned(start), size)] = lo
        gx_ref[:, pl.ds(aligned(start), size)] = slope
        z_refs[b % 2][:, pl.ds(aligned(start), size)] = dot(
            wf[blocks + b], jnp.concatenate([hi, lo, hi], axis=0)
        )

    def first(start, size, core):
        enter(lanes(x_ref, start, size), start, size, 0)

    sweep(first)
    for b in range(4):
        d = dils[b]
        m = DILATIONS.index(d)
        z_ref = z_refs[b % 2]

        def step(start, size, core, b=b, d=d, m=m, z_ref=z_ref):
            _, _, u_ref, gh_ref = keep(b)
            times = size // 128
            left = tile_rows(lanes(mf, start, size, slice(16 * m, 16 * m + 8)), 8)
            right = tile_rows(lanes(mf, start, size, slice(16 * m + 8, 16 * m + 16)), 8)
            cb = jnp.concatenate([bias[2 * (blocks + b)]] * times, axis=1)
            hidden = lanes(z_ref, start, size, slice(CH, 2 * CH)) + cb
            hidden = hidden + left * from_left(z_ref, slice(0, CH), start, size, d, EXT)
            hidden = hidden + right * from_right(z_ref, slice(2 * CH, 3 * CH), start, size, d, EXT)
            act, slope = gelu_both(hidden)
            hi, lo = split(act)
            u_ref[:CH, pl.ds(aligned(start), size)] = hi
            u_ref[CH:, pl.ds(aligned(start), size)] = lo
            gh_ref[:, pl.ds(aligned(start), size)] = slope
            pbias = jnp.concatenate([bias[2 * (blocks + b) + 1]] * times, axis=1)
            out = (
                lanes(x_ref, start, size)
                + dot(pf[blocks + b], jnp.concatenate([hi, lo, hi], axis=0))
                + pbias
            )
            if b < 3:
                x_ref[:, pl.ds(aligned(start), size)] = out
                enter(out, start, size, b + 1)
            else:
                last(out, start, size, core)

        sweep(step)


def stack_backward(g_ref, gh_refs, blocks, dils, wb, pb, mb, keep, acc, finish, last):
    dk1, dk2, dpa, csum, psum = acc

    def enter(grad, start, size, core, b):
        _, _, u_ref, slope_ref = keep(b)
        hi, lo = split(grad)
        q = dot(pb[blocks + b], jnp.concatenate([hi, lo, hi], axis=0))
        gh = lanes(slope_ref, start, size) * q
        ghi, glo = split(gh)
        gh_refs[b % 2][:CH, pl.ds(aligned(start), size)] = ghi
        gh_refs[b % 2][CH:, pl.ds(aligned(start), size)] = glo
        if core:
            dpa[b] += dot_nt(jnp.concatenate([hi, lo], axis=0), lanes(u_ref, start, size))
            csum[b] += lane_fold(gh)
            psum[b] += lane_fold(grad)

    for ref in acc:
        ref[...] = jnp.zeros(ref.shape, ref.dtype)

    def first(start, size, core):
        enter(lanes(g_ref, start, size), start, size, core, 3)

    sweep(first)
    for b in (3, 2, 1, 0):
        d = dils[b]
        m = DILATIONS.index(d)
        gh_ref = gh_refs[b % 2]

        def step(start, size, core, b=b, d=d, m=m, gh_ref=gh_ref):
            a_ref, gx_ref, _, _ = keep(b)
            left = tile_rows(lanes(mb, start, size, slice(32 * m, 32 * m + 16)), 4)
            right = tile_rows(lanes(mb, start, size, slice(32 * m + 16, 32 * m + 32)), 4)
            parts = []
            for rows in (slice(0, CH), slice(CH, 2 * CH)):
                parts.append(
                    jnp.concatenate(
                        [
                            from_right(gh_ref, rows, start, size, d, EXT) * right,
                            lanes(gh_ref, start, size, rows),
                            from_left(gh_ref, rows, start, size, d, EXT) * left,
                        ],
                        axis=0,
                    )
                )
            ghi, glo = parts
            both = dot(wb[blocks + b], ghi)
            ga = both[:CH] + both[CH:] + dot(wb[blocks + b, :CH], glo)
            if core:
                act = lanes(a_ref, start, size)
                dk1[b] += dot_nt(ghi, act)
                dk2[b] += dot_nt(glo, act[:CH])
            out = lanes(g_ref, start, size) + lanes(gx_ref, start, size) * ga
            if b > 0:
                g_ref[:, pl.ds(aligned(start), size)] = out
                enter(out, start, size, core, b - 1)
            else:
                last(out, start, size, core)

        sweep(step)
    for b in range(4):
        dk = dk1[b, :, :CH] + dk1[b, :, CH:] + dk2[b]
        dp = dpa[b, :CH, :CH] + dpa[b, CH:, :CH] + dpa[b, :CH, CH:]
        finish(b, dk, dp, csum[b], psum[b])


def store_grads(grads):
    kept = {}

    def finish(b, dk, dp, csum, psum):
        kept[b] = (dk, dp)
        if b % 2:
            at = b // 2
            grads[at * 192 : (at + 1) * 192, :] = jnp.concatenate([kept[b - 1][0], dk], axis=1)
            grads[GRAD_PROJ + at * CH : GRAD_PROJ + (at + 1) * CH, :] = jnp.concatenate(
                [kept[b - 1][1], dp], axis=1
            )
        put_column(grads, 2 * b, csum)
        put_column(grads, 2 * b + 1, psum)

    return finish


def put_column(grads, at, folded):
    lane = lax.broadcasted_iota(jnp.int32, (CH, 128), 1)
    total = jnp.sum(folded, axis=1, keepdims=True)
    grads[GRAD_BIAS:, :] = jnp.where(lane == at, total, grads[GRAD_BIAS:, :])


def to_halves(value, sel, e_ref, o_ref, start, size):
    hi, lo = split(value)
    both = jnp.concatenate([hi, lo], axis=0)
    half = start // 2
    for i in range(size // 256):
        out = dot(both[:, i * 256 : (i + 1) * 256], sel).astype(BF)
        e_ref[:, pl.ds(aligned(half + i * 128), 128)] = out[:, :128]
        o_ref[:, pl.ds(aligned(half + i * 128), 128)] = out[:, 128:]


def pair_stack(e_ref, o_ref, mhb, start, size):
    masks = [tile_rows(lanes(mhb, start, size, slice(16 * i, 16 * i + 16)), 4) for i in range(3)]
    parts = []
    for rows in (slice(0, CH), slice(CH, 2 * CH)):
        parts.append(
            jnp.concatenate(
                [
                    from_left(o_ref, rows, start, size, 1, HEXT) * masks[0],
                    lanes(e_ref, start, size, rows),
                    lanes(o_ref, start, size, rows) * masks[1],
                    from_right(e_ref, rows, start, size, 1, HEXT) * masks[2],
                ],
                axis=0,
            )
        )
    return parts


def pair_gather(w, parts):
    both = dot(w[...], parts[0])
    return both[:CH] + both[CH:] + dot(w[:CH], parts[1])


def spread(w, hl_ref, mh, z_ref, sel, bias_tile, x_ref):
    def first(start, size, core):
        both = lanes(hl_ref, start, size)
        z = dot(w[...], jnp.concatenate([both, both[:CH]], axis=0))
        masks = [tile_rows(lanes(mh, start, size, slice(8 * i, 8 * i + 8)), 8) for i in range(3)]
        at = pl.ds(aligned(start), size)
        z_ref[0:64, at] = z[0:64] * masks[0]
        z_ref[64:128, at] = z[64:128]
        z_ref[128:192, at] = z[128:192] * masks[1]
        z_ref[192:256, at] = z[192:256] * masks[2]

    half_sweep(first)

    def second(start, size, core):
        even = lanes(z_ref, start, size, slice(64, 128)) + from_left(
            z_ref, slice(192, 256), start, size, 1, HEXT
        )
        odd = lanes(z_ref, start, size, slice(128, 192)) + from_right(
            z_ref, slice(0, 64), start, size, 1, HEXT
        )
        ehi, elo = split(even)
        ohi, olo = split(odd)
        for i in range(size // 128):
            cut = slice(i * 128, (i + 1) * 128)
            rows = jnp.concatenate(
                [
                    jnp.concatenate([ehi[:, cut], ohi[:, cut]], axis=1),
                    jnp.concatenate([elo[:, cut], olo[:, cut]], axis=1),
                ],
                axis=0,
            )
            out = dot_nt(rows, sel)
            out = out[:CH] + out[CH:]
            if bias_tile is not None:
                out = out + jnp.concatenate([bias_tile, bias_tile], axis=1)
            x_ref[:, pl.ds(aligned(2 * start + 256 * i), 256)] = out

    half_sweep(second)


def one_hot(ids_row, first, count):
    row = lax.broadcasted_iota(jnp.int32, (count, ids_row.shape[1]), 0) + first
    return jnp.where(row == ids_row, 1.0, 0.0).astype(BF)


def encode_kernel(
    frames, lo, hi, clip, codes, wf, pf, dg, cbt, bias,
    mf, mb, mh, mhb, a_out, gx_out, u_out, gh_out, f_hi, f_lo, latent, chosen, chosen_hl, cbg,
    x_ref, z0, z1, clip_ref, e_ref, o_ref, d_ref, ids_ref,
):
    sel = selector()
    x_ref[:, :CORE] = frames[...]
    x_ref[:, CORE : CORE + HALO] = hi[:CH]
    x_ref[:, CORE + HALO :] = lo[:CH]
    clip_ref[:, :CORE] = jnp.broadcast_to(clip[...].astype(F32), (8, CORE))
    clip_ref[:, CORE : CORE + HALO] = jnp.broadcast_to(hi[128:129], (8, HALO))
    clip_ref[:, CORE + HALO :] = jnp.broadcast_to(lo[128:129], (8, HALO))
    ids_ref[:, :HCORE] = jnp.broadcast_to(codes[...], (8, HCORE))
    ids_ref[:, HCORE:] = jnp.broadcast_to((hi[129:130] + lo[129:130]).astype(jnp.int32), (8, HALO))

    def links(start, size, core):
        at = pl.ds(aligned(start), size)
        here = lanes(clip_ref, start, size)

        def same(other):
            return jnp.where(other == here, 1.0, 0.0)

        for m, d in enumerate(DILATIONS):
            left = same(from_left(clip_ref, slice(None), start, size, d, EXT))
            right = same(from_right(clip_ref, slice(None), start, size, d, EXT))
            mf[16 * m : 16 * m + 8, at] = left
            mf[16 * m + 8 : 16 * m + 16, at] = right
            mb[32 * m : 32 * m + 16, at] = tile_rows(left, 2).astype(BF)
            mb[32 * m + 16 : 32 * m + 32, at] = tile_rows(right, 2).astype(BF)
            if m == 0:
                two = same(from_right(clip_ref, slice(None), start, size, 2, EXT))
                rows = jnp.concatenate([left, right, two, two], axis=0).astype(BF)
                half = start // 2
                for i in range(size // 256):
                    out = dot(rows[:, i * 256 : (i + 1) * 256], sel)[:, :128]
                    hat = pl.ds(aligned(half + 128 * i), 128)
                    mh[:, hat] = out[:24]
                    for n in range(3):
                        mhb[16 * n : 16 * n + 16, hat] = tile_rows(
                            out[8 * n : 8 * n + 8], 2
                        ).astype(BF)

    sweep(links)

    def pick(start, size, core):
        at = pl.ds(aligned(start), size)
        both = dot(cbt[...], one_hot(lanes(ids_ref, start, size, slice(0, 1)), 0, CODES))
        chosen[:, at] = both[:CH] + both[CH:]
        chosen_hl[:, at] = both.astype(BF)

    half_sweep(pick)

    def keep(b):
        return a_out.at[b], gx_out.at[b], u_out.at[b], gh_out.at[b]

    def last(out, start, size, core):
        to_halves(out, sel, e_ref, o_ref, start, size)

    stack_forward(x_ref, (z0, z1), 0, DILATIONS, wf, pf, bias, mf, keep, last)

    def down(start, size, core):
        at = pl.ds(aligned(start), size)
        parts = pair_stack(e_ref, o_ref, mhb, start, size)
        value = pair_gather(dg, parts) + jnp.concatenate([bias[16]] * (size // 128), axis=1)
        latent[:, at] = value
        if core:
            f_hi[:, at] = parts[0]
            f_lo[:, at] = parts[1]
            dhi, dlo = split(2.0 * (lanes(chosen, start, size) - value))
            d_ref[:CH, at] = dhi
            d_ref[CH:, at] = dlo

    half_sweep(down)

    def codes_back(i, carry):
        parts = []
        for side in range(2):
            hot = one_hot(ids_ref[0:1, :HCORE], i * 256 + side * (CODES // 2), 256)
            out = dot_nt(hot, d_ref[...])
            parts.append(out[:, :CH] + out[:, CH:])
        cbg[pl.ds(pl.multiple_of(i * 256, 256), 256), :] = jnp.concatenate(parts, axis=1)
        return carry

    lax.fori_loop(0, CODES // 512, codes_back, 0)


def sum_refs():
    return [
        pltpu.VMEM((4, 3 * CH, 2 * CH), F32),
        pltpu.VMEM((4, 3 * CH, CH), F32),
        pltpu.VMEM((4, 2 * CH, 2 * CH), F32),
        pltpu.VMEM((4, CH, 128), F32),
        pltpu.VMEM((4, CH, 128), F32),
    ]


def decode_kernel(
    cot, lo, hi, chosen_hl, mf, mb, mh, mhb, wf, wb, pf, pb, ug, us, bias,
    rebuilt, quant_grad, grads,
    x_ref, z0, z1, zu, a_s, gx_s, u_s, gh_s, g0, g1, e_ref, o_ref, up1, up2, usum, *acc,
):
    sel = selector()
    spread(us, chosen_hl, mh, zu, sel, bias[17], x_ref)

    def keep(b):
        return a_s.at[b], gx_s.at[b], u_s.at[b], gh_s.at[b]

    def last(out, start, size, core):
        if core:
            rebuilt[:, pl.ds(aligned(start), size)] = out

    order = DILATIONS[::-1]
    stack_forward(x_ref, (z0, z1), 4, order, wf, pf, bias, mf, keep, last)
    x_ref[:, :CORE] = cot[...]
    x_ref[:, CORE : CORE + HALO] = hi[CH : 2 * CH]
    x_ref[:, CORE + HALO :] = lo[CH : 2 * CH]
    for ref in (up1, up2, usum):
        ref[...] = jnp.zeros(ref.shape, F32)
    grads[GRAD_BIAS:, :] = jnp.zeros((CH, 128), F32)

    def last_back(out, start, size, core):
        to_halves(out, sel, e_ref, o_ref, start, size)
        if core:
            usum[...] += lane_fold(out)

    stack_backward(
        x_ref, (g0, g1), 4, order, wb, pb, mb, keep, acc, store_grads(grads), last_back
    )

    def up(start, size, core):
        parts = pair_stack(e_ref, o_ref, mhb, start, size)
        quant_grad[:, pl.ds(aligned(start), size)] = pair_gather(ug, parts)
        if core:
            both = lanes(chosen_hl, start, size)
            up1[...] += dot_nt(parts[0], both)
            up2[...] += dot_nt(parts[1], both[:CH])

    half_sweep(up)
    total = up1[:, :CH] + up1[:, CH:] + up2[...]
    grads[GRAD_PAIR:GRAD_BIAS, :] = jnp.concatenate([total[: 2 * CH], total[2 * CH :]], axis=1)
    put_column(grads, 8, usum[...])


def encode_back_kernel(
    latent, chosen, quant_grad, f_hi, f_lo, a_in, gx_in, u_in, gh_in, mb, mh, wb, pb, ds_,
    frames_grad, grads,
    x_ref, zu, l_ref, g0, g1, down1, down2, dsum, *acc,
):
    sel = selector()
    for ref in (down1, down2, dsum):
        ref[...] = jnp.zeros(ref.shape, F32)
    grads[GRAD_BIAS:, :] = jnp.zeros((CH, 128), F32)

    def first(start, size, core):
        at = pl.ds(aligned(start), size)
        value = quant_grad[:, at] + (2.0 * COMMIT) * (latent[:, at] - chosen[:, at])
        hi, lo = split(value)
        l_ref[:CH, at] = hi
        l_ref[CH:, at] = lo
        if core:
            dsum[...] += lane_fold(value)
            fh = f_hi[:, at]
            down1[...] += dot_nt(jnp.concatenate([hi, lo], axis=0), fh)
            down2[...] += dot_nt(hi, f_lo[:, at])

    half_sweep(first)
    spread(ds_, l_ref, mh, zu, sel, None, x_ref)

    def keep(b):
        return a_in.at[b], gx_in.at[b], u_in.at[b], gh_in.at[b]

    def last(out, start, size, core):
        if core:
            frames_grad[:, pl.ds(aligned(start), size)] = out

    stack_backward(
        x_ref, (g0, g1), 0, DILATIONS, wb, pb, mb, keep, acc, store_grads(grads), last
    )
    total = down1[:CH] + down1[CH:] + down2[...]
    grads[GRAD_PAIR : GRAD_PAIR + CH, :] = total[:, : 2 * CH]
    grads[GRAD_PAIR + CH : GRAD_BIAS, :] = total[:, 2 * CH :]
    put_column(grads, 8, dsum[...])


def unpack_kernel(
    enc, dec, cb,
    ec, ecb, ep, epb, dw, db, cg, uw, ub, dc, dcb, dp, dpb,
):
    for src, conv, cbias, proj, pbias, single in (
        (enc, ec, ecb, ep, epb, db),
        (dec, dc, dcb, dp, dpb, ub),
    ):
        rows = src[GRAD_BIAS:, :].T
        for b in range(4):
            at = slice((b % 2) * CH, (b % 2 + 1) * CH)
            p = b // 2
            conv[b] = src[p * 192 : (p + 1) * 192, at].reshape(3, CH, CH)
            proj[b] = src[GRAD_PROJ + p * CH : GRAD_PROJ + (p + 1) * CH, at]
            cbias[b : b + 1, :] = rows[2 * b : 2 * b + 1]
            pbias[b : b + 1, :] = rows[2 * b + 1 : 2 * b + 2]
        single[...] = rows[8:9]
    for k in range(4):
        a, b = k // 2, k % 2
        dw[k] = enc[GRAD_PAIR + a * CH : GRAD_PAIR + (a + 1) * CH, b * CH : (b + 1) * CH]
        uw[k] = dec[GRAD_PAIR + b * CH : GRAD_PAIR + (b + 1) * CH, a * CH : (a + 1) * CH]
    cg[: CODES // 2, :] = cb[:, :CH]
    cg[CODES // 2 :, :] = cb[:, CH:]


def shape(dims, kind=F32):
    return jax.ShapeDtypeStruct(dims, kind)


def call(kernel, outs, scratch=(), flops=0, limit=56):
    return pl.pallas_call(
        kernel,
        out_shape=outs,
        scratch_shapes=list(scratch),
        compiler_params=pltpu.CompilerParams(vmem_limit_bytes=limit * MB),
        cost_estimate=pl.CostEstimate(flops=flops, bytes_accessed=2**22, transcendentals=0),
    )


def halves(kind=BF, rows=2 * CH):
    return pltpu.VMEM((rows, HEXT), kind)


def whole(kind=F32, rows=CH):
    return pltpu.VMEM((rows, EXT), kind)


def local_prep(ec, ecb, ep, epb, dw, db, cb, uw, ub, dc, dcb, dp, dpb):
    return call(
        prep_kernel,
        [
            shape((8, 192, 192), BF),
            shape((8, 128, 192), BF),
            shape((8, 64, 192), BF),
            shape((8, 64, 192), BF),
            shape((128, 256), BF),
            shape((256, 192), BF),
            shape((128, 256), BF),
            shape((256, 192), BF),
            shape((128, CODES), BF),
            shape((18, CH, 128)),
        ],
    )(ec, ecb, ep, epb, dw, db.reshape(1, CH), cb, uw, ub.reshape(1, CH), dc, dcb, dp, dpb)


def local_encode(frames, lo, hi, clip, codes, wf, pf, dg, cbt, bias):
    return call(
        encode_kernel,
        [
            shape((64, EXT)),
            shape((128, EXT), BF),
            shape((24, HEXT)),
            shape((48, HEXT), BF),
            shape((4, 128, EXT), BF),
            shape((4, 64, EXT)),
            shape((4, 128, EXT), BF),
            shape((4, 64, EXT)),
            shape((256, HCORE), BF),
            shape((256, HCORE), BF),
            shape((CH, HEXT)),
            shape((CH, HEXT)),
            shape((2 * CH, HEXT), BF),
            shape((CODES // 2, 128)),
        ],
        [
            whole(),
            whole(rows=192),
            whole(rows=192),
            whole(rows=8),
            halves(),
            halves(),
            pltpu.VMEM((2 * CH, HCORE), BF),
            pltpu.VMEM((8, HEXT), jnp.int32),
        ],
        flops=10**10,
    )(frames, lo, hi, clip, codes, wf, pf, dg, cbt, bias)


def local_decode(cot, lo, hi, chosen_hl, mf, mb, mh, mhb, wf, wb, pf, pb, ug, us, bias):
    return call(
        decode_kernel,
        [shape((CH, CORE)), shape((CH, HEXT)), shape((GRAD_ROWS, 128))],
        [
            whole(),
            whole(rows=192),
            whole(rows=192),
            halves(F32, 256),
            pltpu.VMEM((4, 128, EXT), BF),
            pltpu.VMEM((4, CH, EXT), F32),
            pltpu.VMEM((4, 128, EXT), BF),
            pltpu.VMEM((4, CH, EXT), F32),
            whole(BF, 128),
            whole(BF, 128),
            halves(),
            halves(),
            pltpu.VMEM((256, 128), F32),
            pltpu.VMEM((256, CH), F32),
            pltpu.VMEM((CH, 128), F32),
            *sum_refs(),
        ],
        flops=2 * 10**10,
    )(cot, lo, hi, chosen_hl, mf, mb, mh, mhb, wf, wb, pf, pb, ug, us, bias)


def local_encode_back(latent, chosen, quant_grad, f_hi, f_lo, a, gx, u, gh, mb, mh, wb, pb, ds_):
    return call(
        encode_back_kernel,
        [shape((CH, CORE)), shape((GRAD_ROWS, 128))],
        [
            whole(),
            halves(F32, 256),
            halves(),
            whole(BF, 128),
            whole(BF, 128),
            pltpu.VMEM((128, 256), F32),
            pltpu.VMEM((CH, 256), F32),
            pltpu.VMEM((CH, 128), F32),
            *sum_refs(),
        ],
        flops=10**10,
    )(latent, chosen, quant_grad, f_hi, f_lo, a, gx, u, gh, mb, mh, wb, pb, ds_)


def local_unpack(enc, dec, cb):
    block = [shape((4, 3, CH, CH)), shape((4, CH)), shape((4, CH, CH)), shape((4, CH))]
    return call(
        unpack_kernel,
        [
            *block,
            shape((4, CH, CH)),
            shape((1, CH)),
            shape((CODES, CH)),
            shape((4, CH, CH)),
            shape((1, CH)),
            *block,
        ],
    )(enc, dec, cb)


def edges(frames, cotangent, clip, codes):
    count = lax.axis_size("tm")
    me = lax.axis_index("tm")

    def packed(cut, half, after, at_end):
        clip_row = jnp.where(at_end, -1.0, clip[:, cut].astype(F32))
        code_row = jnp.pad(codes[:, half].astype(F32), ((0, 0), after))
        blank = jnp.zeros((6, HALO), F32)
        return jnp.concatenate(
            [frames[:, cut], cotangent[:, cut], clip_row, code_row, blank], axis=0
        )

    tail = packed(slice(CORE - HALO, CORE), slice(HCORE - 64, HCORE), (64, 0), me == count - 1)
    front = packed(slice(0, HALO), slice(0, 64), (0, 64), me == 0)
    ring = [(i, (i + 1) % count) for i in range(count)]
    back = [(j, i) for i, j in ring]
    return lax.ppermute(tail, "tm", ring), lax.ppermute(front, "tm", back)


def turn(axis, stride, size, shift):
    count = lax.axis_size(axis)
    pairs = []
    for i in range(count):
        digit = i // stride % size
        pairs.append((i, i + ((digit + shift) % size - digit) * stride))
    return pairs


def digits():
    tm = lax.axis_size("tm")
    out = [("tm", 1, 2)]
    stride = 2
    while stride < tm:
        size = min(4, tm // stride)
        out.append(("tm", stride, size))
        stride *= size
    return out


def exchange(value, axis, stride, size):
    if size == 2:
        return value + lax.ppermute(value, axis, turn(axis, stride, 2, 1))
    got = [lax.ppermute(value, axis, turn(axis, stride, 4, s)) for s in (1, 2, 3)]
    return (value + got[1]) + (got[0] + got[2])


def sum_all(value):
    rows = value.shape[0]
    for digit in digits()[:1]:
        value = exchange(value, *digit)
    size = lax.axis_size("batch")
    part = rows // size
    me = lax.axis_index("batch")

    def cut(s):
        return lax.dynamic_slice_in_dim(value, lax.rem(me + s, size) * part, part, 0)

    got = [
        lax.ppermute(cut(s), "batch", [(i, (i + s) % size) for i in range(size)])
        for s in range(1, size)
    ]
    if size == 4:
        mine = (cut(0) + got[1]) + (got[0] + got[2])
    else:
        mine = cut(0) + got[0]
    for digit in digits()[1:]:
        mine = exchange(mine, *digit)
    out = jnp.zeros_like(value)
    out = lax.dynamic_update_slice_in_dim(out, mine, me * part, 0)
    for s in range(1, size):
        other = lax.ppermute(mine, "batch", [(i, (i + s) % size) for i in range(size)])
        out = lax.dynamic_update_slice_in_dim(out, other, lax.rem(me + size - s, size) * part, 0)
    return out


def on_device(
    frames, clip_start, code_ids, cotangent,
    enc_conv, enc_conv_bias, enc_proj, enc_proj_bias, downscale_weight, downscale_bias,
    codebook, up_weight, up_bias, dec_conv, dec_conv_bias, dec_proj, dec_proj_bias,
):
    frames = frames.reshape(CH, CORE)
    cotangent = cotangent.reshape(CH, CORE)
    lo, hi = edges(frames, cotangent, clip_start, code_ids)
    wf, wb, pf, pb, dg, ds_, ug, us, cbt, bias = local_prep(
        enc_conv, enc_conv_bias, enc_proj, enc_proj_bias, downscale_weight, downscale_bias,
        codebook, up_weight, up_bias, dec_conv, dec_conv_bias, dec_proj, dec_proj_bias,
    )
    (mf, mb, mh, mhb, a, gx, u, gh, f_hi, f_lo, latent, chosen, chosen_hl, cbg) = local_encode(
        frames, lo, hi, clip_start, code_ids, wf, pf, dg, cbt, bias
    )
    cb_sum = sum_all(cbg)
    rebuilt, quant_grad, dec_grads = local_decode(
        cotangent, lo, hi, chosen_hl, mf, mb, mh, mhb, wf, wb, pf, pb, ug, us, bias
    )
    dec_sum = sum_all(dec_grads)
    frames_grad, enc_grads = local_encode_back(
        latent, chosen, quant_grad, f_hi, f_lo, a, gx, u, gh, mb, mh, wb, pb, ds_
    )
    enc_sum = sum_all(enc_grads)
    out = list(local_unpack(enc_sum, dec_sum, cb_sum))
    out[5] = out[5].reshape(CH)
    out[8] = out[8].reshape(CH)
    return (rebuilt[None], frames_grad[None], *out)


def solution(mesh):
    split_spec = P("batch", None, "tm")
    row_spec = P("batch", "tm")
    return jax.shard_map(
        on_device,
        mesh=mesh,
        in_specs=(split_spec, row_spec, row_spec, split_spec) + (P(),) * 13,
        out_specs=(split_spec, split_spec) + (P(),) * 13,
        check_vma=False,
    )
```

```python
import functools

import jax
import jax.numpy as jnp
from jax import lax
from jax.experimental import pallas as pl
from jax.experimental.pallas import tpu as pltpu
from jax.sharding import PartitionSpec as P

COMMIT = 0.02
DILATIONS = (1, 3, 9, 27)
BF = jnp.bfloat16
F32 = jnp.float32
CH = 64
CODES = 2048
CORE = 4096
HALO = 128
EXT = CORE + 2 * HALO
HCORE = CORE // 2
HEXT = EXT // 2
STEP = 1024
G0 = 0.7978845608028654
G1 = G0 * 0.044715
MB = 2**20
GRAD_PROJ = 384
GRAD_PAIR = 512
GRAD_BIAS = 640
GRAD_ROWS = 704
CODE_ROWS = CODES // 2
ALL_ROWS = CODE_ROWS + 2 * GRAD_ROWS


BLOCK_ROWS = 448
PAIR_AT = 4 * BLOCK_ROWS
WEIGHT_ROWS = PAIR_AT + 384


PARTS = {"conv": (0, 192), "conv_back": (192, 128), "proj": (320, 64), "proj_back": (384, 64)}


def part_rows(name, b):
    first, rows = PARTS[name]
    return slice(BLOCK_ROWS * b + first, BLOCK_ROWS * b + first + rows)


def part(w, name, b):
    return w[part_rows(name, b), :192]


def dot(a, b):
    return jnp.dot(a, b, preferred_element_type=F32)


def dot_nt(a, b):
    return lax.dot_general(a, b, (((1,), (1,)), ((), ())), preferred_element_type=F32)


def split(v):
    hi = v.astype(BF)
    return hi, (v - hi.astype(F32)).astype(BF)


def gelu_both(v):
    s = v * v
    t = jnp.tanh(v * (G0 + G1 * s))
    cdf = 0.5 + 0.5 * t
    slope = cdf + (0.5 * v) * (1.0 - t * t) * (G0 + (3.0 * G1) * s)
    return v * cdf, slope


def tile_rows(rows, times):
    return jnp.concatenate([rows] * times, axis=0)


def aligned(start):
    return start if isinstance(start, int) else pl.multiple_of(start, 128)


def lanes(ref, start, size, rows=slice(None)):
    return ref[rows, pl.ds(aligned(start), size)]


def wrap(start, length):
    return start % length if isinstance(start, int) else lax.rem(start + length, length)


def from_left(ref, rows, start, size, offset, length):
    win = jnp.concatenate(
        [lanes(ref, wrap(start - 128, length), 128, rows), lanes(ref, start, size, rows)], axis=1
    )
    return pltpu.roll(win, offset, 1)[:, 128:]


def from_right(ref, rows, start, size, offset, length):
    win = jnp.concatenate(
        [lanes(ref, start, size, rows), lanes(ref, wrap(start + size, length), 128, rows)], axis=1
    )
    return pltpu.roll(win, size + 128 - offset, 1)[:, :size]


def sweep(fn, step=STEP):
    for i in range(CORE // step):
        fn(i * step, step, True)
    fn(CORE, 2 * HALO, False)


def half_sweep(fn, step=STEP // 2):
    for i in range(HCORE // step):
        fn(i * step, step, True)
    fn(HCORE, HALO, False)


def lane_fold(v):
    out = v[:, :128]
    for i in range(1, v.shape[1] // 128):
        out = out + v[:, i * 128 : (i + 1) * 128]
    return out


def selector():
    row = lax.broadcasted_iota(jnp.int32, (256, 256), 0)
    col = lax.broadcasted_iota(jnp.int32, (256, 256), 1)
    source = jnp.where(col < 128, 2 * col, 2 * (col - 128) + 1)
    return jnp.where(row == source, 1.0, 0.0).astype(BF)


def pack_kernel(frames, cot, clip, codes, front, tail, clip_v, codes_v, sems):
    first, final = slice(0, HALO), slice(CORE - HALO, CORE)
    copies = [
        pltpu.make_async_copy(src, dst, sems.at[n])
        for n, (src, dst) in enumerate(
            (
                (frames.at[:, first], front.at[:CH]),
                (frames.at[:, final], tail.at[:CH]),
                (cot.at[:, first], front.at[CH : 2 * CH]),
                (cot.at[:, final], tail.at[CH : 2 * CH]),
                (clip, clip_v),
                (codes, codes_v),
            )
        )
    ]
    for copy in copies:
        copy.start()
    for copy in copies:
        copy.wait()
    me = lax.axis_index("tm")
    count = lax.axis_size("tm")
    lane = lax.broadcasted_iota(jnp.int32, (1, HALO), 1)
    blank = jnp.zeros((6, HALO), F32)
    for out, cut, at_end, half, keep in (
        (front, first, me == 0, slice(0, HALO), lane < 64),
        (tail, final, me == count - 1, slice(HCORE - HALO, HCORE), lane >= 64),
    ):
        clip_row = jnp.where(at_end, -1.0, clip_v[:, cut].astype(F32))
        code_row = jnp.where(keep, codes_v[:, half].astype(F32), 0.0)
        out[2 * CH :, :] = jnp.concatenate([clip_row, code_row, blank], axis=0)


def prep_kernel(*refs):
    sources, outs, scratch = refs[:14], refs[14:19], refs[19:]
    sems = scratch[-1]
    copies = [
        pltpu.make_async_copy(src, dst, sems.at[n])
        for n, (src, dst) in enumerate(zip(sources, scratch[:14]))
    ]
    for copy in copies:
        copy.start()
    for copy in copies:
        copy.wait()
    ec, ecb, ep, epb, dw, db, cb, uw, ub, dc, dcb, dp, dpb, codes = scratch[:14]
    enc_w, dec_w, bias, cbt, chosen = outs

    def forms(w):
        hi, lo = split(w)
        return jnp.concatenate([hi, hi, lo], axis=1)

    def stacked(w):
        hi, lo = split(w)
        return jnp.concatenate([hi, lo], axis=0)

    def column(row):
        return jnp.broadcast_to(row, (128, CH)).T

    cbt[...] = stacked(cb[...])
    pick(codes, cbt, chosen, 0, HCORE, 1024)
    for n, (conv, cbias, proj, pbias) in enumerate(((ec, ecb, ep, epb), (dc, dcb, dp, dpb))):
        weights = (enc_w, dec_w)[n]
        for b in range(4):
            at = 4 * n + b
            weights[part_rows("conv", b), :192] = forms(conv[b].reshape(3 * CH, CH))
            weights[part_rows("conv_back", b), :192] = stacked(jnp.concatenate([conv[b, k].T for k in range(3)], axis=1))
            weights[part_rows("proj", b), :192] = forms(proj[b])
            weights[part_rows("proj_back", b), :192] = forms(proj[b].T)
            bias[2 * at] = column(cbias[b : b + 1, :])
            bias[2 * at + 1] = column(pbias[b : b + 1, :])
    bias[16] = column(db[...])
    bias[17] = column(ub[...])
    enc_w[PAIR_AT : PAIR_AT + 128, :] = stacked(jnp.concatenate([dw[k] for k in range(4)], axis=1))
    enc_w[PAIR_AT + 128 :, :192] = forms(jnp.concatenate([dw[k].T for k in range(4)], axis=0))
    dec_w[PAIR_AT : PAIR_AT + 128, :] = stacked(jnp.concatenate([uw[k].T for k in range(4)], axis=1))
    dec_w[PAIR_AT + 128 :, :192] = forms(jnp.concatenate([uw[k] for k in range(4)], axis=0))


def one_hot(ids_row, first, count):
    row = lax.broadcasted_iota(jnp.int32, (count, ids_row.shape[1]), 0) + first
    return jnp.where(row == ids_row, 1.0, 0.0).astype(BF)


def pick(ids, cbt, chosen, begin, end, step):
    for start in range(begin, end, step):
        at = slice(start - begin, start - begin + step)
        to = slice(start, start + step)
        both = dot(cbt[...], one_hot(ids[0:1, at], 0, CODES))
        chosen[:, to] = both[:CH] + both[CH:]


def stack_forward(x_ref, z_refs, blocks, dils, w, bias, mf, keep, last):
    def enter(value, start, size, b):
        act, slope = gelu_both(value)
        hi, lo = split(act)
        a_ref, gx_ref, _, _ = keep(b)
        a_ref[:CH, pl.ds(aligned(start), size)] = hi
        a_ref[CH:, pl.ds(aligned(start), size)] = lo
        gx_ref[:, pl.ds(aligned(start), size)] = slope
        z_refs[b % 2][:, pl.ds(aligned(start), size)] = dot(
            part(w, "conv", b), jnp.concatenate([hi, lo, hi], axis=0)
        )

    def first(start, size, core):
        enter(lanes(x_ref, start, size), start, size, 0)

    sweep(first)
    for b in range(4):
        d = dils[b]
        m = DILATIONS.index(d)
        z_ref = z_refs[b % 2]

        def step(start, size, core, b=b, d=d, m=m, z_ref=z_ref):
            _, _, u_ref, gh_ref = keep(b)
            times = size // 128
            left = tile_rows(lanes(mf, start, size, slice(16 * m, 16 * m + 8)), 8)
            right = tile_rows(lanes(mf, start, size, slice(16 * m + 8, 16 * m + 16)), 8)
            cb = jnp.concatenate([bias[2 * (blocks + b)]] * times, axis=1)
            hidden = lanes(z_ref, start, size, slice(CH, 2 * CH)) + cb
            hidden = hidden + left * from_left(z_ref, slice(0, CH), start, size, d, EXT)
            hidden = hidden + right * from_right(z_ref, slice(2 * CH, 3 * CH), start, size, d, EXT)
            act, slope = gelu_both(hidden)
            hi, lo = split(act)
            u_ref[:CH, pl.ds(aligned(start), size)] = hi
            u_ref[CH:, pl.ds(aligned(start), size)] = lo
            gh_ref[:, pl.ds(aligned(start), size)] = slope
            pbias = jnp.concatenate([bias[2 * (blocks + b) + 1]] * times, axis=1)
            out = (
                lanes(x_ref, start, size)
                + dot(part(w, "proj", b), jnp.concatenate([hi, lo, hi], axis=0))
                + pbias
            )
            if b < 3:
                x_ref[:, pl.ds(aligned(start), size)] = out
                enter(out, start, size, b + 1)
            else:
                last(out, start, size, core)

        sweep(step)


def stack_backward(g_ref, gh_refs, blocks, dils, w, mb, keep, acc, finish, last):
    dk1, dk2, dpa, csum, psum = acc

    def enter(grad, start, size, core, b):
        _, _, u_ref, slope_ref = keep(b)
        hi, lo = split(grad)
        q = dot(part(w, "proj_back", b), jnp.concatenate([hi, lo, hi], axis=0))
        gh = lanes(slope_ref, start, size) * q
        ghi, glo = split(gh)
        gh_refs[b % 2][:CH, pl.ds(aligned(start), size)] = ghi
        gh_refs[b % 2][CH:, pl.ds(aligned(start), size)] = glo
        if core:
            dpa[b] += dot_nt(jnp.concatenate([hi, lo], axis=0), lanes(u_ref, start, size))
            csum[b] += lane_fold(gh)
            psum[b] += lane_fold(grad)

    for ref in acc:
        ref[...] = jnp.zeros(ref.shape, ref.dtype)

    def first(start, size, core):
        enter(lanes(g_ref, start, size), start, size, core, 3)

    sweep(first)
    for b in (3, 2, 1, 0):
        d = dils[b]
        m = DILATIONS.index(d)
        gh_ref = gh_refs[b % 2]

        def step(start, size, core, b=b, d=d, m=m, gh_ref=gh_ref):
            a_ref, gx_ref, _, _ = keep(b)
            left = tile_rows(lanes(mb, start, size, slice(32 * m, 32 * m + 16)), 4)
            right = tile_rows(lanes(mb, start, size, slice(32 * m + 16, 32 * m + 32)), 4)
            parts = []
            for rows in (slice(0, CH), slice(CH, 2 * CH)):
                parts.append(
                    jnp.concatenate(
                        [
                            from_right(gh_ref, rows, start, size, d, EXT) * right,
                            lanes(gh_ref, start, size, rows),
                            from_left(gh_ref, rows, start, size, d, EXT) * left,
                        ],
                        axis=0,
                    )
                )
            ghi, glo = parts
            both = dot(part(w, "conv_back", b), ghi)
            ga = both[:CH] + both[CH:] + dot(part(w, "conv_back", b)[:CH], glo)
            if core:
                act = lanes(a_ref, start, size)
                dk1[b] += dot_nt(ghi, act)
                dk2[b] += dot_nt(glo, act[:CH])
            out = lanes(g_ref, start, size) + lanes(gx_ref, start, size) * ga
            if b > 0:
                g_ref[:, pl.ds(aligned(start), size)] = out
                enter(out, start, size, core, b - 1)
            else:
                last(out, start, size, core)

        sweep(step)
    for b in range(4):
        dk = dk1[b, :, :CH] + dk1[b, :, CH:] + dk2[b]
        dp = dpa[b, :CH, :CH] + dpa[b, CH:, :CH] + dpa[b, :CH, CH:]
        finish(b, dk, dp, csum[b], psum[b])


def store_grads(grads):
    kept = {}

    def finish(b, dk, dp, csum, psum):
        kept[b] = (dk, dp)
        if b % 2:
            at = b // 2
            grads[at * 192 : (at + 1) * 192, :] = jnp.concatenate([kept[b - 1][0], dk], axis=1)
            grads[GRAD_PROJ + at * CH : GRAD_PROJ + (at + 1) * CH, :] = jnp.concatenate(
                [kept[b - 1][1], dp], axis=1
            )
        put_column(grads, 2 * b, csum)
        put_column(grads, 2 * b + 1, psum)

    return finish


def put_column(grads, at, folded):
    lane = lax.broadcasted_iota(jnp.int32, (CH, 128), 1)
    total = jnp.sum(folded, axis=1, keepdims=True)
    grads[GRAD_BIAS:, :] = jnp.where(lane == at, total, grads[GRAD_BIAS:, :])


def to_halves(value, sel, e_ref, o_ref, start, size):
    hi, lo = split(value)
    both = jnp.concatenate([hi, lo], axis=0)
    half = start // 2
    for i in range(size // 256):
        out = dot(both[:, i * 256 : (i + 1) * 256], sel).astype(BF)
        e_ref[:, pl.ds(aligned(half + i * 128), 128)] = out[:, :128]
        o_ref[:, pl.ds(aligned(half + i * 128), 128)] = out[:, 128:]


def pair_stack(e_ref, o_ref, mhb, start, size):
    masks = [tile_rows(lanes(mhb, start, size, slice(16 * i, 16 * i + 16)), 4) for i in range(3)]
    parts = []
    for rows in (slice(0, CH), slice(CH, 2 * CH)):
        parts.append(
            jnp.concatenate(
                [
                    from_left(o_ref, rows, start, size, 1, HEXT) * masks[0],
                    lanes(e_ref, start, size, rows),
                    lanes(o_ref, start, size, rows) * masks[1],
                    from_right(e_ref, rows, start, size, 1, HEXT) * masks[2],
                ],
                axis=0,
            )
        )
    return parts


def pair_gather(w, parts):
    both = dot(w[...], parts[0])
    return both[:CH] + both[CH:] + dot(w[:CH], parts[1])


def spread(w, hl_ref, mh, z_refs, sel, bias_tile, x_ref):
    def first(start, size, core):
        both = lanes(hl_ref, start, size)
        z = dot(w, jnp.concatenate([both, both[:CH]], axis=0))
        masks = [tile_rows(lanes(mh, start, size, slice(8 * i, 8 * i + 8)), 8) for i in range(3)]
        at = pl.ds(aligned(start), size)
        z_refs[0][:, at] = z[0:64] * masks[0]
        z_refs[1][:, at] = z[64:128]
        z_refs[2][:, at] = z[128:192] * masks[1]
        z_refs[3][:, at] = z[192:256] * masks[2]

    half_sweep(first)

    def second(start, size, core):
        every = slice(None)
        even = lanes(z_refs[1], start, size) + from_left(z_refs[3], every, start, size, 1, HEXT)
        odd = lanes(z_refs[2], start, size) + from_right(z_refs[0], every, start, size, 1, HEXT)
        ehi, elo = split(even)
        ohi, olo = split(odd)
        for i in range(size // 128):
            cut = slice(i * 128, (i + 1) * 128)
            rows = jnp.concatenate(
                [
                    jnp.concatenate([ehi[:, cut], ohi[:, cut]], axis=1),
                    jnp.concatenate([elo[:, cut], olo[:, cut]], axis=1),
                ],
                axis=0,
            )
            out = dot_nt(rows, sel)
            out = out[:CH] + out[CH:]
            if bias_tile is not None:
                out = out + jnp.concatenate([bias_tile, bias_tile], axis=1)
            x_ref[:, pl.ds(aligned(2 * start + 256 * i), 256)] = out

    half_sweep(second)


def ring_fill(ref, core, hi, lo):
    if core is not None:
        ref[:, :CORE] = core
    ref[:, CORE : CORE + HALO] = hi
    ref[:, CORE + HALO :] = lo


def find_links(clip_ref, sel, mf, mb, mh, mhb):
    def links(start, size, core):
        at = pl.ds(aligned(start), size)
        here = lanes(clip_ref, start, size)

        def same(other):
            return jnp.where(other == here, 1.0, 0.0)

        for m, d in enumerate(DILATIONS):
            left = same(from_left(clip_ref, slice(None), start, size, d, EXT))
            right = same(from_right(clip_ref, slice(None), start, size, d, EXT))
            mf[16 * m : 16 * m + 8, at] = left
            mf[16 * m + 8 : 16 * m + 16, at] = right
            mb[32 * m : 32 * m + 16, at] = tile_rows(left, 2).astype(BF)
            mb[32 * m + 16 : 32 * m + 32, at] = tile_rows(right, 2).astype(BF)
            if m == 0:
                two = same(from_right(clip_ref, slice(None), start, size, 2, EXT))
                rows = jnp.concatenate([left, right, two, two], axis=0).astype(BF)
                half = start // 2
                for i in range(size // 256):
                    out = dot(rows[:, i * 256 : (i + 1) * 256], sel)[:, :128]
                    hat = pl.ds(aligned(half + 128 * i), 128)
                    mh[:, hat] = out[:24]
                    for n in range(3):
                        mhb[16 * n : 16 * n + 16, hat] = tile_rows(
                            out[8 * n : 8 * n + 8], 2
                        ).astype(BF)

    sweep(links)


def sum_refs():
    return [
        pltpu.VMEM((4, 3 * CH, 2 * CH), F32),
        pltpu.VMEM((4, 3 * CH, CH), F32),
        pltpu.VMEM((4, 2 * CH, 2 * CH), F32),
        pltpu.VMEM((4, CH, 128), F32),
        pltpu.VMEM((4, CH, 128), F32),
    ]


def state_refs():
    return [
        whole(),
        whole(rows=192),
        whole(rows=192),
        pltpu.VMEM((4, 128, EXT), BF),
        pltpu.VMEM((4, CH, EXT), F32),
        pltpu.VMEM((4, 128, EXT), BF),
        pltpu.VMEM((4, CH, EXT), F32),
        whole(),
        whole(BF, 128),
        whole(BF, 128),
        halves(),
        halves(),
        *sum_refs(),
    ]


def decode_kernel(
    cot, lo, hi, clip, chosen_in, cbt, weights, bias,
    rebuilt, quant_grad, grads, mf, mb, mh, mhb, chosen, chosen_hl, ids,
    up1, up2, usum, clip_ref, sems, x_ref, z0, z1, a_s, gx_s, u_s, gh_s, g_ref, g0, g1, e_ref, o_ref,
    *acc,
):
    ug = weights.at[PAIR_AT : PAIR_AT + 128]
    us = weights[PAIR_AT + 128 :, :192]
    cot_in = pltpu.make_async_copy(cot, g_ref.at[:, :CORE], sems.at[0])
    cot_in.start()
    sel = selector()
    ring_fill(
        clip_ref,
        jnp.broadcast_to(clip[...].astype(F32), (8, CORE)),
        jnp.broadcast_to(hi[128:129], (8, HALO)),
        jnp.broadcast_to(lo[128:129], (8, HALO)),
    )
    find_links(clip_ref, sel, mf, mb, mh, mhb)
    chosen[:, :HCORE] = chosen_in[...]
    ids[...] = jnp.broadcast_to((hi[129:130] + lo[129:130]).astype(jnp.int32), (8, HALO))
    pick(ids, cbt, chosen, HCORE, HEXT, HALO)
    chi, clo = split(chosen[...])
    chosen_hl[:CH] = chi
    chosen_hl[CH:] = clo
    zu = [z0.at[:CH], z0.at[CH : 2 * CH], z0.at[2 * CH :], z1.at[:CH]]
    spread(us, chosen_hl, mh, zu, sel, bias[17], x_ref)

    def keep(b):
        return a_s.at[b], gx_s.at[b], u_s.at[b], gh_s.at[b]

    def last(out, start, size, core):
        if core:
            x_ref[:, pl.ds(aligned(start), size)] = out

    order = DILATIONS[::-1]
    stack_forward(x_ref, (z0, z1), 4, order, weights, bias, mf, keep, last)
    rebuilt_out = pltpu.make_async_copy(x_ref.at[:, :CORE], rebuilt, sems.at[1])
    rebuilt_out.start()
    cot_in.wait()
    ring_fill(g_ref, None, hi[CH : 2 * CH], lo[CH : 2 * CH])
    for ref in (up1, up2, usum):
        ref[...] = jnp.zeros(ref.shape, F32)
    grads[GRAD_BIAS:, :] = jnp.zeros((CH, 128), F32)

    def last_back(out, start, size, core):
        to_halves(out, sel, e_ref, o_ref, start, size)
        if core:
            usum[...] += lane_fold(out)

    stack_backward(
        g_ref, (g0, g1), 4, order, weights, mb, keep, acc, store_grads(grads), last_back
    )

    def up(start, size, core):
        parts = pair_stack(e_ref, o_ref, mhb, start, size)
        quant_grad[:, pl.ds(aligned(start), size)] = pair_gather(ug, parts)
        if core:
            both = lanes(chosen_hl, start, size)
            up1[...] += dot_nt(parts[0], both)
            up2[...] += dot_nt(parts[1], both[:CH])

    half_sweep(up)
    total = up1[:, :CH] + up1[:, CH:] + up2[...]
    grads[GRAD_PAIR:GRAD_BIAS, :] = jnp.concatenate([total[: 2 * CH], total[2 * CH :]], axis=1)
    put_column(grads, 8, usum[...])
    rebuilt_out.wait()


def encode_kernel(
    frames, lo, hi, codes, quant_grad, dec_grads, chosen, mf, mb, mh, mhb, weights, bias,
    frames_grad, sums,
    d_ref, l_ref, down1, down2, dsum,
    x_ref, z0, z1, a_s, gx_s, u_s, gh_s, g_ref, g0, g1, e_ref, o_ref, *acc,
):
    dg = weights.at[PAIR_AT : PAIR_AT + 128]
    ds_ = weights[PAIR_AT + 128 :, :192]
    sel = selector()
    ring_fill(x_ref, frames[...], hi[:CH], lo[:CH])
    grads = sums.at[CODE_ROWS : CODE_ROWS + GRAD_ROWS]
    sums[CODE_ROWS + GRAD_ROWS :, :] = dec_grads[...]

    def keep(b):
        return a_s.at[b], gx_s.at[b], u_s.at[b], gh_s.at[b]

    def last(out, start, size, core):
        to_halves(out, sel, e_ref, o_ref, start, size)

    stack_forward(x_ref, (z0, z1), 0, DILATIONS, weights, bias, mf, keep, last)
    for ref in (down1, down2, dsum):
        ref[...] = jnp.zeros(ref.shape, F32)
    grads[GRAD_BIAS:, :] = jnp.zeros((CH, 128), F32)

    def down(start, size, core):
        at = pl.ds(aligned(start), size)
        parts = pair_stack(e_ref, o_ref, mhb, start, size)
        value = pair_gather(dg, parts) + jnp.concatenate([bias[16]] * (size // 128), axis=1)
        gap = value - lanes(chosen, start, size)
        grad = quant_grad[:, at] + (2.0 * COMMIT) * gap
        hi, lo = split(grad)
        l_ref[:CH, at] = hi
        l_ref[CH:, at] = lo
        if core:
            dhi, dlo = split(-2.0 * gap)
            d_ref[:CH, at] = dhi
            d_ref[CH:, at] = dlo
            dsum[...] += lane_fold(grad)
            down1[...] += dot_nt(jnp.concatenate([hi, lo], axis=0), parts[0])
            down2[...] += dot_nt(hi, parts[1])

    half_sweep(down)
    def codes_back(i, carry):
        hot = one_hot(codes[...], i * 256, 256)
        out = dot_nt(d_ref[...], hot)
        out = out[:CH] + out[CH:]
        at = pl.multiple_of(i * 128, 128)
        sums[pl.ds(at, CH), :] = out[:, :128]
        sums[pl.ds(at + CH, CH), :] = out[:, 128:]
        return carry

    lax.fori_loop(0, CODES // 256, codes_back, 0)
    zu = [z0.at[:CH], z0.at[CH : 2 * CH], z0.at[2 * CH :], z1.at[:CH]]
    spread(ds_, l_ref, mh, zu, sel, None, g_ref)

    def last_back(out, start, size, core):
        if core:
            frames_grad[:, pl.ds(aligned(start), size)] = out

    stack_backward(
        g_ref, (g0, g1), 0, DILATIONS, weights, mb, keep, acc, store_grads(grads), last_back
    )
    total = down1[:CH] + down1[CH:] + down2[...]
    grads[GRAD_PAIR : GRAD_PAIR + CH, :] = total[:, : 2 * CH]
    grads[GRAD_PAIR + CH : GRAD_BIAS, :] = total[:, 2 * CH :]
    put_column(grads, 8, dsum[...])


def unpack_kernel(
    sums,
    cg, ec, ecb, ep, epb, dw, db, uw, ub, dc, dcb, dp, dpb,
):
    for i in range(CODES // 128):
        cg[:, i * 128 : (i + 1) * 128] = sums[i * CH : (i + 1) * CH, :]
    enc = sums.at[CODE_ROWS : CODE_ROWS + GRAD_ROWS]
    dec = sums.at[CODE_ROWS + GRAD_ROWS :]
    for src, conv, cbias, proj, pbias, single in (
        (enc, ec, ecb, ep, epb, db),
        (dec, dc, dcb, dp, dpb, ub),
    ):
        rows = src[GRAD_BIAS:, :].T
        for b in range(4):
            at = slice((b % 2) * CH, (b % 2 + 1) * CH)
            p = b // 2
            conv[b] = src[p * 192 : (p + 1) * 192, at].reshape(3, CH, CH)
            proj[b] = src[GRAD_PROJ + p * CH : GRAD_PROJ + (p + 1) * CH, at]
            cbias[b : b + 1, :] = rows[2 * b : 2 * b + 1]
            pbias[b : b + 1, :] = rows[2 * b + 1 : 2 * b + 2]
        single[...] = rows[8:9]
    for k in range(4):
        a, b = k // 2, k % 2
        dw[k] = enc[GRAD_PAIR + a * CH : GRAD_PAIR + (a + 1) * CH, b * CH : (b + 1) * CH]
        uw[k] = dec[GRAD_PAIR + b * CH : GRAD_PAIR + (b + 1) * CH, a * CH : (a + 1) * CH]


def shape(dims, kind=F32):
    return jax.ShapeDtypeStruct(dims, kind)


def call(kernel, outs, scratch=(), flops=0, limit=40, in_specs=None, out_specs=None):
    extra = {}
    if in_specs is not None:
        extra["in_specs"] = in_specs
    if out_specs is not None:
        extra["out_specs"] = out_specs
    return pl.pallas_call(
        kernel,
        out_shape=outs,
        scratch_shapes=list(scratch),
        compiler_params=pltpu.CompilerParams(vmem_limit_bytes=limit * MB),
        cost_estimate=pl.CostEstimate(flops=flops, bytes_accessed=2**20, transcendentals=0),
        **extra,
    )


def halves(kind=BF, rows=2 * CH):
    return pltpu.VMEM((rows, HEXT), kind)


def whole(kind=F32, rows=CH):
    return pltpu.VMEM((rows, EXT), kind)


FAR = pl.BlockSpec(memory_space=pltpu.HBM)


def far(*values):
    return [pltpu.with_memory_space_constraint(v, pltpu.HBM) for v in values]
LOCAL = pl.BlockSpec()


def local_pack(frames, cot, clip, codes):
    return call(
        pack_kernel,
        [shape((136, HALO)), shape((136, HALO))],
        [
            pltpu.VMEM((1, CORE), jnp.int32),
            pltpu.VMEM((1, HCORE), jnp.int32),
            pltpu.SemaphoreType.DMA((6,)),
        ],
        in_specs=[FAR] * 4,
    )(*far(frames, cot, clip, codes))


def local_prep(*args):
    return call(
        prep_kernel,
        [
            shape((WEIGHT_ROWS, 256), BF),
            shape((WEIGHT_ROWS, 256), BF),
            shape((18, CH, 128)),
            shape((128, CODES), BF),
            shape((CH, HCORE)),
        ],
        [pltpu.VMEM(a.shape, a.dtype) for a in args] + [pltpu.SemaphoreType.DMA((14,))],
        flops=2 * 10**9,
        limit=40,
        in_specs=[FAR] * 14,
    )(*far(*args))


def local_decode(cot, *args):
    return call(
        decode_kernel,
        [
            shape((CH, CORE)),
            shape((CH, HEXT)),
            shape((GRAD_ROWS, 128)),
            shape((64, EXT)),
            shape((128, EXT), BF),
            shape((24, HEXT)),
            shape((48, HEXT), BF),
            shape((CH, HEXT)),
        ],
        [
            halves(),
            pltpu.VMEM((8, HALO), jnp.int32),
            pltpu.VMEM((256, 128), F32),
            pltpu.VMEM((256, CH), F32),
            pltpu.VMEM((CH, 128), F32),
            whole(rows=8),
            pltpu.SemaphoreType.DMA((2,)),
            *state_refs(),
        ],
        flops=2 * 10**10,
        limit=40,
        in_specs=[FAR] + [LOCAL] * 7,
        out_specs=[FAR] + [LOCAL] * 7,
    )(*far(cot), *args)


def local_encode(*args):
    return call(
        encode_kernel,
        [shape((CH, CORE)), shape((ALL_ROWS, 128))],
        [
            pltpu.VMEM((2 * CH, HCORE), BF),
            halves(),
            pltpu.VMEM((128, 256), F32),
            pltpu.VMEM((CH, 256), F32),
            pltpu.VMEM((CH, 128), F32),
            *state_refs(),
        ],
        flops=2 * 10**10,
        limit=40,
    )(*args)


def local_unpack(sums):
    block = [shape((4, 3, CH, CH)), shape((4, CH)), shape((4, CH, CH)), shape((4, CH))]
    return call(
        unpack_kernel,
        [
            shape((CH, CODES)),
            *block,
            shape((4, CH, CH)),
            shape((1, CH)),
            shape((4, CH, CH)),
            shape((1, CH)),
            *block,
        ],
    )(sums)


def pairing(axis, stride, size, round_):
    partner = {2: [[1, 0]], 4: [[1, 0, 3, 2], [3, 2, 1, 0]]}[size][round_]
    pairs = []
    for i in range(lax.axis_size(axis)):
        digit = i // stride % size
        pairs.append((i, i + (partner[digit] - digit) * stride))
    return pairs


def rounds():
    tm, batch = lax.axis_size("tm"), lax.axis_size("batch")
    out = []

    def add(axis, stride, size):
        digit = lax.axis_index(axis) // stride % size
        if size == 2:
            out.append((axis, pairing(axis, stride, 2, 0), digit))
        else:
            out.append((axis, pairing(axis, stride, 4, 0), (digit ^ (digit // 2)) % 2))
            out.append((axis, pairing(axis, stride, 4, 1), digit // 2))

    add("tm", 1, 2)
    stride = 2
    while stride < tm:
        size = min(4, tm // stride)
        add("tm", stride, size)
        stride *= size
    add("batch", 1, batch)
    return out


SCATTER = 3


def sum_all(value):
    plan = rounds()
    kept = []
    for n, (axis, pairs, bit) in enumerate(plan):
        if n < SCATTER:
            half = value.shape[0] // 2
            mine = lax.dynamic_slice_in_dim(value, bit * half, half, 0)
            other = lax.dynamic_slice_in_dim(value, (1 - bit) * half, half, 0)
            value = mine + lax.ppermute(other, axis, pairs)
        else:
            value = value + lax.ppermute(value, axis, pairs)
    for axis, pairs, bit in plan[:SCATTER][::-1]:
        other = lax.ppermute(value, axis, pairs)
        half = value.shape[0]
        out = jnp.zeros((2 * half, value.shape[1]), value.dtype)
        out = lax.dynamic_update_slice_in_dim(out, value, bit * half, 0)
        value = lax.dynamic_update_slice_in_dim(out, other, (1 - bit) * half, 0)
    return value


def on_device(
    frames, clip_start, code_ids, cotangent,
    enc_conv, enc_conv_bias, enc_proj, enc_proj_bias, downscale_weight, downscale_bias,
    codebook, up_weight, up_bias, dec_conv, dec_conv_bias, dec_proj, dec_proj_bias,
):
    frames = frames.reshape(CH, CORE)
    cotangent = cotangent.reshape(CH, CORE)
    front, tail = local_pack(frames, cotangent, clip_start, code_ids)
    count = lax.axis_size("tm")
    ring = [(i, (i + 1) % count) for i in range(count)]
    lo = lax.ppermute(tail, "tm", ring)
    hi = lax.ppermute(front, "tm", [(j, i) for i, j in ring])
    enc_w, dec_w, bias, cbt, chosen = local_prep(
        enc_conv, enc_conv_bias, enc_proj, enc_proj_bias,
        downscale_weight, downscale_bias.reshape(1, CH),
        codebook.T, up_weight, up_bias.reshape(1, CH),
        dec_conv, dec_conv_bias, dec_proj, dec_proj_bias, code_ids,
    )
    rebuilt, quant_grad, dec_grads, mf, mb, mh, mhb, chosen = local_decode(
        cotangent, lo, hi, clip_start, chosen, cbt, dec_w, bias
    )
    frames_grad, sums = local_encode(
        frames, lo, hi, code_ids, quant_grad, dec_grads, chosen, mf, mb, mh, mhb,
        enc_w, bias,
    )
    out = list(local_unpack(sum_all(sums)))
    cg = out.pop(0).T
    out[5] = out[5].reshape(CH)
    out[7] = out[7].reshape(CH)
    out.insert(6, cg)
    return (rebuilt[None], frames_grad[None], *out)


def solution(mesh):
    split_spec = P("batch", None, "tm")
    row_spec = P("batch", "tm")
    return jax.shard_map(
        on_device,
        mesh=mesh,
        in_specs=(split_spec, row_spec, row_spec, split_spec) + (P(),) * 13,
        out_specs=(split_spec, split_spec) + (P(),) * 13,
        check_vma=False,
    )
```

```python
import functools

import jax
import jax.numpy as jnp
from jax import lax
from jax.experimental import pallas as pl
from jax.experimental.pallas import tpu as pltpu
from jax.sharding import PartitionSpec as P

COMMIT = 0.02
DILATIONS = (1, 3, 9, 27)
BF = jnp.bfloat16
F32 = jnp.float32
CH = 64
CODES = 2048
CORE = 4096
HALO = 128
EXT = CORE + 2 * HALO
HCORE = CORE // 2
HEXT = EXT // 2
STEP = 1024
G0 = 0.7978845608028654
G1 = G0 * 0.044715
MB = 2**20
GRAD_PROJ = 384
GRAD_PAIR = 512
GRAD_BIAS = 640
GRAD_ROWS = 704
CODE_ROWS = CODES // 2
ALL_ROWS = CODE_ROWS + 2 * GRAD_ROWS


BLOCK_ROWS = 448
PAIR_AT = 4 * BLOCK_ROWS
WEIGHT_ROWS = PAIR_AT + 384


PARTS = {"conv": (0, 192), "conv_back": (192, 128), "proj": (320, 64), "proj_back": (384, 64)}


def part_rows(name, b):
    first, rows = PARTS[name]
    return slice(BLOCK_ROWS * b + first, BLOCK_ROWS * b + first + rows)


def part(w, name, b):
    return w[part_rows(name, b), :192]


def dot(a, b):
    return jnp.dot(a, b, preferred_element_type=F32)


def dot_nt(a, b):
    return lax.dot_general(a, b, (((1,), (1,)), ((), ())), preferred_element_type=F32)


def split(v):
    hi = v.astype(BF)
    return hi, (v - hi.astype(F32)).astype(BF)


def gelu_both(v):
    s = v * v
    t = jnp.tanh(v * (G0 + G1 * s))
    cdf = 0.5 + 0.5 * t
    slope = cdf + (0.5 * v) * (1.0 - t * t) * (G0 + (3.0 * G1) * s)
    return v * cdf, slope


def tile_rows(rows, times):
    return jnp.concatenate([rows] * times, axis=0)


def aligned(start):
    return start if isinstance(start, int) else pl.multiple_of(start, 128)


def lanes(ref, start, size, rows=slice(None)):
    return ref[rows, pl.ds(aligned(start), size)]


def wrap(start, length):
    return start % length if isinstance(start, int) else lax.rem(start + length, length)


def from_left(ref, rows, start, size, offset, length):
    win = jnp.concatenate(
        [lanes(ref, wrap(start - 128, length), 128, rows), lanes(ref, start, size, rows)], axis=1
    )
    return pltpu.roll(win, offset, 1)[:, 128:]


def from_right(ref, rows, start, size, offset, length):
    win = jnp.concatenate(
        [lanes(ref, start, size, rows), lanes(ref, wrap(start + size, length), 128, rows)], axis=1
    )
    return pltpu.roll(win, size + 128 - offset, 1)[:, :size]


def sweep(fn, step=STEP):
    for i in range(CORE // step):
        fn(i * step, step, True)
    fn(CORE, 2 * HALO, False)


def half_sweep(fn, step=STEP // 2):
    for i in range(HCORE // step):
        fn(i * step, step, True)
    fn(HCORE, HALO, False)


def lane_fold(v):
    out = v[:, :128]
    for i in range(1, v.shape[1] // 128):
        out = out + v[:, i * 128 : (i + 1) * 128]
    return out


def selector():
    row = lax.broadcasted_iota(jnp.int32, (256, 256), 0)
    col = lax.broadcasted_iota(jnp.int32, (256, 256), 1)
    source = jnp.where(col < 128, 2 * col, 2 * (col - 128) + 1)
    return jnp.where(row == source, 1.0, 0.0).astype(BF)


def pack_kernel(frames, cot, clip, codes, front, tail, clip_v, codes_v, sems):
    first, final = slice(0, HALO), slice(CORE - HALO, CORE)
    copies = [
        pltpu.make_async_copy(src, dst, sems.at[n])
        for n, (src, dst) in enumerate(
            (
                (frames.at[:, first], front.at[:CH]),
                (frames.at[:, final], tail.at[:CH]),
                (cot.at[:, first], front.at[CH : 2 * CH]),
                (cot.at[:, final], tail.at[CH : 2 * CH]),
                (clip, clip_v),
                (codes, codes_v),
            )
        )
    ]
    for copy in copies:
        copy.start()
    for copy in copies:
        copy.wait()
    me = lax.axis_index("tm")
    count = lax.axis_size("tm")
    lane = lax.broadcasted_iota(jnp.int32, (1, HALO), 1)
    blank = jnp.zeros((6, HALO), F32)
    for out, cut, at_end, half, keep in (
        (front, first, me == 0, slice(0, HALO), lane < 64),
        (tail, final, me == count - 1, slice(HCORE - HALO, HCORE), lane >= 64),
    ):
        clip_row = jnp.where(at_end, -1.0, clip_v[:, cut].astype(F32))
        code_row = jnp.where(keep, codes_v[:, half].astype(F32), 0.0)
        out[2 * CH :, :] = jnp.concatenate([clip_row, code_row, blank], axis=0)


def prep_kernel(*refs):
    sources, outs, scratch = refs[:14], refs[14:19], refs[19:]
    sems = scratch[-1]
    copies = [
        pltpu.make_async_copy(src, dst, sems.at[n])
        for n, (src, dst) in enumerate(zip(sources, scratch[:14]))
    ]
    first = (6, 13)
    for n in (*first, *range(6), *range(7, 13)):
        copies[n].start()
    for n in first:
        copies[n].wait()
    ec, ecb, ep, epb, dw, db, cb, uw, ub, dc, dcb, dp, dpb, codes = scratch[:14]
    enc_w, dec_w, bias, cbt, chosen = outs

    def forms(w):
        hi, lo = split(w)
        return jnp.concatenate([hi, hi, lo], axis=1)

    def stacked(w):
        hi, lo = split(w)
        return jnp.concatenate([hi, lo], axis=0)

    def column(row):
        return jnp.broadcast_to(row, (128, CH)).T

    cbt[...] = stacked(cb[...])
    pick(codes, cbt, chosen, 0, HCORE, 1024)
    for n in (*range(6), *range(7, 13)):
        copies[n].wait()
    for n, (conv, cbias, proj, pbias) in enumerate(((ec, ecb, ep, epb), (dc, dcb, dp, dpb))):
        weights = (enc_w, dec_w)[n]
        for b in range(4):
            at = 4 * n + b
            weights[part_rows("conv", b), :192] = forms(conv[b].reshape(3 * CH, CH))
            weights[part_rows("conv_back", b), :192] = stacked(jnp.concatenate([conv[b, k].T for k in range(3)], axis=1))
            weights[part_rows("proj", b), :192] = forms(proj[b])
            weights[part_rows("proj_back", b), :192] = forms(proj[b].T)
            bias[2 * at] = column(cbias[b : b + 1, :])
            bias[2 * at + 1] = column(pbias[b : b + 1, :])
    bias[16] = column(db[...])
    bias[17] = column(ub[...])
    enc_w[PAIR_AT : PAIR_AT + 128, :] = stacked(jnp.concatenate([dw[k] for k in range(4)], axis=1))
    enc_w[PAIR_AT + 128 :, :192] = forms(jnp.concatenate([dw[k].T for k in range(4)], axis=0))
    dec_w[PAIR_AT : PAIR_AT + 128, :] = stacked(jnp.concatenate([uw[k].T for k in range(4)], axis=1))
    dec_w[PAIR_AT + 128 :, :192] = forms(jnp.concatenate([uw[k] for k in range(4)], axis=0))


def one_hot(ids_row, first, count):
    row = lax.broadcasted_iota(jnp.int32, (count, ids_row.shape[1]), 0) + first
    return jnp.where(row == ids_row, 1.0, 0.0).astype(BF)


def pick(ids, cbt, chosen, begin, end, step):
    for start in range(begin, end, step):
        at = slice(start - begin, start - begin + step)
        to = slice(start, start + step)
        both = dot(cbt[...], one_hot(ids[0:1, at], 0, CODES))
        chosen[:, to] = both[:CH] + both[CH:]


def stack_forward(x_ref, z_refs, blocks, dils, w, bias, mf, keep, last):
    def enter(value, start, size, b):
        act, slope = gelu_both(value)
        hi, lo = split(act)
        a_ref, gx_ref, _, _ = keep(b)
        a_ref[:CH, pl.ds(aligned(start), size)] = hi
        a_ref[CH:, pl.ds(aligned(start), size)] = lo
        gx_ref[:, pl.ds(aligned(start), size)] = slope
        z_refs[b % 2][:, pl.ds(aligned(start), size)] = dot(
            part(w, "conv", b), jnp.concatenate([hi, lo, hi], axis=0)
        )

    def first(start, size, core):
        enter(lanes(x_ref, start, size), start, size, 0)

    sweep(first)
    for b in range(4):
        d = dils[b]
        m = DILATIONS.index(d)
        z_ref = z_refs[b % 2]

        def step(start, size, core, b=b, d=d, m=m, z_ref=z_ref):
            _, _, u_ref, gh_ref = keep(b)
            times = size // 128
            left = tile_rows(lanes(mf, start, size, slice(16 * m, 16 * m + 8)), 8)
            right = tile_rows(lanes(mf, start, size, slice(16 * m + 8, 16 * m + 16)), 8)
            cb = jnp.concatenate([bias[2 * (blocks + b)]] * times, axis=1)
            hidden = lanes(z_ref, start, size, slice(CH, 2 * CH)) + cb
            hidden = hidden + left * from_left(z_ref, slice(0, CH), start, size, d, EXT)
            hidden = hidden + right * from_right(z_ref, slice(2 * CH, 3 * CH), start, size, d, EXT)
            act, slope = gelu_both(hidden)
            hi, lo = split(act)
            u_ref[:CH, pl.ds(aligned(start), size)] = hi
            u_ref[CH:, pl.ds(aligned(start), size)] = lo
            gh_ref[:, pl.ds(aligned(start), size)] = slope
            pbias = jnp.concatenate([bias[2 * (blocks + b) + 1]] * times, axis=1)
            out = (
                lanes(x_ref, start, size)
                + dot(part(w, "proj", b), jnp.concatenate([hi, lo, hi], axis=0))
                + pbias
            )
            if b < 3:
                x_ref[:, pl.ds(aligned(start), size)] = out
                enter(out, start, size, b + 1)
            else:
                last(out, start, size, core)

        sweep(step)


def stack_backward(g_ref, gh_refs, blocks, dils, w, mb, keep, acc, finish, last):
    dk1, dk2, dpa, csum, psum = acc

    def enter(grad, start, size, core, b):
        _, _, u_ref, slope_ref = keep(b)
        hi, lo = split(grad)
        q = dot(part(w, "proj_back", b), jnp.concatenate([hi, lo, hi], axis=0))
        gh = lanes(slope_ref, start, size) * q
        ghi, glo = split(gh)
        gh_refs[b % 2][:CH, pl.ds(aligned(start), size)] = ghi
        gh_refs[b % 2][CH:, pl.ds(aligned(start), size)] = glo
        if core:
            dpa[b] += dot_nt(jnp.concatenate([hi, lo], axis=0), lanes(u_ref, start, size))
            csum[b] += lane_fold(gh)
            psum[b] += lane_fold(grad)

    for ref in acc:
        ref[...] = jnp.zeros(ref.shape, ref.dtype)

    def first(start, size, core):
        enter(lanes(g_ref, start, size), start, size, core, 3)

    sweep(first)
    for b in (3, 2, 1, 0):
        d = dils[b]
        m = DILATIONS.index(d)
        gh_ref = gh_refs[b % 2]

        def step(start, size, core, b=b, d=d, m=m, gh_ref=gh_ref):
            a_ref, gx_ref, _, _ = keep(b)
            left = tile_rows(lanes(mb, start, size, slice(32 * m, 32 * m + 16)), 4)
            right = tile_rows(lanes(mb, start, size, slice(32 * m + 16, 32 * m + 32)), 4)
            parts = []
            for rows in (slice(0, CH), slice(CH, 2 * CH)):
                parts.append(
                    jnp.concatenate(
                        [
                            from_right(gh_ref, rows, start, size, d, EXT) * right,
                            lanes(gh_ref, start, size, rows),
                            from_left(gh_ref, rows, start, size, d, EXT) * left,
                        ],
                        axis=0,
                    )
                )
            ghi, glo = parts
            both = dot(part(w, "conv_back", b), ghi)
            ga = both[:CH] + both[CH:] + dot(part(w, "conv_back", b)[:CH], glo)
            if core:
                act = lanes(a_ref, start, size)
                dk1[b] += dot_nt(ghi, act)
                dk2[b] += dot_nt(glo, act[:CH])
            out = lanes(g_ref, start, size) + lanes(gx_ref, start, size) * ga
            if b > 0:
                g_ref[:, pl.ds(aligned(start), size)] = out
                enter(out, start, size, core, b - 1)
            else:
                last(out, start, size, core)

        sweep(step)
    for b in range(4):
        dk = dk1[b, :, :CH] + dk1[b, :, CH:] + dk2[b]
        dp = dpa[b, :CH, :CH] + dpa[b, CH:, :CH] + dpa[b, :CH, CH:]
        finish(b, dk, dp, csum[b], psum[b])


def store_grads(grads, folded):
    kept = {}

    def finish(b, dk, dp, csum, psum):
        kept[b] = (dk, dp)
        if b % 2:
            at = b // 2
            grads[at * 192 : (at + 1) * 192, :] = jnp.concatenate([kept[b - 1][0], dk], axis=1)
            grads[GRAD_PROJ + at * CH : GRAD_PROJ + (at + 1) * CH, :] = jnp.concatenate(
                [kept[b - 1][1], dp], axis=1
            )
        folded.extend([csum, psum])

    return finish


def store_columns(grads, folded):
    lane = lax.broadcasted_iota(jnp.int32, (CH, 128), 1)
    totals = [jnp.sum(v, axis=1, keepdims=True) for v in folded]
    out = jnp.zeros((CH, 128), F32)
    for at, total in enumerate(totals):
        out = jnp.where(lane == at, total, out)
    grads[GRAD_BIAS:, :] = out


def to_halves(value, sel, e_ref, o_ref, start, size):
    hi, lo = split(value)
    both = jnp.concatenate([hi, lo], axis=0)
    half = start // 2
    for i in range(size // 256):
        out = dot(both[:, i * 256 : (i + 1) * 256], sel).astype(BF)
        e_ref[:, pl.ds(aligned(half + i * 128), 128)] = out[:, :128]
        o_ref[:, pl.ds(aligned(half + i * 128), 128)] = out[:, 128:]


def pair_stack(e_ref, o_ref, mhb, start, size):
    masks = [tile_rows(lanes(mhb, start, size, slice(16 * i, 16 * i + 16)), 4) for i in range(3)]
    parts = []
    for rows in (slice(0, CH), slice(CH, 2 * CH)):
        parts.append(
            jnp.concatenate(
                [
                    from_left(o_ref, rows, start, size, 1, HEXT) * masks[0],
                    lanes(e_ref, start, size, rows),
                    lanes(o_ref, start, size, rows) * masks[1],
                    from_right(e_ref, rows, start, size, 1, HEXT) * masks[2],
                ],
                axis=0,
            )
        )
    return parts


def pair_gather(w, parts):
    both = dot(w[...], parts[0])
    return both[:CH] + both[CH:] + dot(w[:CH], parts[1])


def spread(w, hl_ref, mh, z_refs, sel, bias_tile, x_ref):
    def first(start, size, core):
        both = lanes(hl_ref, start, size)
        z = dot(w, jnp.concatenate([both, both[:CH]], axis=0))
        masks = [tile_rows(lanes(mh, start, size, slice(8 * i, 8 * i + 8)), 8) for i in range(3)]
        at = pl.ds(aligned(start), size)
        z_refs[0][:, at] = z[0:64] * masks[0]
        z_refs[1][:, at] = z[64:128]
        z_refs[2][:, at] = z[128:192] * masks[1]
        z_refs[3][:, at] = z[192:256] * masks[2]

    half_sweep(first)

    def second(start, size, core):
        every = slice(None)
        even = lanes(z_refs[1], start, size) + from_left(z_refs[3], every, start, size, 1, HEXT)
        odd = lanes(z_refs[2], start, size) + from_right(z_refs[0], every, start, size, 1, HEXT)
        ehi, elo = split(even)
        ohi, olo = split(odd)
        for i in range(size // 128):
            cut = slice(i * 128, (i + 1) * 128)
            rows = jnp.concatenate(
                [
                    jnp.concatenate([ehi[:, cut], ohi[:, cut]], axis=1),
                    jnp.concatenate([elo[:, cut], olo[:, cut]], axis=1),
                ],
                axis=0,
            )
            out = dot_nt(rows, sel)
            out = out[:CH] + out[CH:]
            if bias_tile is not None:
                out = out + jnp.concatenate([bias_tile, bias_tile], axis=1)
            x_ref[:, pl.ds(aligned(2 * start + 256 * i), 256)] = out

    half_sweep(second)


def ring_fill(ref, core, hi, lo):
    if core is not None:
        ref[:, :CORE] = core
    ref[:, CORE : CORE + HALO] = hi
    ref[:, CORE + HALO :] = lo


def find_links(clip_ref, sel, mf, mb, mh, mhb):
    def links(start, size, core):
        at = pl.ds(aligned(start), size)
        here = lanes(clip_ref, start, size)

        def same(other):
            return jnp.where(other == here, 1.0, 0.0)

        for m, d in enumerate(DILATIONS):
            left = same(from_left(clip_ref, slice(None), start, size, d, EXT))
            right = same(from_right(clip_ref, slice(None), start, size, d, EXT))
            mf[16 * m : 16 * m + 8, at] = left
            mf[16 * m + 8 : 16 * m + 16, at] = right
            mb[32 * m : 32 * m + 16, at] = tile_rows(left, 2).astype(BF)
            mb[32 * m + 16 : 32 * m + 32, at] = tile_rows(right, 2).astype(BF)
            if m == 0:
                two = same(from_right(clip_ref, slice(None), start, size, 2, EXT))
                rows = jnp.concatenate([left, right, two, two], axis=0).astype(BF)
                half = start // 2
                for i in range(size // 256):
                    out = dot(rows[:, i * 256 : (i + 1) * 256], sel)[:, :128]
                    hat = pl.ds(aligned(half + 128 * i), 128)
                    mh[:, hat] = out[:24]
                    for n in range(3):
                        mhb[16 * n : 16 * n + 16, hat] = tile_rows(
                            out[8 * n : 8 * n + 8], 2
                        ).astype(BF)

    sweep(links)


def sum_refs():
    return [
        pltpu.VMEM((4, 3 * CH, 2 * CH), F32),
        pltpu.VMEM((4, 3 * CH, CH), F32),
        pltpu.VMEM((4, 2 * CH, 2 * CH), F32),
        pltpu.VMEM((4, CH, 128), F32),
        pltpu.VMEM((4, CH, 128), F32),
    ]


def state_refs():
    return [
        whole(),
        whole(rows=192),
        whole(rows=192),
        pltpu.VMEM((4, 128, EXT), BF),
        pltpu.VMEM((4, CH, EXT), F32),
        pltpu.VMEM((4, 128, EXT), BF),
        pltpu.VMEM((4, CH, EXT), F32),
        whole(),
        whole(BF, 128),
        whole(BF, 128),
        halves(),
        halves(),
        *sum_refs(),
    ]


def decode_kernel(
    cot, lo, hi, clip, chosen_in, cbt, weights, bias,
    rebuilt, quant_grad, grads, mf, mb, mh, mhb, chosen, chosen_hl, ids,
    up1, up2, usum, clip_ref, sems, x_ref, z0, z1, a_s, gx_s, u_s, gh_s, g_ref, g0, g1, e_ref, o_ref,
    *acc,
):
    ug = weights.at[PAIR_AT : PAIR_AT + 128]
    us = weights[PAIR_AT + 128 :, :192]
    cot_in = pltpu.make_async_copy(cot, g_ref.at[:, :CORE], sems.at[0])
    cot_in.start()
    sel = selector()
    ring_fill(
        clip_ref,
        jnp.broadcast_to(clip[...].astype(F32), (8, CORE)),
        jnp.broadcast_to(hi[128:129], (8, HALO)),
        jnp.broadcast_to(lo[128:129], (8, HALO)),
    )
    find_links(clip_ref, sel, mf, mb, mh, mhb)
    chosen[:, :HCORE] = chosen_in[...]
    ids[...] = jnp.broadcast_to((hi[129:130] + lo[129:130]).astype(jnp.int32), (8, HALO))
    pick(ids, cbt, chosen, HCORE, HEXT, HALO)
    chi, clo = split(chosen[...])
    chosen_hl[:CH] = chi
    chosen_hl[CH:] = clo
    zu = [z0.at[:CH], z0.at[CH : 2 * CH], z0.at[2 * CH :], z1.at[:CH]]
    spread(us, chosen_hl, mh, zu, sel, bias[17], x_ref)

    def keep(b):
        return a_s.at[b], gx_s.at[b], u_s.at[b], gh_s.at[b]

    def last(out, start, size, core):
        if core:
            x_ref[:, pl.ds(aligned(start), size)] = out

    order = DILATIONS[::-1]
    stack_forward(x_ref, (z0, z1), 4, order, weights, bias, mf, keep, last)
    rebuilt_out = pltpu.make_async_copy(x_ref.at[:, :CORE], rebuilt, sems.at[1])
    rebuilt_out.start()
    cot_in.wait()
    ring_fill(g_ref, None, hi[CH : 2 * CH], lo[CH : 2 * CH])
    for ref in (up1, up2, usum):
        ref[...] = jnp.zeros(ref.shape, F32)
    folded = []

    def last_back(out, start, size, core):
        to_halves(out, sel, e_ref, o_ref, start, size)
        if core:
            usum[...] += lane_fold(out)

    stack_backward(
        g_ref, (g0, g1), 4, order, weights, mb, keep, acc, store_grads(grads, folded), last_back
    )

    def up(start, size, core):
        parts = pair_stack(e_ref, o_ref, mhb, start, size)
        quant_grad[:, pl.ds(aligned(start), size)] = pair_gather(ug, parts)
        if core:
            both = lanes(chosen_hl, start, size)
            up1[...] += dot_nt(parts[0], both)
            up2[...] += dot_nt(parts[1], both[:CH])

    half_sweep(up)
    total = up1[:, :CH] + up1[:, CH:] + up2[...]
    grads[GRAD_PAIR:GRAD_BIAS, :] = jnp.concatenate([total[: 2 * CH], total[2 * CH :]], axis=1)
    store_columns(grads, folded + [usum[...]])
    rebuilt_out.wait()


def encode_kernel(
    frames, lo, hi, codes, quant_grad, dec_grads, chosen, mf, mb, mh, mhb, weights, bias,
    frames_grad, sums,
    d_ref, l_ref, down1, down2, dsum, sems,
    x_ref, z0, z1, a_s, gx_s, u_s, gh_s, g_ref, g0, g1, e_ref, o_ref, *acc,
):
    dg = weights.at[PAIR_AT : PAIR_AT + 128]
    ds_ = weights[PAIR_AT + 128 :, :192]
    sel = selector()
    ring_fill(x_ref, frames[...], hi[:CH], lo[:CH])
    grads = sums.at[CODE_ROWS : CODE_ROWS + GRAD_ROWS]
    sums[CODE_ROWS + GRAD_ROWS :, :] = dec_grads[...]

    def keep(b):
        return a_s.at[b], gx_s.at[b], u_s.at[b], gh_s.at[b]

    def last(out, start, size, core):
        to_halves(out, sel, e_ref, o_ref, start, size)

    stack_forward(x_ref, (z0, z1), 0, DILATIONS, weights, bias, mf, keep, last)
    for ref in (down1, down2, dsum):
        ref[...] = jnp.zeros(ref.shape, F32)
    folded = []

    def down(start, size, core):
        at = pl.ds(aligned(start), size)
        parts = pair_stack(e_ref, o_ref, mhb, start, size)
        value = pair_gather(dg, parts) + jnp.concatenate([bias[16]] * (size // 128), axis=1)
        gap = value - lanes(chosen, start, size)
        grad = quant_grad[:, at] + (2.0 * COMMIT) * gap
        hi, lo = split(grad)
        l_ref[:CH, at] = hi
        l_ref[CH:, at] = lo
        if core:
            dhi, dlo = split(-2.0 * gap)
            d_ref[:CH, at] = dhi
            d_ref[CH:, at] = dlo
            dsum[...] += lane_fold(grad)
            down1[...] += dot_nt(jnp.concatenate([hi, lo], axis=0), parts[0])
            down2[...] += dot_nt(hi, parts[1])

    half_sweep(down)
    def codes_back(i, carry):
        hot = one_hot(codes[...], i * 512, 512)
        out = dot_nt(d_ref[...], hot)
        out = out[:CH] + out[CH:]
        at = pl.multiple_of(i * 256, 256)
        for n in range(4):
            sums[pl.ds(at + CH * n, CH), :] = out[:, 128 * n : 128 * (n + 1)]
        return carry

    lax.fori_loop(0, CODES // 512, codes_back, 0)
    zu = [z0.at[:CH], z0.at[CH : 2 * CH], z0.at[2 * CH :], z1.at[:CH]]
    spread(ds_, l_ref, mh, zu, sel, None, g_ref)

    leaving = []

    def last_back(out, start, size, core):
        if core:
            at = pl.ds(start, size)
            x_ref[:, at] = out
            leaving.append(
                pltpu.make_async_copy(x_ref.at[:, at], frames_grad.at[:, at], sems.at[len(leaving)])
            )
            leaving[-1].start()

    stack_backward(
        g_ref, (g0, g1), 0, DILATIONS, weights, mb, keep, acc, store_grads(grads, folded), last_back
    )
    total = down1[:CH] + down1[CH:] + down2[...]
    grads[GRAD_PAIR : GRAD_PAIR + CH, :] = total[:, : 2 * CH]
    grads[GRAD_PAIR + CH : GRAD_BIAS, :] = total[:, 2 * CH :]
    store_columns(grads, folded + [dsum[...]])
    for copy in leaving:
        copy.wait()


def unpack_kernel(
    sums,
    cg, ec, ecb, ep, epb, dw, db, uw, ub, dc, dcb, dp, dpb,
):
    for i in range(CODES // 128):
        cg[:, i * 128 : (i + 1) * 128] = sums[i * CH : (i + 1) * CH, :]
    enc = sums.at[CODE_ROWS : CODE_ROWS + GRAD_ROWS]
    dec = sums.at[CODE_ROWS + GRAD_ROWS :]
    for src, conv, cbias, proj, pbias, single in (
        (enc, ec, ecb, ep, epb, db),
        (dec, dc, dcb, dp, dpb, ub),
    ):
        rows = src[GRAD_BIAS:, :].T
        for b in range(4):
            at = slice((b % 2) * CH, (b % 2 + 1) * CH)
            p = b // 2
            conv[b] = src[p * 192 : (p + 1) * 192, at].reshape(3, CH, CH)
            proj[b] = src[GRAD_PROJ + p * CH : GRAD_PROJ + (p + 1) * CH, at]
            cbias[b : b + 1, :] = rows[2 * b : 2 * b + 1]
            pbias[b : b + 1, :] = rows[2 * b + 1 : 2 * b + 2]
        single[...] = rows[8:9]
    for k in range(4):
        a, b = k // 2, k % 2
        dw[k] = enc[GRAD_PAIR + a * CH : GRAD_PAIR + (a + 1) * CH, b * CH : (b + 1) * CH]
        uw[k] = dec[GRAD_PAIR + b * CH : GRAD_PAIR + (b + 1) * CH, a * CH : (a + 1) * CH]


def shape(dims, kind=F32):
    return jax.ShapeDtypeStruct(dims, kind)


def call(kernel, outs, scratch=(), flops=0, limit=40, in_specs=None, out_specs=None):
    extra = {}
    if in_specs is not None:
        extra["in_specs"] = in_specs
    if out_specs is not None:
        extra["out_specs"] = out_specs
    return pl.pallas_call(
        kernel,
        out_shape=outs,
        scratch_shapes=list(scratch),
        compiler_params=pltpu.CompilerParams(vmem_limit_bytes=limit * MB),
        cost_estimate=pl.CostEstimate(flops=flops, bytes_accessed=2**20, transcendentals=0),
        **extra,
    )


def halves(kind=BF, rows=2 * CH):
    return pltpu.VMEM((rows, HEXT), kind)


def whole(kind=F32, rows=CH):
    return pltpu.VMEM((rows, EXT), kind)


FAR = pl.BlockSpec(memory_space=pltpu.HBM)


def far(*values):
    return [pltpu.with_memory_space_constraint(v, pltpu.HBM) for v in values]
LOCAL = pl.BlockSpec()


def local_pack(frames, cot, clip, codes):
    return call(
        pack_kernel,
        [shape((136, HALO)), shape((136, HALO))],
        [
            pltpu.VMEM((1, CORE), jnp.int32),
            pltpu.VMEM((1, HCORE), jnp.int32),
            pltpu.SemaphoreType.DMA((6,)),
        ],
        in_specs=[FAR] * 4,
    )(*far(frames, cot, clip, codes))


def local_prep(*args):
    return call(
        prep_kernel,
        [
            shape((WEIGHT_ROWS, 256), BF),
            shape((WEIGHT_ROWS, 256), BF),
            shape((18, CH, 128)),
            shape((128, CODES), BF),
            shape((CH, HCORE)),
        ],
        [pltpu.VMEM(a.shape, a.dtype) for a in args] + [pltpu.SemaphoreType.DMA((14,))],
        flops=10**7,
        limit=40,
        in_specs=[FAR] * 14,
    )(*far(*args))


def local_decode(cot, *args):
    return call(
        decode_kernel,
        [
            shape((CH, CORE)),
            shape((CH, HEXT)),
            shape((GRAD_ROWS, 128)),
            shape((64, EXT)),
            shape((128, EXT), BF),
            shape((24, HEXT)),
            shape((48, HEXT), BF),
            shape((CH, HEXT)),
        ],
        [
            halves(),
            pltpu.VMEM((8, HALO), jnp.int32),
            pltpu.VMEM((256, 128), F32),
            pltpu.VMEM((256, CH), F32),
            pltpu.VMEM((CH, 128), F32),
            whole(rows=8),
            pltpu.SemaphoreType.DMA((2,)),
            *state_refs(),
        ],
        flops=2 * 10**10,
        limit=40,
        in_specs=[FAR] + [LOCAL] * 7,
        out_specs=[FAR] + [LOCAL] * 7,
    )(*far(cot), *args)


def local_encode(*args):
    return call(
        encode_kernel,
        [shape((CH, CORE)), shape((ALL_ROWS, 128))],
        [
            pltpu.VMEM((2 * CH, HCORE), BF),
            halves(),
            pltpu.VMEM((128, 256), F32),
            pltpu.VMEM((CH, 256), F32),
            pltpu.VMEM((CH, 128), F32),
            pltpu.SemaphoreType.DMA((CORE // STEP,)),
            *state_refs(),
        ],
        flops=2 * 10**10,
        limit=40,
        in_specs=[LOCAL] * 13,
        out_specs=[FAR, LOCAL],
    )(*args)


def local_unpack(sums):
    block = [shape((4, 3, CH, CH)), shape((4, CH)), shape((4, CH, CH)), shape((4, CH))]
    return call(
        unpack_kernel,
        [
            shape((CH, CODES)),
            *block,
            shape((4, CH, CH)),
            shape((1, CH)),
            shape((4, CH, CH)),
            shape((1, CH)),
            *block,
        ],
    )(sums)


AXES = ("tm", "batch")


def rounds():
    tm, batch = lax.axis_size("tm"), lax.axis_size("batch")
    rings = []
    stride = 2
    while stride < tm:
        size = min(4, tm // stride)
        rings.append(("tm", stride, size))
        stride *= size
    rings.append(("batch", 1, batch))
    devices = [(t, b) for t in range(tm) for b in range(batch)]

    def digit_of(ring, t, b):
        axis, stride, size = ring
        return (t if axis == "tm" else b) // stride % size

    def moved(ring, t, b, n):
        axis, stride, size = ring
        here = digit_of(ring, t, b)
        to = here ^ 1 if n == 0 else 3 - here
        t, b = (t + (to - here) * stride, b) if axis == "tm" else (t, b + (to - here) * stride)
        return t * batch + b

    steps = [(ring, n) for ring in rings for n in range(ring[2] // 2)]
    late = [(ring, n) for ring in rings[1:] + rings[:1] for n in range(ring[2] // 2)]
    me = (lax.axis_index("tm"), lax.axis_index("batch"))

    def bit_of(step):
        digit = digit_of(step[0], *me)
        return (digit ^ (digit // 2)) % 2 if step[1] == 0 else digit // 2

    out = [([(t * batch + b, (t ^ 1) * batch + b) for t, b in devices], me[0] % 2)]
    for plans in zip(steps, late):
        pairs = [(t * batch + b, moved(*plans[t % 2][:1], t, b, plans[t % 2][1])) for t, b in devices]
        out.append((pairs, jnp.where(me[0] % 2 == 0, bit_of(plans[0]), bit_of(plans[1]))))
    return out


SCATTER = 3


def sum_all(value):
    plan = rounds()
    for n, (pairs, bit) in enumerate(plan):
        if n < SCATTER:
            half = value.shape[0] // 2
            mine = lax.dynamic_slice_in_dim(value, bit * half, half, 0)
            other = lax.dynamic_slice_in_dim(value, (1 - bit) * half, half, 0)
            value = mine + lax.ppermute(other, AXES, pairs)
        else:
            value = value + lax.ppermute(value, AXES, pairs)
    for pairs, bit in plan[:SCATTER][::-1]:
        other = lax.ppermute(value, AXES, pairs)
        half = value.shape[0]
        out = jnp.zeros((2 * half, value.shape[1]), value.dtype)
        out = lax.dynamic_update_slice_in_dim(out, value, bit * half, 0)
        value = lax.dynamic_update_slice_in_dim(out, other, (1 - bit) * half, 0)
    return value


def on_device(
    frames, clip_start, code_ids, cotangent,
    enc_conv, enc_conv_bias, enc_proj, enc_proj_bias, downscale_weight, downscale_bias,
    codebook, up_weight, up_bias, dec_conv, dec_conv_bias, dec_proj, dec_proj_bias,
):
    frames = frames.reshape(CH, CORE)
    cotangent = cotangent.reshape(CH, CORE)
    front, tail = local_pack(frames, cotangent, clip_start, code_ids)
    count = lax.axis_size("tm")
    ring = [(i, (i + 1) % count) for i in range(count)]
    lo = lax.ppermute(tail, "tm", ring)
    hi = lax.ppermute(front, "tm", [(j, i) for i, j in ring])
    enc_w, dec_w, bias, cbt, chosen = local_prep(
        enc_conv, enc_conv_bias, enc_proj, enc_proj_bias,
        downscale_weight, downscale_bias.reshape(1, CH),
        codebook.T, up_weight, up_bias.reshape(1, CH),
        dec_conv, dec_conv_bias, dec_proj, dec_proj_bias, code_ids,
    )
    rebuilt, quant_grad, dec_grads, mf, mb, mh, mhb, chosen = local_decode(
        cotangent, lo, hi, clip_start, chosen, cbt, dec_w, bias
    )
    frames_grad, sums = local_encode(
        frames, lo, hi, code_ids, quant_grad, dec_grads, chosen, mf, mb, mh, mhb,
        enc_w, bias,
    )
    out = list(local_unpack(sum_all(sums)))
    cg = out.pop(0).T
    out[5] = out[5].reshape(CH)
    out[7] = out[7].reshape(CH)
    out.insert(6, cg)
    return (rebuilt[None], frames_grad[None], *out)


def solution(mesh):
    split_spec = P("batch", None, "tm")
    row_spec = P("batch", "tm")
    return jax.shard_map(
        on_device,
        mesh=mesh,
        in_specs=(split_spec, row_spec, row_spec, split_spec) + (P(),) * 13,
        out_specs=(split_spec, split_spec) + (P(),) * 13,
        check_vma=False,
    )
```

```python
import functools

import jax
import jax.numpy as jnp
from jax import lax
from jax.experimental import pallas as pl
from jax.experimental.pallas import tpu as pltpu
from jax.sharding import PartitionSpec as P

COMMIT = 0.02
DILATIONS = (1, 3, 9, 27)
BF = jnp.bfloat16
F32 = jnp.float32
CH = 64
CODES = 2048
CORE = 4096
HALO = 128
EXT = CORE + 2 * HALO
HCORE = CORE // 2
HEXT = EXT // 2
STEP = 1024
G0 = 0.7978845608028654
G1 = G0 * 0.044715
MB = 2**20
GRAD_PROJ = 384
GRAD_PAIR = 512
GRAD_BIAS = 640
GRAD_ROWS = 704
CODE_ROWS = CODES // 2
DEC_CUT = 192
SUM_ROWS = CODE_ROWS + DEC_CUT


BLOCK_ROWS = 448
PAIR_AT = 4 * BLOCK_ROWS
WEIGHT_ROWS = PAIR_AT + 384


PARTS = {"conv": (0, 192), "conv_back": (192, 128), "proj": (320, 64), "proj_back": (384, 64)}


def part_rows(name, b):
    first, rows = PARTS[name]
    return slice(BLOCK_ROWS * b + first, BLOCK_ROWS * b + first + rows)


def part(w, name, b):
    return w[part_rows(name, b), :192]


def dot(a, b):
    return jnp.dot(a, b, preferred_element_type=F32)


def dot_nt(a, b):
    return lax.dot_general(a, b, (((1,), (1,)), ((), ())), preferred_element_type=F32)


def split(v):
    hi = v.astype(BF)
    return hi, (v - hi.astype(F32)).astype(BF)


def gelu_both(v):
    s = v * v
    t = jnp.tanh(v * (G0 + G1 * s))
    cdf = 0.5 + 0.5 * t
    slope = cdf + (0.5 * v) * (1.0 - t * t) * (G0 + (3.0 * G1) * s)
    return v * cdf, slope


def tile_rows(rows, times):
    return jnp.concatenate([rows] * times, axis=0)


def aligned(start):
    return start if isinstance(start, int) else pl.multiple_of(start, 128)


def lanes(ref, start, size, rows=slice(None)):
    return ref[rows, pl.ds(aligned(start), size)]


def wrap(start, length):
    return start % length if isinstance(start, int) else lax.rem(start + length, length)


def from_left(ref, rows, start, size, offset, length):
    win = jnp.concatenate(
        [lanes(ref, wrap(start - 128, length), 128, rows), lanes(ref, start, size, rows)], axis=1
    )
    return pltpu.roll(win, offset, 1)[:, 128:]


def from_right(ref, rows, start, size, offset, length):
    win = jnp.concatenate(
        [lanes(ref, start, size, rows), lanes(ref, wrap(start + size, length), 128, rows)], axis=1
    )
    return pltpu.roll(win, size + 128 - offset, 1)[:, :size]


def sweep(fn, step=STEP):
    for i in range(CORE // step):
        fn(i * step, step, True)
    fn(CORE, 2 * HALO, False)


def half_sweep(fn, step=STEP // 2):
    for i in range(HCORE // step):
        fn(i * step, step, True)
    fn(HCORE, HALO, False)


def lane_fold(v):
    out = v[:, :128]
    for i in range(1, v.shape[1] // 128):
        out = out + v[:, i * 128 : (i + 1) * 128]
    return out


def selector():
    row = lax.broadcasted_iota(jnp.int32, (256, 256), 0)
    col = lax.broadcasted_iota(jnp.int32, (256, 256), 1)
    source = jnp.where(col < 128, 2 * col, 2 * (col - 128) + 1)
    return jnp.where(row == source, 1.0, 0.0).astype(BF)


def pack_kernel(frames, cot, clip, codes, front, tail, clip_v, codes_v, sems):
    first, final = slice(0, HALO), slice(CORE - HALO, CORE)
    copies = [
        pltpu.make_async_copy(src, dst, sems.at[n])
        for n, (src, dst) in enumerate(
            (
                (frames.at[:, first], front.at[:CH]),
                (frames.at[:, final], tail.at[:CH]),
                (cot.at[:, first], front.at[CH : 2 * CH]),
                (cot.at[:, final], tail.at[CH : 2 * CH]),
                (clip, clip_v),
                (codes, codes_v),
            )
        )
    ]
    for copy in copies:
        copy.start()
    for copy in copies:
        copy.wait()
    me = lax.axis_index("tm")
    count = lax.axis_size("tm")
    lane = lax.broadcasted_iota(jnp.int32, (1, HALO), 1)
    blank = jnp.zeros((6, HALO), F32)
    for out, cut, at_end, half, keep in (
        (front, first, me == 0, slice(0, HALO), lane < 64),
        (tail, final, me == count - 1, slice(HCORE - HALO, HCORE), lane >= 64),
    ):
        clip_row = jnp.where(at_end, -1.0, clip_v[:, cut].astype(F32))
        code_row = jnp.where(keep, codes_v[:, half].astype(F32), 0.0)
        out[2 * CH :, :] = jnp.concatenate([clip_row, code_row, blank], axis=0)


def prep_kernel(*refs):
    sources, outs, scratch = refs[:14], refs[14:19], refs[19:]
    sems = scratch[-1]
    copies = [
        pltpu.make_async_copy(src, dst, sems.at[n])
        for n, (src, dst) in enumerate(zip(sources, scratch[:14]))
    ]
    first = (6, 13)
    for n in (*first, *range(6), *range(7, 13)):
        copies[n].start()
    for n in first:
        copies[n].wait()
    ec, ecb, ep, epb, dw, db, cb, uw, ub, dc, dcb, dp, dpb, codes = scratch[:14]
    enc_w, dec_w, bias, cbt, chosen = outs

    def forms(w):
        hi, lo = split(w)
        return jnp.concatenate([hi, hi, lo], axis=1)

    def stacked(w):
        hi, lo = split(w)
        return jnp.concatenate([hi, lo], axis=0)

    def column(row):
        return jnp.broadcast_to(row, (128, CH)).T

    cbt[...] = stacked(cb[...])
    pick(codes, cbt, chosen, 0, HCORE, 1024)
    for n in (*range(6), *range(7, 13)):
        copies[n].wait()
    for n, (conv, cbias, proj, pbias) in enumerate(((ec, ecb, ep, epb), (dc, dcb, dp, dpb))):
        weights = (enc_w, dec_w)[n]
        for b in range(4):
            at = 4 * n + b
            weights[part_rows("conv", b), :192] = forms(conv[b].reshape(3 * CH, CH))
            weights[part_rows("conv_back", b), :192] = stacked(jnp.concatenate([conv[b, k].T for k in range(3)], axis=1))
            weights[part_rows("proj", b), :192] = forms(proj[b])
            weights[part_rows("proj_back", b), :192] = forms(proj[b].T)
            bias[2 * at] = column(cbias[b : b + 1, :])
            bias[2 * at + 1] = column(pbias[b : b + 1, :])
    bias[16] = column(db[...])
    bias[17] = column(ub[...])
    enc_w[PAIR_AT : PAIR_AT + 128, :] = stacked(jnp.concatenate([dw[k] for k in range(4)], axis=1))
    enc_w[PAIR_AT + 128 :, :192] = forms(jnp.concatenate([dw[k].T for k in range(4)], axis=0))
    dec_w[PAIR_AT : PAIR_AT + 128, :] = stacked(jnp.concatenate([uw[k].T for k in range(4)], axis=1))
    dec_w[PAIR_AT + 128 :, :192] = forms(jnp.concatenate([uw[k] for k in range(4)], axis=0))


def one_hot(ids_row, first, count):
    row = lax.broadcasted_iota(jnp.int32, (count, ids_row.shape[1]), 0) + first
    return jnp.where(row == ids_row, 1.0, 0.0).astype(BF)


def pick(ids, cbt, chosen, begin, end, step):
    for start in range(begin, end, step):
        at = slice(start - begin, start - begin + step)
        to = slice(start, start + step)
        both = dot(cbt[...], one_hot(ids[0:1, at], 0, CODES))
        chosen[:, to] = both[:CH] + both[CH:]


def stack_forward(x_ref, z_refs, blocks, dils, w, bias, mf, keep, last):
    def enter(value, start, size, b):
        act, slope = gelu_both(value)
        hi, lo = split(act)
        a_ref, gx_ref, _, _ = keep(b)
        a_ref[:CH, pl.ds(aligned(start), size)] = hi
        a_ref[CH:, pl.ds(aligned(start), size)] = lo
        gx_ref[:, pl.ds(aligned(start), size)] = slope
        z_refs[b % 2][:, pl.ds(aligned(start), size)] = dot(
            part(w, "conv", b), jnp.concatenate([hi, lo, hi], axis=0)
        )

    def first(start, size, core):
        enter(lanes(x_ref, start, size), start, size, 0)

    sweep(first)
    for b in range(4):
        d = dils[b]
        m = DILATIONS.index(d)
        z_ref = z_refs[b % 2]

        def step(start, size, core, b=b, d=d, m=m, z_ref=z_ref):
            _, _, u_ref, gh_ref = keep(b)
            times = size // 128
            left = tile_rows(lanes(mf, start, size, slice(16 * m, 16 * m + 8)), 8)
            right = tile_rows(lanes(mf, start, size, slice(16 * m + 8, 16 * m + 16)), 8)
            cb = jnp.concatenate([bias[2 * (blocks + b)]] * times, axis=1)
            hidden = lanes(z_ref, start, size, slice(CH, 2 * CH)) + cb
            hidden = hidden + left * from_left(z_ref, slice(0, CH), start, size, d, EXT)
            hidden = hidden + right * from_right(z_ref, slice(2 * CH, 3 * CH), start, size, d, EXT)
            act, slope = gelu_both(hidden)
            hi, lo = split(act)
            u_ref[:CH, pl.ds(aligned(start), size)] = hi
            u_ref[CH:, pl.ds(aligned(start), size)] = lo
            gh_ref[:, pl.ds(aligned(start), size)] = slope
            pbias = jnp.concatenate([bias[2 * (blocks + b) + 1]] * times, axis=1)
            out = (
                lanes(x_ref, start, size)
                + dot(part(w, "proj", b), jnp.concatenate([hi, lo, hi], axis=0))
                + pbias
            )
            if b < 3:
                x_ref[:, pl.ds(aligned(start), size)] = out
                enter(out, start, size, b + 1)
            else:
                last(out, start, size, core)

        sweep(step)


def stack_backward(g_ref, gh_refs, blocks, dils, w, mb, keep, acc, finish, last):
    dk1, dk2, dpa, csum, psum = acc

    def enter(grad, start, size, core, b):
        _, _, u_ref, slope_ref = keep(b)
        hi, lo = split(grad)
        q = dot(part(w, "proj_back", b), jnp.concatenate([hi, lo, hi], axis=0))
        gh = lanes(slope_ref, start, size) * q
        ghi, glo = split(gh)
        gh_refs[b % 2][:CH, pl.ds(aligned(start), size)] = ghi
        gh_refs[b % 2][CH:, pl.ds(aligned(start), size)] = glo
        if core:
            dpa[b] += dot_nt(jnp.concatenate([hi, lo], axis=0), lanes(u_ref, start, size))
            csum[b] += lane_fold(gh)
            psum[b] += lane_fold(grad)

    for ref in acc:
        ref[...] = jnp.zeros(ref.shape, ref.dtype)

    def first(start, size, core):
        enter(lanes(g_ref, start, size), start, size, core, 3)

    sweep(first)
    for b in (3, 2, 1, 0):
        d = dils[b]
        m = DILATIONS.index(d)
        gh_ref = gh_refs[b % 2]

        def step(start, size, core, b=b, d=d, m=m, gh_ref=gh_ref):
            a_ref, gx_ref, _, _ = keep(b)
            left = tile_rows(lanes(mb, start, size, slice(32 * m, 32 * m + 16)), 4)
            right = tile_rows(lanes(mb, start, size, slice(32 * m + 16, 32 * m + 32)), 4)
            parts = []
            for rows in (slice(0, CH), slice(CH, 2 * CH)):
                parts.append(
                    jnp.concatenate(
                        [
                            from_right(gh_ref, rows, start, size, d, EXT) * right,
                            lanes(gh_ref, start, size, rows),
                            from_left(gh_ref, rows, start, size, d, EXT) * left,
                        ],
                        axis=0,
                    )
                )
            ghi, glo = parts
            both = dot(part(w, "conv_back", b), ghi)
            ga = both[:CH] + both[CH:] + dot(part(w, "conv_back", b)[:CH], glo)
            if core:
                act = lanes(a_ref, start, size)
                dk1[b] += dot_nt(ghi, act)
                dk2[b] += dot_nt(glo, act[:CH])
            out = lanes(g_ref, start, size) + lanes(gx_ref, start, size) * ga
            if b > 0:
                g_ref[:, pl.ds(aligned(start), size)] = out
                enter(out, start, size, core, b - 1)
            else:
                last(out, start, size, core)

        sweep(step)
    for b in range(4):
        dk = dk1[b, :, :CH] + dk1[b, :, CH:] + dk2[b]
        dp = dpa[b, :CH, :CH] + dpa[b, CH:, :CH] + dpa[b, :CH, CH:]
        finish(b, dk, dp, csum[b], psum[b])


def store_grads(grads, folded):
    kept = {}

    def finish(b, dk, dp, csum, psum):
        kept[b] = (dk, dp)
        if b % 2:
            at = b // 2
            grads[at * 192 : (at + 1) * 192, :] = jnp.concatenate([kept[b - 1][0], dk], axis=1)
            grads[GRAD_PROJ + at * CH : GRAD_PROJ + (at + 1) * CH, :] = jnp.concatenate(
                [kept[b - 1][1], dp], axis=1
            )
        folded.extend([csum, psum])

    return finish


def store_columns(grads, folded):
    lane = lax.broadcasted_iota(jnp.int32, (CH, 128), 1)
    totals = [jnp.sum(v, axis=1, keepdims=True) for v in folded]
    out = jnp.zeros((CH, 128), F32)
    for at, total in enumerate(totals):
        out = jnp.where(lane == at, total, out)
    grads[GRAD_BIAS:, :] = out


def to_halves(value, sel, e_ref, o_ref, start, size):
    hi, lo = split(value)
    both = jnp.concatenate([hi, lo], axis=0)
    half = start // 2
    for i in range(size // 256):
        out = dot(both[:, i * 256 : (i + 1) * 256], sel).astype(BF)
        e_ref[:, pl.ds(aligned(half + i * 128), 128)] = out[:, :128]
        o_ref[:, pl.ds(aligned(half + i * 128), 128)] = out[:, 128:]


def pair_stack(e_ref, o_ref, mhb, start, size):
    masks = [tile_rows(lanes(mhb, start, size, slice(16 * i, 16 * i + 16)), 4) for i in range(3)]
    parts = []
    for rows in (slice(0, CH), slice(CH, 2 * CH)):
        parts.append(
            jnp.concatenate(
                [
                    from_left(o_ref, rows, start, size, 1, HEXT) * masks[0],
                    lanes(e_ref, start, size, rows),
                    lanes(o_ref, start, size, rows) * masks[1],
                    from_right(e_ref, rows, start, size, 1, HEXT) * masks[2],
                ],
                axis=0,
            )
        )
    return parts


def pair_gather(w, parts):
    both = dot(w[...], parts[0])
    return both[:CH] + both[CH:] + dot(w[:CH], parts[1])


def spread(w, hl_ref, mh, z_refs, sel, bias_tile, x_ref):
    def first(start, size, core):
        both = lanes(hl_ref, start, size)
        z = dot(w, jnp.concatenate([both, both[:CH]], axis=0))
        masks = [tile_rows(lanes(mh, start, size, slice(8 * i, 8 * i + 8)), 8) for i in range(3)]
        at = pl.ds(aligned(start), size)
        z_refs[0][:, at] = z[0:64] * masks[0]
        z_refs[1][:, at] = z[64:128]
        z_refs[2][:, at] = z[128:192] * masks[1]
        z_refs[3][:, at] = z[192:256] * masks[2]

    half_sweep(first)

    def second(start, size, core):
        every = slice(None)
        even = lanes(z_refs[1], start, size) + from_left(z_refs[3], every, start, size, 1, HEXT)
        odd = lanes(z_refs[2], start, size) + from_right(z_refs[0], every, start, size, 1, HEXT)
        ehi, elo = split(even)
        ohi, olo = split(odd)
        for i in range(size // 128):
            cut = slice(i * 128, (i + 1) * 128)
            rows = jnp.concatenate(
                [
                    jnp.concatenate([ehi[:, cut], ohi[:, cut]], axis=1),
                    jnp.concatenate([elo[:, cut], olo[:, cut]], axis=1),
                ],
                axis=0,
            )
            out = dot_nt(rows, sel)
            out = out[:CH] + out[CH:]
            if bias_tile is not None:
                out = out + jnp.concatenate([bias_tile, bias_tile], axis=1)
            x_ref[:, pl.ds(aligned(2 * start + 256 * i), 256)] = out

    half_sweep(second)


def ring_fill(ref, core, hi, lo):
    if core is not None:
        ref[:, :CORE] = core
    ref[:, CORE : CORE + HALO] = hi
    ref[:, CORE + HALO :] = lo


def find_links(clip_ref, sel, mf, mb, mh, mhb):
    def links(start, size, core):
        at = pl.ds(aligned(start), size)
        here = lanes(clip_ref, start, size)

        def same(other):
            return jnp.where(other == here, 1.0, 0.0)

        for m, d in enumerate(DILATIONS):
            left = same(from_left(clip_ref, slice(None), start, size, d, EXT))
            right = same(from_right(clip_ref, slice(None), start, size, d, EXT))
            mf[16 * m : 16 * m + 8, at] = left
            mf[16 * m + 8 : 16 * m + 16, at] = right
            mb[32 * m : 32 * m + 16, at] = tile_rows(left, 2).astype(BF)
            mb[32 * m + 16 : 32 * m + 32, at] = tile_rows(right, 2).astype(BF)
            if m == 0:
                two = same(from_right(clip_ref, slice(None), start, size, 2, EXT))
                rows = jnp.concatenate([left, right, two, two], axis=0).astype(BF)
                half = start // 2
                for i in range(size // 256):
                    out = dot(rows[:, i * 256 : (i + 1) * 256], sel)[:, :128]
                    hat = pl.ds(aligned(half + 128 * i), 128)
                    mh[:, hat] = out[:24]
                    for n in range(3):
                        mhb[16 * n : 16 * n + 16, hat] = tile_rows(
                            out[8 * n : 8 * n + 8], 2
                        ).astype(BF)

    sweep(links)


def sum_refs():
    return [
        pltpu.VMEM((4, 3 * CH, 2 * CH), F32),
        pltpu.VMEM((4, 3 * CH, CH), F32),
        pltpu.VMEM((4, 2 * CH, 2 * CH), F32),
        pltpu.VMEM((4, CH, 128), F32),
        pltpu.VMEM((4, CH, 128), F32),
    ]


def state_refs():
    return [
        whole(),
        whole(rows=192),
        whole(rows=192),
        pltpu.VMEM((4, 128, EXT), BF),
        pltpu.VMEM((4, CH, EXT), F32),
        pltpu.VMEM((4, 128, EXT), BF),
        pltpu.VMEM((4, CH, EXT), F32),
        whole(),
        whole(BF, 128),
        whole(BF, 128),
        halves(),
        halves(),
        *sum_refs(),
    ]


def decode_kernel(
    cot, lo, hi, clip, chosen_in, cbt, weights, bias,
    rebuilt, quant_grad, grads, mf, mb, mh, mhb, chosen, chosen_hl, ids,
    up1, up2, usum, clip_ref, sems, x_ref, z0, z1, a_s, gx_s, u_s, gh_s, g_ref, g0, g1, e_ref, o_ref,
    *acc,
):
    ug = weights.at[PAIR_AT : PAIR_AT + 128]
    us = weights[PAIR_AT + 128 :, :192]
    cot_in = pltpu.make_async_copy(cot, g_ref.at[:, :CORE], sems.at[0])
    cot_in.start()
    sel = selector()
    ring_fill(
        clip_ref,
        jnp.broadcast_to(clip[...].astype(F32), (8, CORE)),
        jnp.broadcast_to(hi[128:129], (8, HALO)),
        jnp.broadcast_to(lo[128:129], (8, HALO)),
    )
    find_links(clip_ref, sel, mf, mb, mh, mhb)
    chosen[:, :HCORE] = chosen_in[...]
    ids[...] = jnp.broadcast_to((hi[129:130] + lo[129:130]).astype(jnp.int32), (8, HALO))
    pick(ids, cbt, chosen, HCORE, HEXT, HALO)
    chi, clo = split(chosen[...])
    chosen_hl[:CH] = chi
    chosen_hl[CH:] = clo
    zu = [z0.at[:CH], z0.at[CH : 2 * CH], z0.at[2 * CH :], z1.at[:CH]]
    spread(us, chosen_hl, mh, zu, sel, bias[17], x_ref)

    def keep(b):
        return a_s.at[b], gx_s.at[b], u_s.at[b], gh_s.at[b]

    def last(out, start, size, core):
        if core:
            x_ref[:, pl.ds(aligned(start), size)] = out

    order = DILATIONS[::-1]
    stack_forward(x_ref, (z0, z1), 4, order, weights, bias, mf, keep, last)
    rebuilt_out = pltpu.make_async_copy(x_ref.at[:, :CORE], rebuilt, sems.at[1])
    rebuilt_out.start()
    cot_in.wait()
    ring_fill(g_ref, None, hi[CH : 2 * CH], lo[CH : 2 * CH])
    for ref in (up1, up2, usum):
        ref[...] = jnp.zeros(ref.shape, F32)
    folded = []

    def last_back(out, start, size, core):
        to_halves(out, sel, e_ref, o_ref, start, size)
        if core:
            usum[...] += lane_fold(out)

    stack_backward(
        g_ref, (g0, g1), 4, order, weights, mb, keep, acc, store_grads(grads, folded), last_back
    )

    def up(start, size, core):
        parts = pair_stack(e_ref, o_ref, mhb, start, size)
        quant_grad[:, pl.ds(aligned(start), size)] = pair_gather(ug, parts)
        if core:
            both = lanes(chosen_hl, start, size)
            up1[...] += dot_nt(parts[0], both)
            up2[...] += dot_nt(parts[1], both[:CH])

    half_sweep(up)
    total = up1[:, :CH] + up1[:, CH:] + up2[...]
    grads[GRAD_PAIR:GRAD_BIAS, :] = jnp.concatenate([total[: 2 * CH], total[2 * CH :]], axis=1)
    store_columns(grads, folded + [usum[...]])
    rebuilt_out.wait()


def encode_kernel(
    frames, lo, hi, codes, quant_grad, dec_grads, chosen, mf, mb, mh, mhb, weights, bias,
    frames_grad, sums, sums_b,
    d_ref, l_ref, down1, down2, dsum, sems,
    x_ref, z0, z1, a_s, gx_s, u_s, gh_s, g_ref, g0, g1, e_ref, o_ref, *acc,
):
    dg = weights.at[PAIR_AT : PAIR_AT + 128]
    ds_ = weights[PAIR_AT + 128 :, :192]
    sel = selector()
    ring_fill(x_ref, frames[...], hi[:CH], lo[:CH])
    grads = sums_b.at[GRAD_ROWS - DEC_CUT :]
    sums[CODE_ROWS:, :] = dec_grads[:DEC_CUT, :]
    sums_b[: GRAD_ROWS - DEC_CUT, :] = dec_grads[DEC_CUT:, :]

    def keep(b):
        return a_s.at[b], gx_s.at[b], u_s.at[b], gh_s.at[b]

    def last(out, start, size, core):
        to_halves(out, sel, e_ref, o_ref, start, size)

    stack_forward(x_ref, (z0, z1), 0, DILATIONS, weights, bias, mf, keep, last)
    for ref in (down1, down2, dsum):
        ref[...] = jnp.zeros(ref.shape, F32)
    folded = []

    def down(start, size, core):
        at = pl.ds(aligned(start), size)
        parts = pair_stack(e_ref, o_ref, mhb, start, size)
        value = pair_gather(dg, parts) + jnp.concatenate([bias[16]] * (size // 128), axis=1)
        gap = value - lanes(chosen, start, size)
        grad = quant_grad[:, at] + (2.0 * COMMIT) * gap
        hi, lo = split(grad)
        l_ref[:CH, at] = hi
        l_ref[CH:, at] = lo
        if core:
            dhi, dlo = split(-2.0 * gap)
            d_ref[:CH, at] = dhi
            d_ref[CH:, at] = dlo
            dsum[...] += lane_fold(grad)
            down1[...] += dot_nt(jnp.concatenate([hi, lo], axis=0), parts[0])
            down2[...] += dot_nt(hi, parts[1])

    half_sweep(down)
    def codes_back(i, carry):
        hot = one_hot(codes[...], i * 512, 512)
        out = dot_nt(d_ref[...], hot)
        out = out[:CH] + out[CH:]
        at = pl.multiple_of(i * 256, 256)
        for n in range(4):
            sums[pl.ds(at + CH * n, CH), :] = out[:, 128 * n : 128 * (n + 1)]
        return carry

    lax.fori_loop(0, CODES // 512, codes_back, 0)
    zu = [z0.at[:CH], z0.at[CH : 2 * CH], z0.at[2 * CH :], z1.at[:CH]]
    spread(ds_, l_ref, mh, zu, sel, None, g_ref)

    leaving = []

    def last_back(out, start, size, core):
        if core:
            at = pl.ds(start, size)
            x_ref[:, at] = out
            leaving.append(
                pltpu.make_async_copy(x_ref.at[:, at], frames_grad.at[:, at], sems.at[len(leaving)])
            )
            leaving[-1].start()

    stack_backward(
        g_ref, (g0, g1), 0, DILATIONS, weights, mb, keep, acc, store_grads(grads, folded), last_back
    )
    total = down1[:CH] + down1[CH:] + down2[...]
    grads[GRAD_PAIR : GRAD_PAIR + CH, :] = total[:, : 2 * CH]
    grads[GRAD_PAIR + CH : GRAD_BIAS, :] = total[:, 2 * CH :]
    store_columns(grads, folded + [dsum[...]])
    for copy in leaving:
        copy.wait()


def unpack_kernel(
    sums, sums_b,
    cg, ec, ecb, ep, epb, dw, db, uw, ub, dc, dcb, dp, dpb,
):
    for i in range(CODES // 128):
        cg[:, i * 128 : (i + 1) * 128] = sums[i * CH : (i + 1) * CH, :]

    def enc(first, rows):
        at = GRAD_ROWS - DEC_CUT + first
        return sums_b[at : at + rows, :]

    def dec(first, rows):
        if first < DEC_CUT:
            return sums[CODE_ROWS + first : CODE_ROWS + first + rows, :]
        return sums_b[first - DEC_CUT : first - DEC_CUT + rows, :]

    for src, conv, cbias, proj, pbias, single in (
        (enc, ec, ecb, ep, epb, db),
        (dec, dc, dcb, dp, dpb, ub),
    ):
        rows = src(GRAD_BIAS, CH).T
        for b in range(4):
            at = slice((b % 2) * CH, (b % 2 + 1) * CH)
            p = b // 2
            conv[b] = src(p * 192, 192)[:, at].reshape(3, CH, CH)
            proj[b] = src(GRAD_PROJ + p * CH, CH)[:, at]
            cbias[b : b + 1, :] = rows[2 * b : 2 * b + 1]
            pbias[b : b + 1, :] = rows[2 * b + 1 : 2 * b + 2]
        single[...] = rows[8:9]
    for k in range(4):
        a, b = k // 2, k % 2
        dw[k] = enc(GRAD_PAIR + a * CH, CH)[:, b * CH : (b + 1) * CH]
        uw[k] = dec(GRAD_PAIR + b * CH, CH)[:, a * CH : (a + 1) * CH]


def shape(dims, kind=F32):
    return jax.ShapeDtypeStruct(dims, kind)


def call(kernel, outs, scratch=(), flops=0, limit=40, in_specs=None, out_specs=None):
    extra = {}
    if in_specs is not None:
        extra["in_specs"] = in_specs
    if out_specs is not None:
        extra["out_specs"] = out_specs
    return pl.pallas_call(
        kernel,
        out_shape=outs,
        scratch_shapes=list(scratch),
        compiler_params=pltpu.CompilerParams(vmem_limit_bytes=limit * MB),
        cost_estimate=pl.CostEstimate(flops=flops, bytes_accessed=2**20, transcendentals=0),
        **extra,
    )


def halves(kind=BF, rows=2 * CH):
    return pltpu.VMEM((rows, HEXT), kind)


def whole(kind=F32, rows=CH):
    return pltpu.VMEM((rows, EXT), kind)


FAR = pl.BlockSpec(memory_space=pltpu.HBM)


def far(*values):
    return [pltpu.with_memory_space_constraint(v, pltpu.HBM) for v in values]
LOCAL = pl.BlockSpec()


def local_pack(frames, cot, clip, codes):
    return call(
        pack_kernel,
        [shape((136, HALO)), shape((136, HALO))],
        [
            pltpu.VMEM((1, CORE), jnp.int32),
            pltpu.VMEM((1, HCORE), jnp.int32),
            pltpu.SemaphoreType.DMA((6,)),
        ],
        in_specs=[FAR] * 4,
    )(*far(frames, cot, clip, codes))


def local_prep(*args):
    return call(
        prep_kernel,
        [
            shape((WEIGHT_ROWS, 256), BF),
            shape((WEIGHT_ROWS, 256), BF),
            shape((18, CH, 128)),
            shape((128, CODES), BF),
            shape((CH, HCORE)),
        ],
        [pltpu.VMEM(a.shape, a.dtype) for a in args] + [pltpu.SemaphoreType.DMA((14,))],
        flops=10**7,
        limit=40,
        in_specs=[FAR] * 14,
    )(*far(*args))


def local_decode(cot, *args):
    return call(
        decode_kernel,
        [
            shape((CH, CORE)),
            shape((CH, HEXT)),
            shape((GRAD_ROWS, 128)),
            shape((64, EXT)),
            shape((128, EXT), BF),
            shape((24, HEXT)),
            shape((48, HEXT), BF),
            shape((CH, HEXT)),
        ],
        [
            halves(),
            pltpu.VMEM((8, HALO), jnp.int32),
            pltpu.VMEM((256, 128), F32),
            pltpu.VMEM((256, CH), F32),
            pltpu.VMEM((CH, 128), F32),
            whole(rows=8),
            pltpu.SemaphoreType.DMA((2,)),
            *state_refs(),
        ],
        flops=2 * 10**10,
        limit=40,
        in_specs=[FAR] + [LOCAL] * 7,
        out_specs=[FAR] + [LOCAL] * 7,
    )(*far(cot), *args)


def local_encode(*args):
    return call(
        encode_kernel,
        [shape((CH, CORE)), shape((SUM_ROWS, 128)), shape((SUM_ROWS, 128))],
        [
            pltpu.VMEM((2 * CH, HCORE), BF),
            halves(),
            pltpu.VMEM((128, 256), F32),
            pltpu.VMEM((CH, 256), F32),
            pltpu.VMEM((CH, 128), F32),
            pltpu.SemaphoreType.DMA((CORE // STEP,)),
            *state_refs(),
        ],
        flops=2 * 10**10,
        limit=40,
        in_specs=[LOCAL] * 13,
        out_specs=[FAR, LOCAL, LOCAL],
    )(*args)


def local_unpack(sums, sums_b):
    block = [shape((4, 3, CH, CH)), shape((4, CH)), shape((4, CH, CH)), shape((4, CH))]
    return call(
        unpack_kernel,
        [
            shape((CH, CODES)),
            *block,
            shape((4, CH, CH)),
            shape((1, CH)),
            shape((4, CH, CH)),
            shape((1, CH)),
            *block,
        ],
    )(sums, sums_b)


AXES = ("tm", "batch")
ORDERS = (((0, False), (1, False)), ((2, False), (0, True)))
SCATTER = 3


def rounds(chain):
    tm, batch = lax.axis_size("tm"), lax.axis_size("batch")
    rings = []
    stride = 2
    while stride < tm:
        size = min(4, tm // stride)
        rings.append(("tm", stride, size))
        stride *= size
    rings.append(("batch", 1, batch))
    devices = [(t, b) for t in range(tm) for b in range(batch)]

    def digit_of(ring, t, b):
        axis, stride, size = ring
        return (t if axis == "tm" else b) // stride % size

    def moved(ring, n, t, b):
        axis, stride, size = ring
        here = digit_of(ring, t, b)
        to = here ^ 1 if n == 0 else 3 - here
        t, b = (t + (to - here) * stride, b) if axis == "tm" else (t, b + (to - here) * stride)
        return t * batch + b

    def steps(first, swap):
        order = rings[first % len(rings):] + rings[: first % len(rings)]
        out = []
        for ring in order:
            sides = list(range(ring[2] // 2))
            for at, n in enumerate(sides[::-1] if swap else sides):
                out.append((ring, n, at))
        return out

    me = (lax.axis_index("tm"), lax.axis_index("batch"))

    def bit_of(step, swap):
        ring, n, at = step
        digit = digit_of(ring, *me)
        if ring[2] == 2:
            return digit
        if at == 0:
            return digit // 2 if swap else (digit ^ (digit // 2)) % 2
        return digit % 2 if swap else digit // 2

    orders = ORDERS[chain]
    plans = [steps(*o) for o in orders]
    out = [([(t * batch + b, (t ^ 1) * batch + b) for t, b in devices], me[0] % 2)]
    for pair in zip(*plans):
        pairs = [(t * batch + b, moved(*pair[t % 2][:2], t, b)) for t, b in devices]
        bits = [bit_of(p, o[1]) for p, o in zip(pair, orders)]
        out.append((pairs, jnp.where(me[0] % 2 == 0, bits[0], bits[1])))
    return out


def sum_chains(values):
    values = list(values)
    plans = [rounds(c) for c in range(len(values))]
    for n in range(len(plans[0])):
        for c, plan in enumerate(plans):
            pairs, bit = plan[n]
            value = values[c]
            if n < SCATTER:
                half = value.shape[0] // 2
                mine = lax.dynamic_slice_in_dim(value, bit * half, half, 0)
                other = lax.dynamic_slice_in_dim(value, (1 - bit) * half, half, 0)
                values[c] = mine + lax.ppermute(other, AXES, pairs)
            else:
                values[c] = value + lax.ppermute(value, AXES, pairs)
    for n in reversed(range(SCATTER)):
        for c, plan in enumerate(plans):
            pairs, bit = plan[n]
            value = values[c]
            other = lax.ppermute(value, AXES, pairs)
            half = value.shape[0]
            out = jnp.zeros((2 * half, value.shape[1]), value.dtype)
            out = lax.dynamic_update_slice_in_dim(out, value, bit * half, 0)
            values[c] = lax.dynamic_update_slice_in_dim(out, other, (1 - bit) * half, 0)
    return values


def on_device(
    frames, clip_start, code_ids, cotangent,
    enc_conv, enc_conv_bias, enc_proj, enc_proj_bias, downscale_weight, downscale_bias,
    codebook, up_weight, up_bias, dec_conv, dec_conv_bias, dec_proj, dec_proj_bias,
):
    frames = frames.reshape(CH, CORE)
    cotangent = cotangent.reshape(CH, CORE)
    front, tail = local_pack(frames, cotangent, clip_start, code_ids)
    count = lax.axis_size("tm")
    ring = [(i, (i + 1) % count) for i in range(count)]
    lo = lax.ppermute(tail, "tm", ring)
    hi = lax.ppermute(front, "tm", [(j, i) for i, j in ring])
    enc_w, dec_w, bias, cbt, chosen = local_prep(
        enc_conv, enc_conv_bias, enc_proj, enc_proj_bias,
        downscale_weight, downscale_bias.reshape(1, CH),
        codebook.T, up_weight, up_bias.reshape(1, CH),
        dec_conv, dec_conv_bias, dec_proj, dec_proj_bias, code_ids,
    )
    rebuilt, quant_grad, dec_grads, mf, mb, mh, mhb, chosen = local_decode(
        cotangent, lo, hi, clip_start, chosen, cbt, dec_w, bias
    )
    frames_grad, *sums = local_encode(
        frames, lo, hi, code_ids, quant_grad, dec_grads, chosen, mf, mb, mh, mhb,
        enc_w, bias,
    )
    out = list(local_unpack(*sum_chains(sums)))
    cg = out.pop(0).T
    out[5] = out[5].reshape(CH)
    out[7] = out[7].reshape(CH)
    out.insert(6, cg)
    return (rebuilt[None], frames_grad[None], *out)


def solution(mesh):
    split_spec = P("batch", None, "tm")
    row_spec = P("batch", "tm")
    return jax.shard_map(
        on_device,
        mesh=mesh,
        in_specs=(split_spec, row_spec, row_spec, split_spec) + (P(),) * 13,
        out_specs=(split_spec, split_spec) + (P(),) * 13,
        check_vma=False,
    )
```

```python
import functools

import jax
import jax.numpy as jnp
from jax import lax
from jax.experimental import pallas as pl
from jax.experimental.pallas import tpu as pltpu
from jax.sharding import PartitionSpec as P

COMMIT = 0.02
DILATIONS = (1, 3, 9, 27)
BF = jnp.bfloat16
F32 = jnp.float32
CH = 64
CODES = 2048
CORE = 4096
HALO = 128
EXT = CORE + 2 * HALO
HCORE = CORE // 2
HEXT = EXT // 2
STEP = 1024
G0 = 0.7978845608028654
G1 = G0 * 0.044715
MB = 2**20
GRAD_PROJ = 384
GRAD_PAIR = 512
GRAD_BIAS = 640
GRAD_ROWS = 704
CODE_ROWS = CODES // 2
DEC_CUT = 192
SUM_ROWS = CODE_ROWS + DEC_CUT


BLOCK_ROWS = 448
PAIR_AT = 4 * BLOCK_ROWS
WEIGHT_ROWS = PAIR_AT + 384


PARTS = {"conv": (0, 192), "conv_back": (192, 128), "proj": (320, 64), "proj_back": (384, 64)}


def part_rows(name, b):
    first, rows = PARTS[name]
    return slice(BLOCK_ROWS * b + first, BLOCK_ROWS * b + first + rows)


def part(w, name, b):
    return w[part_rows(name, b), :192]


def dot(a, b):
    return jnp.dot(a, b, preferred_element_type=F32)


def dot_nt(a, b):
    return lax.dot_general(a, b, (((1,), (1,)), ((), ())), preferred_element_type=F32)


def split(v):
    hi = v.astype(BF)
    return hi, (v - hi.astype(F32)).astype(BF)


def gelu_both(v):
    s = v * v
    t = jnp.tanh(v * (G0 + G1 * s))
    cdf = 0.5 + 0.5 * t
    slope = cdf + (0.5 * v) * (1.0 - t * t) * (G0 + (3.0 * G1) * s)
    return v * cdf, slope


def tile_rows(rows, times):
    return jnp.concatenate([rows] * times, axis=0)


def aligned(start):
    return start if isinstance(start, int) else pl.multiple_of(start, 128)


def lanes(ref, start, size, rows=slice(None)):
    return ref[rows, pl.ds(aligned(start), size)]


def wrap(start, length):
    return start % length if isinstance(start, int) else lax.rem(start + length, length)


def from_left(ref, rows, start, size, offset, length):
    win = jnp.concatenate(
        [lanes(ref, wrap(start - 128, length), 128, rows), lanes(ref, start, size, rows)], axis=1
    )
    return pltpu.roll(win, offset, 1)[:, 128:]


def from_right(ref, rows, start, size, offset, length):
    win = jnp.concatenate(
        [lanes(ref, start, size, rows), lanes(ref, wrap(start + size, length), 128, rows)], axis=1
    )
    return pltpu.roll(win, size + 128 - offset, 1)[:, :size]


def sweep(fn, step=STEP):
    for i in range(CORE // step):
        fn(i * step, step, True)
    fn(CORE, 2 * HALO, False)


def half_sweep(fn, step=STEP // 2):
    for i in range(HCORE // step):
        fn(i * step, step, True)
    fn(HCORE, HALO, False)


def apart(fn):
    pl.when(lax.axis_index("tm") >= 0)(fn)


def lane_fold(v):
    out = v[:, :128]
    for i in range(1, v.shape[1] // 128):
        out = out + v[:, i * 128 : (i + 1) * 128]
    return out


def selector():
    row = lax.broadcasted_iota(jnp.int32, (256, 256), 0)
    col = lax.broadcasted_iota(jnp.int32, (256, 256), 1)
    source = jnp.where(col < 128, 2 * col, 2 * (col - 128) + 1)
    return jnp.where(row == source, 1.0, 0.0).astype(BF)


def pack_kernel(frames, cot, clip, codes, front, tail, clip_v, codes_v, sems):
    first, final = slice(0, HALO), slice(CORE - HALO, CORE)
    copies = [
        pltpu.make_async_copy(src, dst, sems.at[n])
        for n, (src, dst) in enumerate(
            (
                (frames.at[:, first], front.at[:CH]),
                (frames.at[:, final], tail.at[:CH]),
                (cot.at[:, first], front.at[CH : 2 * CH]),
                (cot.at[:, final], tail.at[CH : 2 * CH]),
                (clip, clip_v),
                (codes, codes_v),
            )
        )
    ]
    for copy in copies:
        copy.start()
    for copy in copies:
        copy.wait()
    me = lax.axis_index("tm")
    count = lax.axis_size("tm")
    lane = lax.broadcasted_iota(jnp.int32, (1, HALO), 1)
    blank = jnp.zeros((6, HALO), F32)
    for out, cut, at_end, half, keep in (
        (front, first, me == 0, slice(0, HALO), lane < 64),
        (tail, final, me == count - 1, slice(HCORE - HALO, HCORE), lane >= 64),
    ):
        clip_row = jnp.where(at_end, -1.0, clip_v[:, cut].astype(F32))
        code_row = jnp.where(keep, codes_v[:, half].astype(F32), 0.0)
        out[2 * CH :, :] = jnp.concatenate([clip_row, code_row, blank], axis=0)


def prep_kernel(*refs):
    sources, outs, scratch = refs[:14], refs[14:19], refs[19:]
    sems = scratch[-1]
    copies = [
        pltpu.make_async_copy(src, dst, sems.at[n])
        for n, (src, dst) in enumerate(zip(sources, scratch[:14]))
    ]
    first = (6, 13)
    for n in (*first, *range(6), *range(7, 13)):
        copies[n].start()
    for n in first:
        copies[n].wait()
    ec, ecb, ep, epb, dw, db, cb, uw, ub, dc, dcb, dp, dpb, codes = scratch[:14]
    enc_w, dec_w, bias, cbt, chosen = outs

    def forms(w):
        hi, lo = split(w)
        return jnp.concatenate([hi, hi, lo], axis=1)

    def stacked(w):
        hi, lo = split(w)
        return jnp.concatenate([hi, lo], axis=0)

    def column(row):
        return jnp.broadcast_to(row, (128, CH)).T

    cbt[...] = stacked(cb[...])
    pick(codes, cbt, chosen, 0, HCORE, 1024)
    for n in (*range(6), *range(7, 13)):
        copies[n].wait()
    for n, (conv, cbias, proj, pbias) in enumerate(((ec, ecb, ep, epb), (dc, dcb, dp, dpb))):
        weights = (enc_w, dec_w)[n]
        for b in range(4):
            at = 4 * n + b
            weights[part_rows("conv", b), :192] = forms(conv[b].reshape(3 * CH, CH))
            weights[part_rows("conv_back", b), :192] = stacked(jnp.concatenate([conv[b, k].T for k in range(3)], axis=1))
            weights[part_rows("proj", b), :192] = forms(proj[b])
            weights[part_rows("proj_back", b), :192] = forms(proj[b].T)
            bias[2 * at] = column(cbias[b : b + 1, :])
            bias[2 * at + 1] = column(pbias[b : b + 1, :])
    bias[16] = column(db[...])
    bias[17] = column(ub[...])
    enc_w[PAIR_AT : PAIR_AT + 128, :] = stacked(jnp.concatenate([dw[k] for k in range(4)], axis=1))
    enc_w[PAIR_AT + 128 :, :192] = forms(jnp.concatenate([dw[k].T for k in range(4)], axis=0))
    dec_w[PAIR_AT : PAIR_AT + 128, :] = stacked(jnp.concatenate([uw[k].T for k in range(4)], axis=1))
    dec_w[PAIR_AT + 128 :, :192] = forms(jnp.concatenate([uw[k] for k in range(4)], axis=0))


def one_hot(ids_row, first, count):
    row = lax.broadcasted_iota(jnp.int32, (count, ids_row.shape[1]), 0) + first
    return jnp.where(row == ids_row, 1.0, 0.0).astype(BF)


def pick(ids, cbt, chosen, begin, end, step):
    for start in range(begin, end, step):
        at = slice(start - begin, start - begin + step)
        to = slice(start, start + step)
        both = dot(cbt[...], one_hot(ids[0:1, at], 0, CODES))
        chosen[:, to] = both[:CH] + both[CH:]


def stack_forward(x_ref, z_refs, blocks, dils, w, bias, mf, keep, last):
    def enter(value, start, size, b):
        act, slope = gelu_both(value)
        hi, lo = split(act)
        a_ref, gx_ref, _, _ = keep(b)
        a_ref[:CH, pl.ds(aligned(start), size)] = hi
        a_ref[CH:, pl.ds(aligned(start), size)] = lo
        gx_ref[:, pl.ds(aligned(start), size)] = slope
        z_refs[b % 2][:, pl.ds(aligned(start), size)] = dot(
            part(w, "conv", b), jnp.concatenate([hi, lo, hi], axis=0)
        )

    def first(start, size, core):
        enter(lanes(x_ref, start, size), start, size, 0)

    sweep(first)
    for b in range(4):
        d = dils[b]
        m = DILATIONS.index(d)
        z_ref = z_refs[b % 2]

        def step(start, size, core, b=b, d=d, m=m, z_ref=z_ref):
            _, _, u_ref, gh_ref = keep(b)
            times = size // 128
            left = tile_rows(lanes(mf, start, size, slice(16 * m, 16 * m + 8)), 8)
            right = tile_rows(lanes(mf, start, size, slice(16 * m + 8, 16 * m + 16)), 8)
            cb = jnp.concatenate([bias[2 * (blocks + b)]] * times, axis=1)
            hidden = lanes(z_ref, start, size, slice(CH, 2 * CH)) + cb
            hidden = hidden + left * from_left(z_ref, slice(0, CH), start, size, d, EXT)
            hidden = hidden + right * from_right(z_ref, slice(2 * CH, 3 * CH), start, size, d, EXT)
            act, slope = gelu_both(hidden)
            hi, lo = split(act)
            u_ref[:CH, pl.ds(aligned(start), size)] = hi
            u_ref[CH:, pl.ds(aligned(start), size)] = lo
            gh_ref[:, pl.ds(aligned(start), size)] = slope
            pbias = jnp.concatenate([bias[2 * (blocks + b) + 1]] * times, axis=1)
            out = (
                lanes(x_ref, start, size)
                + dot(part(w, "proj", b), jnp.concatenate([hi, lo, hi], axis=0))
                + pbias
            )
            if b < 3:
                x_ref[:, pl.ds(aligned(start), size)] = out
                enter(out, start, size, b + 1)
            else:
                last(out, start, size, core)

        sweep(step)


def stack_backward(g_ref, gh_refs, blocks, dils, w, mb, keep, acc, finish, last):
    dk1, dk2, dpa, csum, psum = acc

    def enter(grad, start, size, core, b):
        _, _, u_ref, slope_ref = keep(b)
        hi, lo = split(grad)
        q = dot(part(w, "proj_back", b), jnp.concatenate([hi, lo, hi], axis=0))
        gh = lanes(slope_ref, start, size) * q
        ghi, glo = split(gh)
        gh_refs[b % 2][:CH, pl.ds(aligned(start), size)] = ghi
        gh_refs[b % 2][CH:, pl.ds(aligned(start), size)] = glo
        if core:
            dpa[b] += dot_nt(jnp.concatenate([hi, lo], axis=0), lanes(u_ref, start, size))
            csum[b] += lane_fold(gh)
            psum[b] += lane_fold(grad)

    for ref in acc:
        ref[...] = jnp.zeros(ref.shape, ref.dtype)

    def first(start, size, core):
        enter(lanes(g_ref, start, size), start, size, core, 3)

    sweep(first)
    for b in (3, 2, 1, 0):
        d = dils[b]
        m = DILATIONS.index(d)
        gh_ref = gh_refs[b % 2]

        def step(start, size, core, b=b, d=d, m=m, gh_ref=gh_ref):
            a_ref, gx_ref, _, _ = keep(b)
            left = tile_rows(lanes(mb, start, size, slice(32 * m, 32 * m + 16)), 4)
            right = tile_rows(lanes(mb, start, size, slice(32 * m + 16, 32 * m + 32)), 4)
            parts = []
            for rows in (slice(0, CH), slice(CH, 2 * CH)):
                parts.append(
                    jnp.concatenate(
                        [
                            from_right(gh_ref, rows, start, size, d, EXT) * right,
                            lanes(gh_ref, start, size, rows),
                            from_left(gh_ref, rows, start, size, d, EXT) * left,
                        ],
                        axis=0,
                    )
                )
            ghi, glo = parts
            both = dot(part(w, "conv_back", b), ghi)
            ga = both[:CH] + both[CH:] + dot(part(w, "conv_back", b)[:CH], glo)
            if core:
                act = lanes(a_ref, start, size)
                dk1[b] += dot_nt(ghi, act)
                dk2[b] += dot_nt(glo, act[:CH])
            out = lanes(g_ref, start, size) + lanes(gx_ref, start, size) * ga
            if b > 0:
                g_ref[:, pl.ds(aligned(start), size)] = out
                enter(out, start, size, core, b - 1)
            else:
                last(out, start, size, core)

        sweep(step)
    for b in range(4):
        dk = dk1[b, :, :CH] + dk1[b, :, CH:] + dk2[b]
        dp = dpa[b, :CH, :CH] + dpa[b, CH:, :CH] + dpa[b, :CH, CH:]
        finish(b, dk, dp, csum[b], psum[b])


def store_grads(grads, folded):
    kept = {}

    def finish(b, dk, dp, csum, psum):
        kept[b] = (dk, dp)
        if b % 2:
            at = b // 2
            grads[at * 192 : (at + 1) * 192, :] = jnp.concatenate([kept[b - 1][0], dk], axis=1)
            grads[GRAD_PROJ + at * CH : GRAD_PROJ + (at + 1) * CH, :] = jnp.concatenate(
                [kept[b - 1][1], dp], axis=1
            )
        folded.extend([csum, psum])

    return finish


def store_columns(grads, folded):
    lane = lax.broadcasted_iota(jnp.int32, (CH, 128), 1)
    totals = [jnp.sum(v, axis=1, keepdims=True) for v in folded]
    out = jnp.zeros((CH, 128), F32)
    for at, total in enumerate(totals):
        out = jnp.where(lane == at, total, out)
    grads[GRAD_BIAS:, :] = out


def to_halves(value, sel, e_ref, o_ref, start, size):
    hi, lo = split(value)
    both = jnp.concatenate([hi, lo], axis=0)
    half = start // 2
    for i in range(size // 256):
        out = dot(both[:, i * 256 : (i + 1) * 256], sel).astype(BF)
        e_ref[:, pl.ds(aligned(half + i * 128), 128)] = out[:, :128]
        o_ref[:, pl.ds(aligned(half + i * 128), 128)] = out[:, 128:]


def pair_stack(e_ref, o_ref, mhb, start, size):
    masks = [tile_rows(lanes(mhb, start, size, slice(16 * i, 16 * i + 16)), 4) for i in range(3)]
    parts = []
    for rows in (slice(0, CH), slice(CH, 2 * CH)):
        parts.append(
            jnp.concatenate(
                [
                    from_left(o_ref, rows, start, size, 1, HEXT) * masks[0],
                    lanes(e_ref, start, size, rows),
                    lanes(o_ref, start, size, rows) * masks[1],
                    from_right(e_ref, rows, start, size, 1, HEXT) * masks[2],
                ],
                axis=0,
            )
        )
    return parts


def pair_gather(w, parts):
    both = dot(w[...], parts[0])
    return both[:CH] + both[CH:] + dot(w[:CH], parts[1])


def spread(w, hl_ref, mh, z_refs, sel, bias_tile, x_ref):
    def first(start, size, core):
        both = lanes(hl_ref, start, size)
        z = dot(w, jnp.concatenate([both, both[:CH]], axis=0))
        masks = [tile_rows(lanes(mh, start, size, slice(8 * i, 8 * i + 8)), 8) for i in range(3)]
        at = pl.ds(aligned(start), size)
        z_refs[0][:, at] = z[0:64] * masks[0]
        z_refs[1][:, at] = z[64:128]
        z_refs[2][:, at] = z[128:192] * masks[1]
        z_refs[3][:, at] = z[192:256] * masks[2]

    half_sweep(first)

    def second(start, size, core):
        every = slice(None)
        even = lanes(z_refs[1], start, size) + from_left(z_refs[3], every, start, size, 1, HEXT)
        odd = lanes(z_refs[2], start, size) + from_right(z_refs[0], every, start, size, 1, HEXT)
        ehi, elo = split(even)
        ohi, olo = split(odd)
        for i in range(size // 128):
            cut = slice(i * 128, (i + 1) * 128)
            rows = jnp.concatenate(
                [
                    jnp.concatenate([ehi[:, cut], ohi[:, cut]], axis=1),
                    jnp.concatenate([elo[:, cut], olo[:, cut]], axis=1),
                ],
                axis=0,
            )
            out = dot_nt(rows, sel)
            out = out[:CH] + out[CH:]
            if bias_tile is not None:
                out = out + jnp.concatenate([bias_tile, bias_tile], axis=1)
            x_ref[:, pl.ds(aligned(2 * start + 256 * i), 256)] = out

    half_sweep(second)


def ring_fill(ref, core, hi, lo):
    if core is not None:
        ref[:, :CORE] = core
    ref[:, CORE : CORE + HALO] = hi
    ref[:, CORE + HALO :] = lo


def find_links(clip_ref, sel, mf, mb, mh, mhb):
    def links(start, size, core):
        at = pl.ds(aligned(start), size)
        here = lanes(clip_ref, start, size)

        def same(other):
            return jnp.where(other == here, 1.0, 0.0)

        for m, d in enumerate(DILATIONS):
            left = same(from_left(clip_ref, slice(None), start, size, d, EXT))
            right = same(from_right(clip_ref, slice(None), start, size, d, EXT))
            mf[16 * m : 16 * m + 8, at] = left
            mf[16 * m + 8 : 16 * m + 16, at] = right
            mb[32 * m : 32 * m + 16, at] = tile_rows(left, 2).astype(BF)
            mb[32 * m + 16 : 32 * m + 32, at] = tile_rows(right, 2).astype(BF)
            if m == 0:
                two = same(from_right(clip_ref, slice(None), start, size, 2, EXT))
                rows = jnp.concatenate([left, right, two, two], axis=0).astype(BF)
                half = start // 2
                for i in range(size // 256):
                    out = dot(rows[:, i * 256 : (i + 1) * 256], sel)[:, :128]
                    hat = pl.ds(aligned(half + 128 * i), 128)
                    mh[:, hat] = out[:24]
                    for n in range(3):
                        mhb[16 * n : 16 * n + 16, hat] = tile_rows(
                            out[8 * n : 8 * n + 8], 2
                        ).astype(BF)

    sweep(links)


def sum_refs():
    return [
        pltpu.VMEM((4, 3 * CH, 2 * CH), F32),
        pltpu.VMEM((4, 3 * CH, CH), F32),
        pltpu.VMEM((4, 2 * CH, 2 * CH), F32),
        pltpu.VMEM((4, CH, 128), F32),
        pltpu.VMEM((4, CH, 128), F32),
    ]


def state_refs():
    return [
        whole(),
        whole(rows=192),
        whole(rows=192),
        pltpu.VMEM((4, 128, EXT), BF),
        pltpu.VMEM((4, CH, EXT), F32),
        pltpu.VMEM((4, 128, EXT), BF),
        pltpu.VMEM((4, CH, EXT), F32),
        whole(),
        whole(BF, 128),
        whole(BF, 128),
        halves(),
        halves(),
        *sum_refs(),
    ]


def decode_kernel(
    cot, lo, hi, clip, chosen_in, cbt, weights, bias,
    rebuilt, quant_grad, grads, mf, mb, mh, mhb, chosen, chosen_hl, ids,
    up1, up2, usum, clip_ref, sems, x_ref, z0, z1, a_s, gx_s, u_s, gh_s, g_ref, g0, g1, e_ref, o_ref,
    *acc,
):
    ug = weights.at[PAIR_AT : PAIR_AT + 128]
    us = weights.at[PAIR_AT + 128 :]
    cot_in = pltpu.make_async_copy(cot, g_ref.at[:, :CORE], sems.at[0])
    cot_in.start()
    sel = selector()
    ring_fill(
        clip_ref,
        jnp.broadcast_to(clip[...].astype(F32), (8, CORE)),
        jnp.broadcast_to(hi[128:129], (8, HALO)),
        jnp.broadcast_to(lo[128:129], (8, HALO)),
    )
    apart(lambda: find_links(clip_ref, selector(), mf, mb, mh, mhb))
    chosen[:, :HCORE] = chosen_in[...]
    ids[...] = jnp.broadcast_to((hi[129:130] + lo[129:130]).astype(jnp.int32), (8, HALO))
    pick(ids, cbt, chosen, HCORE, HEXT, HALO)
    chi, clo = split(chosen[...])
    chosen_hl[:CH] = chi
    chosen_hl[CH:] = clo
    zu = [z0.at[:CH], z0.at[CH : 2 * CH], z0.at[2 * CH :], z1.at[:CH]]
    apart(lambda: spread(us[:, :192], chosen_hl, mh, zu, selector(), bias[17], x_ref))

    def keep(b):
        return a_s.at[b], gx_s.at[b], u_s.at[b], gh_s.at[b]

    def last(out, start, size, core):
        if core:
            x_ref[:, pl.ds(aligned(start), size)] = out

    order = DILATIONS[::-1]
    apart(lambda: stack_forward(x_ref, (z0, z1), 4, order, weights, bias, mf, keep, last))
    rebuilt_out = pltpu.make_async_copy(x_ref.at[:, :CORE], rebuilt, sems.at[1])
    rebuilt_out.start()
    cot_in.wait()
    ring_fill(g_ref, None, hi[CH : 2 * CH], lo[CH : 2 * CH])
    for ref in (up1, up2, usum):
        ref[...] = jnp.zeros(ref.shape, F32)
    @apart
    def _():
        folded = []
        take = selector()

        def last_back(out, start, size, core):
            to_halves(out, take, e_ref, o_ref, start, size)
            if core:
                usum[...] += lane_fold(out)

        stack_backward(
            g_ref, (g0, g1), 4, order, weights, mb, keep, acc, store_grads(grads, folded), last_back
        )
        store_columns(grads, folded + [usum[...]])

    def up(start, size, core):
        parts = pair_stack(e_ref, o_ref, mhb, start, size)
        quant_grad[:, pl.ds(aligned(start), size)] = pair_gather(ug, parts)
        if core:
            both = lanes(chosen_hl, start, size)
            up1[...] += dot_nt(parts[0], both)
            up2[...] += dot_nt(parts[1], both[:CH])

    half_sweep(up)
    total = up1[:, :CH] + up1[:, CH:] + up2[...]
    grads[GRAD_PAIR:GRAD_BIAS, :] = jnp.concatenate([total[: 2 * CH], total[2 * CH :]], axis=1)
    rebuilt_out.wait()


def encode_kernel(
    frames, lo, hi, codes, quant_grad, dec_grads, chosen, mf, mb, mh, mhb, weights, bias,
    frames_grad, all_sums,
    d_ref, l_ref, down1, down2, dsum, sems,
    x_ref, z0, z1, a_s, gx_s, u_s, gh_s, g_ref, g0, g1, e_ref, o_ref, *acc,
):
    dg = weights.at[PAIR_AT : PAIR_AT + 128]
    ds_ = weights.at[PAIR_AT + 128 :]
    ring_fill(x_ref, frames[...], hi[:CH], lo[:CH])
    sums, sums_b = all_sums.at[:SUM_ROWS], all_sums.at[SUM_ROWS:]
    grads = sums_b.at[GRAD_ROWS - DEC_CUT :]
    sums[CODE_ROWS:, :] = dec_grads[:DEC_CUT, :]
    sums_b[: GRAD_ROWS - DEC_CUT, :] = dec_grads[DEC_CUT:, :]

    def keep(b):
        return a_s.at[b], gx_s.at[b], u_s.at[b], gh_s.at[b]

    @apart
    def _():
        take = selector()

        def last(out, start, size, core):
            to_halves(out, take, e_ref, o_ref, start, size)

        stack_forward(x_ref, (z0, z1), 0, DILATIONS, weights, bias, mf, keep, last)

    for ref in (down1, down2, dsum):
        ref[...] = jnp.zeros(ref.shape, F32)
    folded = []

    def down(start, size, core):
        at = pl.ds(aligned(start), size)
        parts = pair_stack(e_ref, o_ref, mhb, start, size)
        value = pair_gather(dg, parts) + jnp.concatenate([bias[16]] * (size // 128), axis=1)
        gap = value - lanes(chosen, start, size)
        grad = quant_grad[:, at] + (2.0 * COMMIT) * gap
        hi, lo = split(grad)
        l_ref[:CH, at] = hi
        l_ref[CH:, at] = lo
        if core:
            dhi, dlo = split(-2.0 * gap)
            d_ref[:CH, at] = dhi
            d_ref[CH:, at] = dlo
            dsum[...] += lane_fold(grad)
            down1[...] += dot_nt(jnp.concatenate([hi, lo], axis=0), parts[0])
            down2[...] += dot_nt(hi, parts[1])

    apart(lambda: half_sweep(down))

    def codes_back(i, carry):
        hot = one_hot(codes[...], i * 512, 512)
        out = dot_nt(d_ref[...], hot)
        out = out[:CH] + out[CH:]
        at = pl.multiple_of(i * 256, 256)
        for n in range(4):
            sums[pl.ds(at + CH * n, CH), :] = out[:, 128 * n : 128 * (n + 1)]
        return carry

    lax.fori_loop(0, CODES // 512, codes_back, 0)
    zu = [z0.at[:CH], z0.at[CH : 2 * CH], z0.at[2 * CH :], z1.at[:CH]]
    apart(lambda: spread(ds_[:, :192], l_ref, mh, zu, selector(), None, g_ref))

    @apart
    def _():
        folded = []
        leaving = []

        def last_back(out, start, size, core):
            if core:
                at = pl.ds(start, size)
                x_ref[:, at] = out
                leaving.append(
                    pltpu.make_async_copy(
                        x_ref.at[:, at], frames_grad.at[:, at], sems.at[len(leaving)]
                    )
                )
                leaving[-1].start()

        stack_backward(
            g_ref, (g0, g1), 0, DILATIONS, weights, mb, keep, acc, store_grads(grads, folded), last_back
        )
        total = down1[:CH] + down1[CH:] + down2[...]
        grads[GRAD_PAIR : GRAD_PAIR + CH, :] = total[:, : 2 * CH]
        grads[GRAD_PAIR + CH : GRAD_BIAS, :] = total[:, 2 * CH :]
        store_columns(grads, folded + [dsum[...]])
        for copy in leaving:
            copy.wait()


def unpack_kernel(
    all_sums,
    cg, ec, ecb, ep, epb, dw, db, uw, ub, dc, dcb, dp, dpb,
):
    sums, sums_b = all_sums.at[:SUM_ROWS], all_sums.at[SUM_ROWS:]
    for i in range(CODES // 128):
        cg[:, i * 128 : (i + 1) * 128] = sums[i * CH : (i + 1) * CH, :]

    def enc(first, rows):
        at = GRAD_ROWS - DEC_CUT + first
        return sums_b[at : at + rows, :]

    def dec(first, rows):
        if first < DEC_CUT:
            return sums[CODE_ROWS + first : CODE_ROWS + first + rows, :]
        return sums_b[first - DEC_CUT : first - DEC_CUT + rows, :]

    for src, conv, cbias, proj, pbias, single in (
        (enc, ec, ecb, ep, epb, db),
        (dec, dc, dcb, dp, dpb, ub),
    ):
        rows = src(GRAD_BIAS, CH).T
        for b in range(4):
            at = slice((b % 2) * CH, (b % 2 + 1) * CH)
            p = b // 2
            conv[b] = src(p * 192, 192)[:, at].reshape(3, CH, CH)
            proj[b] = src(GRAD_PROJ + p * CH, CH)[:, at]
            cbias[b : b + 1, :] = rows[2 * b : 2 * b + 1]
            pbias[b : b + 1, :] = rows[2 * b + 1 : 2 * b + 2]
        single[...] = rows[8:9]
    for k in range(4):
        a, b = k // 2, k % 2
        dw[k] = enc(GRAD_PAIR + a * CH, CH)[:, b * CH : (b + 1) * CH]
        uw[k] = dec(GRAD_PAIR + b * CH, CH)[:, a * CH : (a + 1) * CH]


def shape(dims, kind=F32):
    return jax.ShapeDtypeStruct(dims, kind)


def call(kernel, outs, scratch=(), flops=0, limit=40, in_specs=None, out_specs=None):
    extra = {}
    if in_specs is not None:
        extra["in_specs"] = in_specs
    if out_specs is not None:
        extra["out_specs"] = out_specs
    return pl.pallas_call(
        kernel,
        out_shape=outs,
        scratch_shapes=list(scratch),
        compiler_params=pltpu.CompilerParams(vmem_limit_bytes=limit * MB),
        cost_estimate=pl.CostEstimate(flops=flops, bytes_accessed=2**20, transcendentals=0),
        **extra,
    )


def halves(kind=BF, rows=2 * CH):
    return pltpu.VMEM((rows, HEXT), kind)


def whole(kind=F32, rows=CH):
    return pltpu.VMEM((rows, EXT), kind)


FAR = pl.BlockSpec(memory_space=pltpu.HBM)


def far(*values):
    return [pltpu.with_memory_space_constraint(v, pltpu.HBM) for v in values]
LOCAL = pl.BlockSpec()


def local_pack(frames, cot, clip, codes):
    return call(
        pack_kernel,
        [shape((136, HALO)), shape((136, HALO))],
        [
            pltpu.VMEM((1, CORE), jnp.int32),
            pltpu.VMEM((1, HCORE), jnp.int32),
            pltpu.SemaphoreType.DMA((6,)),
        ],
        in_specs=[FAR] * 4,
    )(*far(frames, cot, clip, codes))


def local_prep(*args):
    return call(
        prep_kernel,
        [
            shape((WEIGHT_ROWS, 256), BF),
            shape((WEIGHT_ROWS, 256), BF),
            shape((18, CH, 128)),
            shape((128, CODES), BF),
            shape((CH, HCORE)),
        ],
        [pltpu.VMEM(a.shape, a.dtype) for a in args] + [pltpu.SemaphoreType.DMA((14,))],
        flops=10**7,
        limit=40,
        in_specs=[FAR] * 14,
    )(*far(*args))


def local_decode(cot, *args):
    return call(
        decode_kernel,
        [
            shape((CH, CORE)),
            shape((CH, HEXT)),
            shape((GRAD_ROWS, 128)),
            shape((64, EXT)),
            shape((128, EXT), BF),
            shape((24, HEXT)),
            shape((48, HEXT), BF),
            shape((CH, HEXT)),
        ],
        [
            halves(),
            pltpu.VMEM((8, HALO), jnp.int32),
            pltpu.VMEM((256, 128), F32),
            pltpu.VMEM((256, CH), F32),
            pltpu.VMEM((CH, 128), F32),
            whole(rows=8),
            pltpu.SemaphoreType.DMA((2,)),
            *state_refs(),
        ],
        flops=2 * 10**10,
        limit=40,
        in_specs=[FAR] + [LOCAL] * 7,
        out_specs=[FAR] + [LOCAL] * 7,
    )(*far(cot), *args)


def local_encode(*args):
    return call(
        encode_kernel,
        [shape((CH, CORE)), shape((2 * SUM_ROWS, 128))],
        [
            pltpu.VMEM((2 * CH, HCORE), BF),
            halves(),
            pltpu.VMEM((128, 256), F32),
            pltpu.VMEM((CH, 256), F32),
            pltpu.VMEM((CH, 128), F32),
            pltpu.SemaphoreType.DMA((CORE // STEP,)),
            *state_refs(),
        ],
        flops=2 * 10**10,
        limit=40,
        in_specs=[LOCAL] * 13,
        out_specs=[FAR, LOCAL],
    )(*args)


def local_unpack(sums):
    block = [shape((4, 3, CH, CH)), shape((4, CH)), shape((4, CH, CH)), shape((4, CH))]
    return call(
        unpack_kernel,
        [
            shape((CH, CODES)),
            *block,
            shape((4, CH, CH)),
            shape((1, CH)),
            shape((4, CH, CH)),
            shape((1, CH)),
            *block,
        ],
    )(sums)


AXES = ("tm", "batch")
FIRST = (0, 1)
SCATTER = 1


def plan_of(first_of):
    tm, batch = lax.axis_size("tm"), lax.axis_size("batch")
    rings = []
    stride = 2
    while stride < tm:
        size = min(4, tm // stride)
        rings.append(("tm", stride, size))
        stride *= size
    rings.append(("batch", 1, batch))
    devices = [(t, b) for t in range(tm) for b in range(batch)]
    me = (lax.axis_index("tm"), lax.axis_index("batch"))

    def digit_of(ring, t, b):
        axis, stride, size = ring
        return (t if axis == "tm" else b) // stride % size

    def turned(ring, by, t, b):
        axis, stride, size = ring
        here = digit_of(ring, t, b)
        by = ((here + by) % size - here) * stride
        to = (t + by, b) if axis == "tm" else (t, b + by)
        return (t * batch + b, to[0] * batch + to[1])

    out = []
    for n in range(len(rings)):
        own = [rings[(n + f) % len(rings)] for f in first_of]
        size = own[0][2]
        turns = [[turned(own[t % 2], s, t, b) for t, b in devices] for s in range(1, size)]
        digit = jnp.where(me[0] % 2 == 0, digit_of(own[0], *me), digit_of(own[1], *me))
        out.append((turns, digit))
    return out


def piece(value, index, count):
    rows = value.shape[0] // count
    return lax.dynamic_slice_in_dim(value, lax.rem(index, count) * rows, rows, 0)


def added(mine, got):
    if len(got) == 1:
        return mine + got[0]
    return (mine + got[1]) + (got[0] + got[2])


def gathered(mine, got, digit):
    count, rows = len(got) + 1, mine.shape[0]
    out = jnp.zeros((count * rows, mine.shape[1]), mine.dtype)
    for s, part in enumerate([mine] + got):
        at = lax.rem(digit - s + count, count) * rows
        out = lax.dynamic_update_slice_in_dim(out, part, at, 0)
    return out


def sum_all(value):
    tm, batch = lax.axis_size("tm"), lax.axis_size("batch")
    core = lax.axis_index("tm") % 2
    swap = [(t * batch + b, (t ^ 1) * batch + b) for t in range(tm) for b in range(batch)]
    plan = plan_of(FIRST)
    value = piece(value, core, 2) + lax.ppermute(piece(value, core + 1, 2), AXES, swap)
    for n, (turns, digit) in enumerate(plan):
        count = len(turns) + 1
        if n < SCATTER:
            got = [
                lax.ppermute(piece(value, digit + s + 1, count), AXES, turn)
                for s, turn in enumerate(turns)
            ]
            value = added(piece(value, digit, count), got)
        else:
            value = added(value, [lax.ppermute(value, AXES, turn) for turn in turns])
    for turns, digit in plan[:SCATTER][::-1]:
        value = gathered(value, [lax.ppermute(value, AXES, turn) for turn in turns], digit)
    return gathered(value, [lax.ppermute(value, AXES, swap)], core)


def on_device(
    frames, clip_start, code_ids, cotangent,
    enc_conv, enc_conv_bias, enc_proj, enc_proj_bias, downscale_weight, downscale_bias,
    codebook, up_weight, up_bias, dec_conv, dec_conv_bias, dec_proj, dec_proj_bias,
):
    frames = frames.reshape(CH, CORE)
    cotangent = cotangent.reshape(CH, CORE)
    front, tail = local_pack(frames, cotangent, clip_start, code_ids)
    count = lax.axis_size("tm")
    ring = [(i, (i + 1) % count) for i in range(count)]
    lo = lax.ppermute(tail, "tm", ring)
    hi = lax.ppermute(front, "tm", [(j, i) for i, j in ring])
    enc_w, dec_w, bias, cbt, chosen = local_prep(
        enc_conv, enc_conv_bias, enc_proj, enc_proj_bias,
        downscale_weight, downscale_bias.reshape(1, CH),
        codebook.T, up_weight, up_bias.reshape(1, CH),
        dec_conv, dec_conv_bias, dec_proj, dec_proj_bias, code_ids,
    )
    rebuilt, quant_grad, dec_grads, mf, mb, mh, mhb, chosen = local_decode(
        cotangent, lo, hi, clip_start, chosen, cbt, dec_w, bias
    )
    frames_grad, sums = local_encode(
        frames, lo, hi, code_ids, quant_grad, dec_grads, chosen, mf, mb, mh, mhb,
        enc_w, bias,
    )
    out = list(local_unpack(sum_all(sums)))
    cg = out.pop(0).T
    out[5] = out[5].reshape(CH)
    out[7] = out[7].reshape(CH)
    out.insert(6, cg)
    return (rebuilt[None], frames_grad[None], *out)


def solution(mesh):
    split_spec = P("batch", None, "tm")
    row_spec = P("batch", "tm")
    return jax.shard_map(
        on_device,
        mesh=mesh,
        in_specs=(split_spec, row_spec, row_spec, split_spec) + (P(),) * 13,
        out_specs=(split_spec, split_spec) + (P(),) * 13,
        check_vma=False,
    )
```

```python
import functools

import jax
import jax.numpy as jnp
from jax import lax
from jax.experimental import pallas as pl
from jax.experimental.pallas import tpu as pltpu
from jax.sharding import PartitionSpec as P

COMMIT = 0.02
DILATIONS = (1, 3, 9, 27)
BF = jnp.bfloat16
F32 = jnp.float32
CH = 64
CODES = 2048
CORE = 4096
HALO = 128
EXT = CORE + 2 * HALO
HCORE = CORE // 2
HEXT = EXT // 2
G0 = 0.7978845608028654
G1 = G0 * 0.044715
MB = 2**20
GRAD_PROJ = 384
GRAD_PAIR = 512
GRAD_BIAS = 640
GRAD_ROWS = 704
CODE_ROWS = CODES // 2
DEC_CUT = 192
SUM_ROWS = CODE_ROWS + DEC_CUT


BLOCK_ROWS = 448
PAIR_AT = 4 * BLOCK_ROWS
WEIGHT_ROWS = PAIR_AT + 384


PARTS = {"conv": (0, 192), "conv_back": (192, 128), "proj": (320, 64), "proj_back": (384, 64)}


def part_rows(name, b):
    first, rows = PARTS[name]
    return slice(BLOCK_ROWS * b + first, BLOCK_ROWS * b + first + rows)


def part(w, name, b):
    return w[part_rows(name, b), :192]


def dot(a, b):
    return jnp.dot(a, b, preferred_element_type=F32)


def dot_nt(a, b):
    return lax.dot_general(a, b, (((1,), (1,)), ((), ())), preferred_element_type=F32)


def split(v):
    hi = v.astype(BF)
    return hi, (v - hi.astype(F32)).astype(BF)


def gelu_both(v):
    s = v * v
    t = jnp.tanh(v * (G0 + G1 * s))
    cdf = 0.5 + 0.5 * t
    slope = cdf + (0.5 * v) * (1.0 - t * t) * (G0 + (3.0 * G1) * s)
    return v * cdf, slope


def tile_rows(rows, times):
    return jnp.concatenate([rows] * times, axis=0)


def aligned(start):
    return start if isinstance(start, int) else pl.multiple_of(start, 128)


def lanes(ref, start, size, rows=slice(None)):
    return ref[rows, pl.ds(aligned(start), size)]


def wrap(start, length):
    return start % length if isinstance(start, int) else lax.rem(start + length, length)


def from_left(ref, rows, start, size, offset, length):
    if size == length:
        return pltpu.roll(lanes(ref, 0, length, rows), offset, 1)
    win = jnp.concatenate(
        [lanes(ref, wrap(start - 128, length), 128, rows), lanes(ref, start, size, rows)], axis=1
    )
    return pltpu.roll(win, offset, 1)[:, 128:]


def from_right(ref, rows, start, size, offset, length):
    if size == length:
        return pltpu.roll(lanes(ref, 0, length, rows), length - offset, 1)
    win = jnp.concatenate(
        [lanes(ref, start, size, rows), lanes(ref, wrap(start + size, length), 128, rows)], axis=1
    )
    return pltpu.roll(win, size + 128 - offset, 1)[:, :size]


def sweep(fn):
    fn(0, EXT, True)


def half_sweep(fn):
    fn(0, HEXT, True)


def apart(fn):
    pl.when(lax.axis_index("tm") >= 0)(fn)


def lane_fold(v):
    out = v[:, :128]
    for i in range(1, v.shape[1] // 128):
        out = out + v[:, i * 128 : (i + 1) * 128]
    return out


def selector():
    row = lax.broadcasted_iota(jnp.int32, (256, 256), 0)
    col = lax.broadcasted_iota(jnp.int32, (256, 256), 1)
    source = jnp.where(col < 128, 2 * col, 2 * (col - 128) + 1)
    return jnp.where(row == source, 1.0, 0.0).astype(BF)


def pack_kernel(frames, cot, clip, codes, front, tail, clip_v, codes_v, sems):
    first, final = slice(0, HALO), slice(CORE - HALO, CORE)
    copies = [
        pltpu.make_async_copy(src, dst, sems.at[n])
        for n, (src, dst) in enumerate(
            (
                (frames.at[:, first], front.at[:CH]),
                (frames.at[:, final], tail.at[:CH]),
                (cot.at[:, first], front.at[CH : 2 * CH]),
                (cot.at[:, final], tail.at[CH : 2 * CH]),
                (clip, clip_v),
                (codes, codes_v),
            )
        )
    ]
    for copy in copies:
        copy.start()
    for copy in copies:
        copy.wait()
    me = lax.axis_index("tm")
    count = lax.axis_size("tm")
    lane = lax.broadcasted_iota(jnp.int32, (1, HALO), 1)
    blank = jnp.zeros((6, HALO), F32)
    for out, cut, at_end, half, keep in (
        (front, first, me == 0, slice(0, HALO), lane < 64),
        (tail, final, me == count - 1, slice(HCORE - HALO, HCORE), lane >= 64),
    ):
        clip_row = jnp.where(at_end, -1.0, clip_v[:, cut].astype(F32))
        code_row = jnp.where(keep, codes_v[:, half].astype(F32), 0.0)
        out[2 * CH :, :] = jnp.concatenate([clip_row, code_row, blank], axis=0)


def prep_kernel(*refs):
    sources, outs, scratch = refs[:14], refs[14:19], refs[19:]
    cb, codes = refs[6], refs[13]
    sems = scratch[-1]
    copies = [
        pltpu.make_async_copy(src, dst, sems.at[n])
        for n, (src, dst) in enumerate(zip(sources, scratch[:14]))
    ]
    for n in (*range(6), *range(7, 13)):
        copies[n].start()
    ec, ecb, ep, epb, dw, db, _, uw, ub, dc, dcb, dp, dpb = scratch[:13]
    enc_w, dec_w, bias, cbt, chosen = outs

    def forms(w):
        hi, lo = split(w)
        return jnp.concatenate([hi, hi, lo], axis=1)

    def stacked(w):
        hi, lo = split(w)
        return jnp.concatenate([hi, lo], axis=0)

    def column(row):
        return jnp.broadcast_to(row, (128, CH)).T

    cbt[...] = stacked(cb[...])
    pick(codes, cbt, chosen, 0, HCORE, 1024)
    for n in (*range(6), *range(7, 13)):
        copies[n].wait()
    for n, (conv, cbias, proj, pbias) in enumerate(((ec, ecb, ep, epb), (dc, dcb, dp, dpb))):
        weights = (enc_w, dec_w)[n]
        for b in range(4):
            at = 4 * n + b
            weights[part_rows("conv", b), :192] = forms(conv[b].reshape(3 * CH, CH))
            weights[part_rows("conv_back", b), :192] = stacked(jnp.concatenate([conv[b, k].T for k in range(3)], axis=1))
            weights[part_rows("proj", b), :192] = forms(proj[b])
            weights[part_rows("proj_back", b), :192] = forms(proj[b].T)
            bias[2 * at] = column(cbias[b : b + 1, :])
            bias[2 * at + 1] = column(pbias[b : b + 1, :])
    bias[16] = column(db[...])
    bias[17] = column(ub[...])
    enc_w[PAIR_AT : PAIR_AT + 128, :] = stacked(jnp.concatenate([dw[k] for k in range(4)], axis=1))
    enc_w[PAIR_AT + 128 :, :192] = forms(jnp.concatenate([dw[k].T for k in range(4)], axis=0))
    dec_w[PAIR_AT : PAIR_AT + 128, :] = stacked(jnp.concatenate([uw[k].T for k in range(4)], axis=1))
    dec_w[PAIR_AT + 128 :, :192] = forms(jnp.concatenate([uw[k] for k in range(4)], axis=0))


def one_hot(ids_row, first, count):
    row = lax.broadcasted_iota(jnp.int32, (count, ids_row.shape[1]), 0) + first
    return jnp.where(row == ids_row, 1.0, 0.0).astype(BF)


def pick(ids, cbt, chosen, begin, end, step):
    for start in range(begin, end, step):
        at = slice(start - begin, start - begin + step)
        to = slice(start, start + step)
        both = dot(cbt[...], one_hot(ids[0:1, at], 0, CODES))
        chosen[:, to] = both[:CH] + both[CH:]


def stack_forward(x_ref, z_refs, blocks, dils, w, bias, mf, keep, last):
    def enter(value, start, size, b):
        act, slope = gelu_both(value)
        hi, lo = split(act)
        a_ref, gx_ref, _, _ = keep(b)
        a_ref[:CH, pl.ds(aligned(start), size)] = hi
        a_ref[CH:, pl.ds(aligned(start), size)] = lo
        gx_ref[:, pl.ds(aligned(start), size)] = slope
        z_refs[b % 2][:, pl.ds(aligned(start), size)] = dot(
            part(w, "conv", b), jnp.concatenate([hi, lo, hi], axis=0)
        )

    def first(start, size, core):
        enter(lanes(x_ref, start, size), start, size, 0)

    sweep(first)
    for b in range(4):
        d = dils[b]
        m = DILATIONS.index(d)
        z_ref = z_refs[b % 2]

        def step(start, size, core, b=b, d=d, m=m, z_ref=z_ref):
            _, _, u_ref, gh_ref = keep(b)
            times = size // 128
            left = tile_rows(lanes(mf, start, size, slice(16 * m, 16 * m + 8)), 8)
            right = tile_rows(lanes(mf, start, size, slice(16 * m + 8, 16 * m + 16)), 8)
            cb = jnp.concatenate([bias[2 * (blocks + b)]] * times, axis=1)
            hidden = lanes(z_ref, start, size, slice(CH, 2 * CH)) + cb
            hidden = hidden + left * from_left(z_ref, slice(0, CH), start, size, d, EXT)
            hidden = hidden + right * from_right(z_ref, slice(2 * CH, 3 * CH), start, size, d, EXT)
            act, slope = gelu_both(hidden)
            hi, lo = split(act)
            u_ref[:CH, pl.ds(aligned(start), size)] = hi
            u_ref[CH:, pl.ds(aligned(start), size)] = lo
            gh_ref[:, pl.ds(aligned(start), size)] = slope
            pbias = jnp.concatenate([bias[2 * (blocks + b) + 1]] * times, axis=1)
            out = (
                lanes(x_ref, start, size)
                + dot(part(w, "proj", b), jnp.concatenate([hi, lo, hi], axis=0))
                + pbias
            )
            if b < 3:
                x_ref[:, pl.ds(aligned(start), size)] = out
                enter(out, start, size, b + 1)
            else:
                last(out, start, size, core)

        sweep(step)


def stack_backward(g_ref, gh_refs, blocks, dils, w, mb, keep, acc, finish, last):
    dk1, dk2, dpa, csum, psum = acc

    def enter(grad, start, size, core, b):
        _, _, u_ref, slope_ref = keep(b)
        hi, lo = split(grad)
        q = dot(part(w, "proj_back", b), jnp.concatenate([hi, lo, hi], axis=0))
        gh = lanes(slope_ref, start, size) * q
        ghi, glo = split(gh)
        gh_refs[b % 2][:CH, pl.ds(aligned(start), size)] = ghi
        gh_refs[b % 2][CH:, pl.ds(aligned(start), size)] = glo
        if core:
            both = jnp.concatenate([hi, lo], axis=0)[:, :CORE]
            dpa[b] += dot_nt(both, lanes(u_ref, 0, CORE))
            csum[b] += lane_fold(gh[:, :CORE])
            psum[b] += lane_fold(grad[:, :CORE])

    for ref in acc:
        ref[...] = jnp.zeros(ref.shape, ref.dtype)

    def first(start, size, core):
        enter(lanes(g_ref, start, size), start, size, core, 3)

    sweep(first)
    for b in (3, 2, 1, 0):
        d = dils[b]
        m = DILATIONS.index(d)
        gh_ref = gh_refs[b % 2]

        def step(start, size, core, b=b, d=d, m=m, gh_ref=gh_ref):
            a_ref, gx_ref, _, _ = keep(b)
            left = tile_rows(lanes(mb, start, size, slice(32 * m, 32 * m + 16)), 4)
            right = tile_rows(lanes(mb, start, size, slice(32 * m + 16, 32 * m + 32)), 4)
            parts = []
            for rows in (slice(0, CH), slice(CH, 2 * CH)):
                parts.append(
                    jnp.concatenate(
                        [
                            from_right(gh_ref, rows, start, size, d, EXT) * right,
                            lanes(gh_ref, start, size, rows),
                            from_left(gh_ref, rows, start, size, d, EXT) * left,
                        ],
                        axis=0,
                    )
                )
            ghi, glo = parts
            both = dot(part(w, "conv_back", b), ghi)
            ga = both[:CH] + both[CH:] + dot(part(w, "conv_back", b)[:CH], glo)
            if core:
                act = lanes(a_ref, 0, CORE)
                dk1[b] += dot_nt(ghi[:, :CORE], act)
                dk2[b] += dot_nt(glo[:, :CORE], act[:CH])
            out = lanes(g_ref, start, size) + lanes(gx_ref, start, size) * ga
            if b > 0:
                g_ref[:, pl.ds(aligned(start), size)] = out
                enter(out, start, size, core, b - 1)
            else:
                last(out, start, size, core)

        sweep(step)
    for b in range(4):
        dk = dk1[b, :, :CH] + dk1[b, :, CH:] + dk2[b]
        dp = dpa[b, :CH, :CH] + dpa[b, CH:, :CH] + dpa[b, :CH, CH:]
        finish(b, dk, dp, csum[b], psum[b])


def store_grads(grads, folded):
    kept = {}

    def finish(b, dk, dp, csum, psum):
        kept[b] = (dk, dp)
        if b % 2:
            at = b // 2
            grads[at * 192 : (at + 1) * 192, :] = jnp.concatenate([kept[b - 1][0], dk], axis=1)
            grads[GRAD_PROJ + at * CH : GRAD_PROJ + (at + 1) * CH, :] = jnp.concatenate(
                [kept[b - 1][1], dp], axis=1
            )
        folded.extend([csum, psum])

    return finish


def store_columns(grads, folded):
    lane = lax.broadcasted_iota(jnp.int32, (CH, 128), 1)
    totals = [jnp.sum(v, axis=1, keepdims=True) for v in folded]
    out = jnp.zeros((CH, 128), F32)
    for at, total in enumerate(totals):
        out = jnp.where(lane == at, total, out)
    grads[GRAD_BIAS:, :] = out


def to_halves(value, sel, e_ref, o_ref, start, size):
    hi, lo = split(value)
    both = jnp.concatenate([hi, lo], axis=0)
    half = start // 2
    for i in range(size // 256):
        out = dot(both[:, i * 256 : (i + 1) * 256], sel).astype(BF)
        e_ref[:, pl.ds(aligned(half + i * 128), 128)] = out[:, :128]
        o_ref[:, pl.ds(aligned(half + i * 128), 128)] = out[:, 128:]


def pair_stack(e_ref, o_ref, mhb, start, size):
    masks = [tile_rows(lanes(mhb, start, size, slice(16 * i, 16 * i + 16)), 4) for i in range(3)]
    parts = []
    for rows in (slice(0, CH), slice(CH, 2 * CH)):
        parts.append(
            jnp.concatenate(
                [
                    from_left(o_ref, rows, start, size, 1, HEXT) * masks[0],
                    lanes(e_ref, start, size, rows),
                    lanes(o_ref, start, size, rows) * masks[1],
                    from_right(e_ref, rows, start, size, 1, HEXT) * masks[2],
                ],
                axis=0,
            )
        )
    return parts


def pair_gather(w, parts):
    both = dot(w[...], parts[0])
    return both[:CH] + both[CH:] + dot(w[:CH], parts[1])


def spread(w, hl_ref, mh, z_refs, sel, bias_tile, x_ref):
    def first(start, size, core):
        both = lanes(hl_ref, start, size)
        z = dot(w, jnp.concatenate([both, both[:CH]], axis=0))
        masks = [tile_rows(lanes(mh, start, size, slice(8 * i, 8 * i + 8)), 8) for i in range(3)]
        at = pl.ds(aligned(start), size)
        z_refs[0][:, at] = z[0:64] * masks[0]
        z_refs[1][:, at] = z[64:128]
        z_refs[2][:, at] = z[128:192] * masks[1]
        z_refs[3][:, at] = z[192:256] * masks[2]

    half_sweep(first)

    def second(start, size, core):
        every = slice(None)
        even = lanes(z_refs[1], start, size) + from_left(z_refs[3], every, start, size, 1, HEXT)
        odd = lanes(z_refs[2], start, size) + from_right(z_refs[0], every, start, size, 1, HEXT)
        ehi, elo = split(even)
        ohi, olo = split(odd)
        for i in range(size // 128):
            cut = slice(i * 128, (i + 1) * 128)
            rows = jnp.concatenate(
                [
                    jnp.concatenate([ehi[:, cut], ohi[:, cut]], axis=1),
                    jnp.concatenate([elo[:, cut], olo[:, cut]], axis=1),
                ],
                axis=0,
            )
            out = dot_nt(rows, sel)
            out = out[:CH] + out[CH:]
            if bias_tile is not None:
                out = out + jnp.concatenate([bias_tile, bias_tile], axis=1)
            x_ref[:, pl.ds(aligned(2 * start + 256 * i), 256)] = out

    half_sweep(second)


def ring_fill(ref, core, hi, lo):
    if core is not None:
        ref[:, :CORE] = core
    ref[:, CORE : CORE + HALO] = hi
    ref[:, CORE + HALO :] = lo


def find_links(clip_ref, sel, mf, mb, mh, mhb):
    def links(start, size, core):
        at = pl.ds(aligned(start), size)
        here = lanes(clip_ref, start, size)

        def same(other):
            return jnp.where(other == here, 1.0, 0.0)

        for m, d in enumerate(DILATIONS):
            left = same(from_left(clip_ref, slice(None), start, size, d, EXT))
            right = same(from_right(clip_ref, slice(None), start, size, d, EXT))
            mf[16 * m : 16 * m + 8, at] = left
            mf[16 * m + 8 : 16 * m + 16, at] = right
            mb[32 * m : 32 * m + 16, at] = tile_rows(left, 2).astype(BF)
            mb[32 * m + 16 : 32 * m + 32, at] = tile_rows(right, 2).astype(BF)
            if m == 0:
                two = same(from_right(clip_ref, slice(None), start, size, 2, EXT))
                rows = jnp.concatenate([left, right, two, two], axis=0).astype(BF)
                half = start // 2
                for i in range(size // 256):
                    out = dot(rows[:, i * 256 : (i + 1) * 256], sel)[:, :128]
                    hat = pl.ds(aligned(half + 128 * i), 128)
                    mh[:, hat] = out[:24]
                    for n in range(3):
                        mhb[16 * n : 16 * n + 16, hat] = tile_rows(
                            out[8 * n : 8 * n + 8], 2
                        ).astype(BF)

    sweep(links)


def sum_refs():
    return [
        pltpu.VMEM((4, 3 * CH, 2 * CH), F32),
        pltpu.VMEM((4, 3 * CH, CH), F32),
        pltpu.VMEM((4, 2 * CH, 2 * CH), F32),
        pltpu.VMEM((4, CH, 128), F32),
        pltpu.VMEM((4, CH, 128), F32),
    ]


def state_refs():
    return [
        whole(),
        whole(rows=192),
        whole(rows=192),
        pltpu.VMEM((4, 128, EXT), BF),
        pltpu.VMEM((4, CH, EXT), F32),
        pltpu.VMEM((4, 128, EXT), BF),
        pltpu.VMEM((4, CH, EXT), F32),
        whole(),
        whole(BF, 128),
        whole(BF, 128),
        halves(),
        halves(),
        *sum_refs(),
    ]


def decode_kernel(
    cot, lo, hi, clip, chosen_in, cbt, weights, bias,
    rebuilt, quant_grad, grads, mf, mb, mh, mhb, chosen, chosen_hl, ids,
    up1, up2, usum, clip_ref, sems, x_ref, z0, z1, a_s, gx_s, u_s, gh_s, g_ref, g0, g1, e_ref, o_ref,
    *acc,
):
    ug = weights.at[PAIR_AT : PAIR_AT + 128]
    us = weights.at[PAIR_AT + 128 :]
    cot_in = pltpu.make_async_copy(cot, g_ref.at[:, :CORE], sems.at[0])
    cot_in.start()
    sel = selector()
    ring_fill(
        clip_ref,
        jnp.broadcast_to(clip[...].astype(F32), (8, CORE)),
        jnp.broadcast_to(hi[128:129], (8, HALO)),
        jnp.broadcast_to(lo[128:129], (8, HALO)),
    )
    apart(lambda: find_links(clip_ref, selector(), mf, mb, mh, mhb))
    chosen[:, :HCORE] = chosen_in[...]
    ids[...] = jnp.broadcast_to((hi[129:130] + lo[129:130]).astype(jnp.int32), (8, HALO))
    pick(ids, cbt, chosen, HCORE, HEXT, HALO)
    chi, clo = split(chosen[...])
    chosen_hl[:CH] = chi
    chosen_hl[CH:] = clo
    zu = [z0.at[:CH], z0.at[CH : 2 * CH], z0.at[2 * CH :], z1.at[:CH]]
    apart(lambda: spread(us[:, :192], chosen_hl, mh, zu, selector(), bias[17], x_ref))

    def keep(b):
        return a_s.at[b], gx_s.at[b], u_s.at[b], gh_s.at[b]

    def last(out, start, size, core):
        if core:
            x_ref[:, :CORE] = out[:, :CORE]

    order = DILATIONS[::-1]
    apart(lambda: stack_forward(x_ref, (z0, z1), 4, order, weights, bias, mf, keep, last))
    rebuilt_out = pltpu.make_async_copy(x_ref.at[:, :CORE], rebuilt, sems.at[1])
    rebuilt_out.start()
    cot_in.wait()
    ring_fill(g_ref, None, hi[CH : 2 * CH], lo[CH : 2 * CH])
    for ref in (up1, up2, usum):
        ref[...] = jnp.zeros(ref.shape, F32)
    @apart
    def _():
        folded = []
        take = selector()

        def last_back(out, start, size, core):
            to_halves(out, take, e_ref, o_ref, start, size)
            if core:
                usum[...] += lane_fold(out[:, :CORE])

        stack_backward(
            g_ref, (g0, g1), 4, order, weights, mb, keep, acc, store_grads(grads, folded), last_back
        )
        store_columns(grads, folded + [usum[...]])

    def up(start, size, core):
        parts = pair_stack(e_ref, o_ref, mhb, start, size)
        quant_grad[:, pl.ds(aligned(start), size)] = pair_gather(ug, parts)
        if core:
            both = lanes(chosen_hl, 0, HCORE)
            up1[...] += dot_nt(parts[0][:, :HCORE], both)
            up2[...] += dot_nt(parts[1][:, :HCORE], both[:CH])

    half_sweep(up)
    total = up1[:, :CH] + up1[:, CH:] + up2[...]
    grads[GRAD_PAIR:GRAD_BIAS, :] = jnp.concatenate([total[: 2 * CH], total[2 * CH :]], axis=1)
    rebuilt_out.wait()


def encode_kernel(
    frames, lo, hi, codes, quant_grad, dec_grads, chosen, mf, mb, mh, mhb, weights, bias,
    frames_grad, all_sums,
    d_ref, l_ref, down1, down2, dsum, sems,
    x_ref, z0, z1, a_s, gx_s, u_s, gh_s, g_ref, g0, g1, e_ref, o_ref, *acc,
):
    dg = weights.at[PAIR_AT : PAIR_AT + 128]
    ds_ = weights.at[PAIR_AT + 128 :]
    ring_fill(x_ref, frames[...], hi[:CH], lo[:CH])
    sums, sums_b = all_sums.at[:SUM_ROWS], all_sums.at[SUM_ROWS:]
    grads = sums_b.at[GRAD_ROWS - DEC_CUT :]
    sums[CODE_ROWS:, :] = dec_grads[:DEC_CUT, :]
    sums_b[: GRAD_ROWS - DEC_CUT, :] = dec_grads[DEC_CUT:, :]

    def keep(b):
        return a_s.at[b], gx_s.at[b], u_s.at[b], gh_s.at[b]

    @apart
    def _():
        take = selector()

        def last(out, start, size, core):
            to_halves(out, take, e_ref, o_ref, start, size)

        stack_forward(x_ref, (z0, z1), 0, DILATIONS, weights, bias, mf, keep, last)

    for ref in (down1, down2, dsum):
        ref[...] = jnp.zeros(ref.shape, F32)
    folded = []

    def down(start, size, core):
        at = pl.ds(aligned(start), size)
        parts = pair_stack(e_ref, o_ref, mhb, start, size)
        value = pair_gather(dg, parts) + jnp.concatenate([bias[16]] * (size // 128), axis=1)
        gap = value - lanes(chosen, start, size)
        grad = quant_grad[:, at] + (2.0 * COMMIT) * gap
        hi, lo = split(grad)
        l_ref[:CH, at] = hi
        l_ref[CH:, at] = lo
        if core:
            dhi, dlo = split(-2.0 * gap[:, :HCORE])
            d_ref[:CH, :] = dhi
            d_ref[CH:, :] = dlo
            dsum[...] += lane_fold(grad[:, :HCORE])
            both = jnp.concatenate([hi, lo], axis=0)
            down1[...] += dot_nt(both[:, :HCORE], parts[0][:, :HCORE])
            down2[...] += dot_nt(hi[:, :HCORE], parts[1][:, :HCORE])

    apart(lambda: half_sweep(down))

    def codes_back(i, carry):
        hot = one_hot(codes[...], i * 512, 512)
        out = dot_nt(d_ref[...], hot)
        out = out[:CH] + out[CH:]
        at = pl.multiple_of(i * 256, 256)
        for n in range(4):
            sums[pl.ds(at + CH * n, CH), :] = out[:, 128 * n : 128 * (n + 1)]
        return carry

    lax.fori_loop(0, CODES // 512, codes_back, 0)
    zu = [z0.at[:CH], z0.at[CH : 2 * CH], z0.at[2 * CH :], z1.at[:CH]]
    apart(lambda: spread(ds_[:, :192], l_ref, mh, zu, selector(), None, g_ref))

    @apart
    def _():
        folded = []
        leaving = []

        def last_back(out, start, size, core):
            if core:
                at = slice(0, CORE)
                x_ref[:, at] = out[:, at]
                leaving.append(
                    pltpu.make_async_copy(
                        x_ref.at[:, at], frames_grad.at[:, at], sems.at[len(leaving)]
                    )
                )
                leaving[-1].start()

        stack_backward(
            g_ref, (g0, g1), 0, DILATIONS, weights, mb, keep, acc, store_grads(grads, folded), last_back
        )
        total = down1[:CH] + down1[CH:] + down2[...]
        grads[GRAD_PAIR : GRAD_PAIR + CH, :] = total[:, : 2 * CH]
        grads[GRAD_PAIR + CH : GRAD_BIAS, :] = total[:, 2 * CH :]
        store_columns(grads, folded + [dsum[...]])
        for copy in leaving:
            copy.wait()


def unpack_kernel(
    all_sums,
    cg, ec, ecb, ep, epb, dw, db, uw, ub, dc, dcb, dp, dpb,
):
    sums, sums_b = all_sums.at[:SUM_ROWS], all_sums.at[SUM_ROWS:]
    for i in range(CODES // 128):
        cg[:, i * 128 : (i + 1) * 128] = sums[i * CH : (i + 1) * CH, :]

    def enc(first, rows):
        at = GRAD_ROWS - DEC_CUT + first
        return sums_b[at : at + rows, :]

    def dec(first, rows):
        if first < DEC_CUT:
            return sums[CODE_ROWS + first : CODE_ROWS + first + rows, :]
        return sums_b[first - DEC_CUT : first - DEC_CUT + rows, :]

    for src, conv, cbias, proj, pbias, single in (
        (enc, ec, ecb, ep, epb, db),
        (dec, dc, dcb, dp, dpb, ub),
    ):
        rows = src(GRAD_BIAS, CH).T
        for b in range(4):
            at = slice((b % 2) * CH, (b % 2 + 1) * CH)
            p = b // 2
            conv[b] = src(p * 192, 192)[:, at].reshape(3, CH, CH)
            proj[b] = src(GRAD_PROJ + p * CH, CH)[:, at]
            cbias[b : b + 1, :] = rows[2 * b : 2 * b + 1]
            pbias[b : b + 1, :] = rows[2 * b + 1 : 2 * b + 2]
        single[...] = rows[8:9]
    for k in range(4):
        a, b = k // 2, k % 2
        dw[k] = enc(GRAD_PAIR + a * CH, CH)[:, b * CH : (b + 1) * CH]
        uw[k] = dec(GRAD_PAIR + b * CH, CH)[:, a * CH : (a + 1) * CH]


def shape(dims, kind=F32):
    return jax.ShapeDtypeStruct(dims, kind)


def call(kernel, outs, scratch=(), flops=0, limit=40, in_specs=None, out_specs=None):
    extra = {}
    if in_specs is not None:
        extra["in_specs"] = in_specs
    if out_specs is not None:
        extra["out_specs"] = out_specs
    return pl.pallas_call(
        kernel,
        out_shape=outs,
        scratch_shapes=list(scratch),
        compiler_params=pltpu.CompilerParams(vmem_limit_bytes=limit * MB),
        cost_estimate=pl.CostEstimate(flops=flops, bytes_accessed=2**20, transcendentals=0),
        **extra,
    )


def halves(kind=BF, rows=2 * CH):
    return pltpu.VMEM((rows, HEXT), kind)


def whole(kind=F32, rows=CH):
    return pltpu.VMEM((rows, EXT), kind)


FAR = pl.BlockSpec(memory_space=pltpu.HBM)


def far(*values):
    return [pltpu.with_memory_space_constraint(v, pltpu.HBM) for v in values]
LOCAL = pl.BlockSpec()


def local_pack(frames, cot, clip, codes):
    return call(
        pack_kernel,
        [shape((136, HALO)), shape((136, HALO))],
        [
            pltpu.VMEM((1, CORE), jnp.int32),
            pltpu.VMEM((1, HCORE), jnp.int32),
            pltpu.SemaphoreType.DMA((6,)),
        ],
        in_specs=[FAR] * 4,
    )(*far(frames, cot, clip, codes))


def local_prep(*args):
    return call(
        prep_kernel,
        [
            shape((WEIGHT_ROWS, 256), BF),
            shape((WEIGHT_ROWS, 256), BF),
            shape((18, CH, 128)),
            shape((128, CODES), BF),
            shape((CH, HCORE)),
        ],
        [pltpu.VMEM(a.shape, a.dtype) for a in args] + [pltpu.SemaphoreType.DMA((14,))],
        flops=10**7,
        limit=40,
        in_specs=[LOCAL if n in (6, 13) else FAR for n in range(14)],
    )(*[v if n in (6, 13) else far(v)[0] for n, v in enumerate(args)])


def local_decode(cot, *args):
    return call(
        decode_kernel,
        [
            shape((CH, CORE)),
            shape((CH, HEXT)),
            shape((GRAD_ROWS, 128)),
            shape((64, EXT)),
            shape((128, EXT), BF),
            shape((24, HEXT)),
            shape((48, HEXT), BF),
            shape((CH, HEXT)),
        ],
        [
            halves(),
            pltpu.VMEM((8, HALO), jnp.int32),
            pltpu.VMEM((256, 128), F32),
            pltpu.VMEM((256, CH), F32),
            pltpu.VMEM((CH, 128), F32),
            whole(rows=8),
            pltpu.SemaphoreType.DMA((2,)),
            *state_refs(),
        ],
        flops=2 * 10**10,
        limit=40,
        in_specs=[FAR] + [LOCAL] * 7,
        out_specs=[FAR] + [LOCAL] * 7,
    )(*far(cot), *args)


def local_encode(*args):
    return call(
        encode_kernel,
        [shape((CH, CORE)), shape((2 * SUM_ROWS, 128))],
        [
            pltpu.VMEM((2 * CH, HCORE), BF),
            halves(),
            pltpu.VMEM((128, 256), F32),
            pltpu.VMEM((CH, 256), F32),
            pltpu.VMEM((CH, 128), F32),
            pltpu.SemaphoreType.DMA((1,)),
            *state_refs(),
        ],
        flops=2 * 10**10,
        limit=40,
        in_specs=[LOCAL] * 13,
        out_specs=[FAR, LOCAL],
    )(*args)


def local_unpack(sums):
    block = [shape((4, 3, CH, CH)), shape((4, CH)), shape((4, CH, CH)), shape((4, CH))]
    return call(
        unpack_kernel,
        [
            shape((CH, CODES)),
            *block,
            shape((4, CH, CH)),
            shape((1, CH)),
            shape((4, CH, CH)),
            shape((1, CH)),
            *block,
        ],
    )(sums)


AXES = ("tm", "batch")
FIRST = (0, 1)
SCATTER = 1


def plan_of(first_of):
    tm, batch = lax.axis_size("tm"), lax.axis_size("batch")
    rings = []
    stride = 2
    while stride < tm:
        size = min(4, tm // stride)
        rings.append(("tm", stride, size))
        stride *= size
    rings.append(("batch", 1, batch))
    devices = [(t, b) for t in range(tm) for b in range(batch)]
    me = (lax.axis_index("tm"), lax.axis_index("batch"))

    def digit_of(ring, t, b):
        axis, stride, size = ring
        return (t if axis == "tm" else b) // stride % size

    def turned(ring, by, t, b):
        axis, stride, size = ring
        here = digit_of(ring, t, b)
        by = ((here + by) % size - here) * stride
        to = (t + by, b) if axis == "tm" else (t, b + by)
        return (t * batch + b, to[0] * batch + to[1])

    out = []
    for n in range(len(rings)):
        own = [rings[(n + f) % len(rings)] for f in first_of]
        size = own[0][2]
        turns = [[turned(own[t % 2], s, t, b) for t, b in devices] for s in range(1, size)]
        digit = jnp.where(me[0] % 2 == 0, digit_of(own[0], *me), digit_of(own[1], *me))
        out.append((turns, digit))
    return out


def piece(value, index, count):
    rows = value.shape[0] // count
    return lax.dynamic_slice_in_dim(value, lax.rem(index, count) * rows, rows, 0)


def added(mine, got):
    if len(got) == 1:
        return mine + got[0]
    return (mine + got[1]) + (got[0] + got[2])


def gathered(mine, got, digit):
    count, rows = len(got) + 1, mine.shape[0]
    out = jnp.zeros((count * rows, mine.shape[1]), mine.dtype)
    for s, part in enumerate([mine] + got):
        at = lax.rem(digit - s + count, count) * rows
        out = lax.dynamic_update_slice_in_dim(out, part, at, 0)
    return out


def sum_all(value):
    tm, batch = lax.axis_size("tm"), lax.axis_size("batch")
    core = lax.axis_index("tm") % 2
    swap = [(t * batch + b, (t ^ 1) * batch + b) for t in range(tm) for b in range(batch)]
    plan = plan_of(FIRST)
    value = piece(value, core, 2) + lax.ppermute(piece(value, core + 1, 2), AXES, swap)
    for n, (turns, digit) in enumerate(plan):
        count = len(turns) + 1
        if n < SCATTER:
            got = [
                lax.ppermute(piece(value, digit + s + 1, count), AXES, turn)
                for s, turn in enumerate(turns)
            ]
            value = added(piece(value, digit, count), got)
        else:
            value = added(value, [lax.ppermute(value, AXES, turn) for turn in turns])
    for turns, digit in plan[:SCATTER][::-1]:
        value = gathered(value, [lax.ppermute(value, AXES, turn) for turn in turns], digit)
    return gathered(value, [lax.ppermute(value, AXES, swap)], core)


def on_device(
    frames, clip_start, code_ids, cotangent,
    enc_conv, enc_conv_bias, enc_proj, enc_proj_bias, downscale_weight, downscale_bias,
    codebook, up_weight, up_bias, dec_conv, dec_conv_bias, dec_proj, dec_proj_bias,
):
    frames = frames.reshape(CH, CORE)
    cotangent = cotangent.reshape(CH, CORE)
    front, tail = local_pack(frames, cotangent, clip_start, code_ids)
    count = lax.axis_size("tm")
    ring = [(i, (i + 1) % count) for i in range(count)]
    lo = lax.ppermute(tail, "tm", ring)
    hi = lax.ppermute(front, "tm", [(j, i) for i, j in ring])
    enc_w, dec_w, bias, cbt, chosen = local_prep(
        enc_conv, enc_conv_bias, enc_proj, enc_proj_bias,
        downscale_weight, downscale_bias.reshape(1, CH),
        codebook.T, up_weight, up_bias.reshape(1, CH),
        dec_conv, dec_conv_bias, dec_proj, dec_proj_bias, code_ids,
    )
    rebuilt, quant_grad, dec_grads, mf, mb, mh, mhb, chosen = local_decode(
        cotangent, lo, hi, clip_start, chosen, cbt, dec_w, bias
    )
    frames_grad, sums = local_encode(
        frames, lo, hi, code_ids, quant_grad, dec_grads, chosen, mf, mb, mh, mhb,
        enc_w, bias,
    )
    out = list(local_unpack(sum_all(sums)))
    cg = out.pop(0).T
    out[5] = out[5].reshape(CH)
    out[7] = out[7].reshape(CH)
    out.insert(6, cg)
    return (rebuilt[None], frames_grad[None], *out)


def solution(mesh):
    split_spec = P("batch", None, "tm")
    row_spec = P("batch", "tm")
    return jax.shard_map(
        on_device,
        mesh=mesh,
        in_specs=(split_spec, row_spec, row_spec, split_spec) + (P(),) * 13,
        out_specs=(split_spec, split_spec) + (P(),) * 13,
        check_vma=False,
    )
```

```python
import functools

import jax
import jax.numpy as jnp
from jax import lax
from jax.experimental import pallas as pl
from jax.experimental.pallas import tpu as pltpu
from jax.sharding import PartitionSpec as P

COMMIT = 0.02
DILATIONS = (1, 3, 9, 27)
BF = jnp.bfloat16
F32 = jnp.float32
CH = 64
CODES = 2048
CORE = 4096
HALO = 128
EXT = CORE + 2 * HALO
HCORE = CORE // 2
HEXT = EXT // 2
G0 = 0.7978845608028654
G1 = G0 * 0.044715
MB = 2**20
GRAD_PROJ = 384
GRAD_PAIR = 512
GRAD_BIAS = 640
GRAD_ROWS = 704
CODE_ROWS = CODES // 2
DEC_CUT = 192
SUM_ROWS = CODE_ROWS + DEC_CUT


BLOCK_ROWS = 448
PAIR_AT = 4 * BLOCK_ROWS
WEIGHT_ROWS = PAIR_AT + 384


PARTS = {"conv": (0, 192), "conv_back": (192, 128), "proj": (320, 64), "proj_back": (384, 64)}


def part_rows(name, b):
    first, rows = PARTS[name]
    return slice(BLOCK_ROWS * b + first, BLOCK_ROWS * b + first + rows)


def part(w, name, b):
    return w[part_rows(name, b), :192]


def dot(a, b):
    return jnp.dot(a, b, preferred_element_type=F32)


def dot_nt(a, b):
    return lax.dot_general(a, b, (((1,), (1,)), ((), ())), preferred_element_type=F32)


def split(v):
    hi = v.astype(BF)
    return hi, (v - hi.astype(F32)).astype(BF)


def gelu_both(v):
    s = v * v
    t = jnp.tanh(v * (G0 + G1 * s))
    cdf = 0.5 + 0.5 * t
    slope = cdf + (0.5 * v) * (1.0 - t * t) * (G0 + (3.0 * G1) * s)
    return v * cdf, slope


def tile_rows(rows, times):
    return jnp.concatenate([rows] * times, axis=0)


def aligned(start):
    return start if isinstance(start, int) else pl.multiple_of(start, 128)


def lanes(ref, start, size, rows=slice(None)):
    return ref[rows, pl.ds(aligned(start), size)]


def wrap(start, length):
    return start % length if isinstance(start, int) else lax.rem(start + length, length)


def from_left(ref, rows, start, size, offset, length):
    if size == length:
        return pltpu.roll(lanes(ref, 0, length, rows), offset, 1)
    win = jnp.concatenate(
        [lanes(ref, wrap(start - 128, length), 128, rows), lanes(ref, start, size, rows)], axis=1
    )
    return pltpu.roll(win, offset, 1)[:, 128:]


def from_right(ref, rows, start, size, offset, length):
    if size == length:
        return pltpu.roll(lanes(ref, 0, length, rows), length - offset, 1)
    win = jnp.concatenate(
        [lanes(ref, start, size, rows), lanes(ref, wrap(start + size, length), 128, rows)], axis=1
    )
    return pltpu.roll(win, size + 128 - offset, 1)[:, :size]


def sweep(fn):
    fn(0, EXT, True)


def half_sweep(fn):
    fn(0, HEXT, True)


def apart(fn):
    pl.when(lax.axis_index("tm") >= 0)(fn)


def lane_fold(v):
    out = v[:, :128]
    for i in range(1, v.shape[1] // 128):
        out = out + v[:, i * 128 : (i + 1) * 128]
    return out


def selector():
    row = lax.broadcasted_iota(jnp.int32, (256, 256), 0)
    col = lax.broadcasted_iota(jnp.int32, (256, 256), 1)
    source = jnp.where(col < 128, 2 * col, 2 * (col - 128) + 1)
    return jnp.where(row == source, 1.0, 0.0).astype(BF)


def pack_kernel(frames, cot, clip, codes, front, tail, clip_v, codes_v, sems):
    first, final = slice(0, HALO), slice(CORE - HALO, CORE)
    copies = [
        pltpu.make_async_copy(src, dst, sems.at[n])
        for n, (src, dst) in enumerate(
            (
                (frames.at[:, first], front.at[:CH]),
                (frames.at[:, final], tail.at[:CH]),
                (cot.at[:, first], front.at[CH : 2 * CH]),
                (cot.at[:, final], tail.at[CH : 2 * CH]),
                (clip, clip_v),
                (codes, codes_v),
            )
        )
    ]
    for copy in copies:
        copy.start()
    for copy in copies:
        copy.wait()
    me = lax.axis_index("tm")
    count = lax.axis_size("tm")
    lane = lax.broadcasted_iota(jnp.int32, (1, HALO), 1)
    blank = jnp.zeros((6, HALO), F32)
    for out, cut, at_end, half, keep in (
        (front, first, me == 0, slice(0, HALO), lane < 64),
        (tail, final, me == count - 1, slice(HCORE - HALO, HCORE), lane >= 64),
    ):
        clip_row = jnp.where(at_end, -1.0, clip_v[:, cut].astype(F32))
        code_row = jnp.where(keep, codes_v[:, half].astype(F32), 0.0)
        out[2 * CH :, :] = jnp.concatenate([clip_row, code_row, blank], axis=0)


def prep_kernel(*refs):
    sources, outs, scratch = refs[:14], refs[14:19], refs[19:]
    cb, codes = refs[6], refs[13]
    sems = scratch[-1]
    copies = [
        pltpu.make_async_copy(src, dst, sems.at[n])
        for n, (src, dst) in enumerate(zip(sources, scratch[:14]))
    ]
    for n in (*range(6), *range(7, 13)):
        copies[n].start()
    ec, ecb, ep, epb, dw, db, _, uw, ub, dc, dcb, dp, dpb = scratch[:13]
    enc_w, dec_w, bias, cbt, chosen = outs

    def forms(w):
        hi, lo = split(w)
        return jnp.concatenate([hi, hi, lo], axis=1)

    def stacked(w):
        hi, lo = split(w)
        return jnp.concatenate([hi, lo], axis=0)

    def column(row):
        return jnp.broadcast_to(row, (128, CH)).T

    cbt[...] = stacked(cb[...])
    pick(codes, cbt, chosen, 0, HCORE, 1024)
    for n in (*range(6), *range(7, 13)):
        copies[n].wait()
    for n, (conv, cbias, proj, pbias) in enumerate(((ec, ecb, ep, epb), (dc, dcb, dp, dpb))):
        weights = (enc_w, dec_w)[n]
        for b in range(4):
            at = 4 * n + b
            weights[part_rows("conv", b), :192] = forms(conv[b].reshape(3 * CH, CH))
            weights[part_rows("conv_back", b), :192] = stacked(jnp.concatenate([conv[b, k].T for k in range(3)], axis=1))
            weights[part_rows("proj", b), :192] = forms(proj[b])
            weights[part_rows("proj_back", b), :192] = forms(proj[b].T)
            bias[2 * at] = column(cbias[b : b + 1, :])
            bias[2 * at + 1] = column(pbias[b : b + 1, :])
    bias[16] = column(db[...])
    bias[17] = column(ub[...])
    enc_w[PAIR_AT : PAIR_AT + 128, :] = stacked(jnp.concatenate([dw[k] for k in range(4)], axis=1))
    enc_w[PAIR_AT + 128 :, :192] = forms(jnp.concatenate([dw[k].T for k in range(4)], axis=0))
    dec_w[PAIR_AT : PAIR_AT + 128, :] = stacked(jnp.concatenate([uw[k].T for k in range(4)], axis=1))
    dec_w[PAIR_AT + 128 :, :192] = forms(jnp.concatenate([uw[k] for k in range(4)], axis=0))


def one_hot(ids_row, first, count):
    row = lax.broadcasted_iota(jnp.int32, (count, ids_row.shape[1]), 0) + first
    return jnp.where(row == ids_row, 1.0, 0.0).astype(BF)


def pick(ids, cbt, chosen, begin, end, step):
    for start in range(begin, end, step):
        at = slice(start - begin, start - begin + step)
        to = slice(start, start + step)
        both = dot(cbt[...], one_hot(ids[0:1, at], 0, CODES))
        chosen[:, to] = both[:CH] + both[CH:]


def stack_forward(x_ref, z_refs, blocks, dils, w, bias, mf, keep, last):
    def enter(value, start, size, b):
        act, slope = gelu_both(value)
        hi, lo = split(act)
        a_ref, gx_ref, _, _ = keep(b)
        a_ref[:CH, pl.ds(aligned(start), size)] = hi
        a_ref[CH:, pl.ds(aligned(start), size)] = lo
        gx_ref[:, pl.ds(aligned(start), size)] = slope
        z_refs[b % 2][:, pl.ds(aligned(start), size)] = dot(
            part(w, "conv", b), jnp.concatenate([hi, lo, hi], axis=0)
        )

    def first(start, size, core):
        enter(lanes(x_ref, start, size), start, size, 0)

    sweep(first)
    for b in range(4):
        d = dils[b]
        m = DILATIONS.index(d)
        z_ref = z_refs[b % 2]

        def step(start, size, core, b=b, d=d, m=m, z_ref=z_ref):
            _, _, u_ref, gh_ref = keep(b)
            times = size // 128
            left = tile_rows(lanes(mf, start, size, slice(16 * m, 16 * m + 8)), 8)
            right = tile_rows(lanes(mf, start, size, slice(16 * m + 8, 16 * m + 16)), 8)
            cb = jnp.concatenate([bias[2 * (blocks + b)]] * times, axis=1)
            hidden = lanes(z_ref, start, size, slice(CH, 2 * CH)) + cb
            hidden = hidden + left * from_left(z_ref, slice(0, CH), start, size, d, EXT)
            hidden = hidden + right * from_right(z_ref, slice(2 * CH, 3 * CH), start, size, d, EXT)
            act, slope = gelu_both(hidden)
            hi, lo = split(act)
            u_ref[:CH, pl.ds(aligned(start), size)] = hi
            u_ref[CH:, pl.ds(aligned(start), size)] = lo
            gh_ref[:, pl.ds(aligned(start), size)] = slope
            pbias = jnp.concatenate([bias[2 * (blocks + b) + 1]] * times, axis=1)
            out = (
                lanes(x_ref, start, size)
                + dot(part(w, "proj", b), jnp.concatenate([hi, lo, hi], axis=0))
                + pbias
            )
            if b < 3:
                x_ref[:, pl.ds(aligned(start), size)] = out
                enter(out, start, size, b + 1)
            else:
                last(out, start, size, core)

        sweep(step)


def stack_backward(g_ref, gh_refs, blocks, dils, w, mb, keep, acc, finish, last):
    dk1, dk2, dpa, csum, psum = acc

    def enter(grad, start, size, core, b):
        _, _, u_ref, slope_ref = keep(b)
        hi, lo = split(grad)
        q = dot(part(w, "proj_back", b), jnp.concatenate([hi, lo, hi], axis=0))
        gh = lanes(slope_ref, start, size) * q
        ghi, glo = split(gh)
        gh_refs[b % 2][:CH, pl.ds(aligned(start), size)] = ghi
        gh_refs[b % 2][CH:, pl.ds(aligned(start), size)] = glo
        if core:
            both = jnp.concatenate([hi, lo], axis=0)[:, :CORE]
            dpa[b] = dot_nt(both, lanes(u_ref, 0, CORE))
            csum[b] = lane_fold(gh[:, :CORE])
            psum[b] = lane_fold(grad[:, :CORE])

    def first(start, size, core):
        enter(lanes(g_ref, start, size), start, size, core, 3)

    sweep(first)
    for b in (3, 2, 1, 0):
        d = dils[b]
        m = DILATIONS.index(d)
        gh_ref = gh_refs[b % 2]

        def step(start, size, core, b=b, d=d, m=m, gh_ref=gh_ref):
            a_ref, gx_ref, _, _ = keep(b)
            left = tile_rows(lanes(mb, start, size, slice(32 * m, 32 * m + 16)), 4)
            right = tile_rows(lanes(mb, start, size, slice(32 * m + 16, 32 * m + 32)), 4)
            parts = []
            for rows in (slice(0, CH), slice(CH, 2 * CH)):
                parts.append(
                    jnp.concatenate(
                        [
                            from_right(gh_ref, rows, start, size, d, EXT) * right,
                            lanes(gh_ref, start, size, rows),
                            from_left(gh_ref, rows, start, size, d, EXT) * left,
                        ],
                        axis=0,
                    )
                )
            ghi, glo = parts
            both = dot(part(w, "conv_back", b), ghi)
            ga = both[:CH] + both[CH:] + dot(part(w, "conv_back", b)[:CH], glo)
            if core:
                act = lanes(a_ref, 0, CORE)
                dk1[b] = dot_nt(ghi[:, :CORE], act)
                dk2[b] = dot_nt(glo[:, :CORE], act[:CH])
            out = lanes(g_ref, start, size) + lanes(gx_ref, start, size) * ga
            if b > 0:
                g_ref[:, pl.ds(aligned(start), size)] = out
                enter(out, start, size, core, b - 1)
            else:
                last(out, start, size, core)

        sweep(step)
    for b in range(4):
        dk = dk1[b, :, :CH] + dk1[b, :, CH:] + dk2[b]
        dp = dpa[b, :CH, :CH] + dpa[b, CH:, :CH] + dpa[b, :CH, CH:]
        finish(b, dk, dp, csum[b], psum[b])


def store_grads(grads, folded):
    kept = {}

    def finish(b, dk, dp, csum, psum):
        kept[b] = (dk, dp)
        if b % 2:
            at = b // 2
            grads[at * 192 : (at + 1) * 192, :] = jnp.concatenate([kept[b - 1][0], dk], axis=1)
            grads[GRAD_PROJ + at * CH : GRAD_PROJ + (at + 1) * CH, :] = jnp.concatenate(
                [kept[b - 1][1], dp], axis=1
            )
        folded.extend([csum, psum])

    return finish


def store_columns(grads, folded):
    lane = lax.broadcasted_iota(jnp.int32, (CH, 128), 1)
    totals = [jnp.sum(v, axis=1, keepdims=True) for v in folded]
    out = jnp.zeros((CH, 128), F32)
    for at, total in enumerate(totals):
        out = jnp.where(lane == at, total, out)
    grads[GRAD_BIAS:, :] = out


def to_halves(value, sel, e_ref, o_ref, start, size):
    hi, lo = split(value)
    both = jnp.concatenate([hi, lo], axis=0)
    half = start // 2
    for i in range(size // 256):
        out = dot(both[:, i * 256 : (i + 1) * 256], sel).astype(BF)
        e_ref[:, pl.ds(aligned(half + i * 128), 128)] = out[:, :128]
        o_ref[:, pl.ds(aligned(half + i * 128), 128)] = out[:, 128:]


def pair_stack(e_ref, o_ref, mhb, start, size):
    masks = [tile_rows(lanes(mhb, start, size, slice(16 * i, 16 * i + 16)), 4) for i in range(3)]
    parts = []
    for rows in (slice(0, CH), slice(CH, 2 * CH)):
        parts.append(
            jnp.concatenate(
                [
                    from_left(o_ref, rows, start, size, 1, HEXT) * masks[0],
                    lanes(e_ref, start, size, rows),
                    lanes(o_ref, start, size, rows) * masks[1],
                    from_right(e_ref, rows, start, size, 1, HEXT) * masks[2],
                ],
                axis=0,
            )
        )
    return parts


def pair_gather(w, parts):
    both = dot(w[...], parts[0])
    return both[:CH] + both[CH:] + dot(w[:CH], parts[1])


def spread(w, hl_ref, mh, z_refs, sel, bias_tile, x_ref):
    def first(start, size, core):
        both = lanes(hl_ref, start, size)
        z = dot(w, jnp.concatenate([both, both[:CH]], axis=0))
        masks = [tile_rows(lanes(mh, start, size, slice(8 * i, 8 * i + 8)), 8) for i in range(3)]
        at = pl.ds(aligned(start), size)
        z_refs[0][:, at] = z[0:64] * masks[0]
        z_refs[1][:, at] = z[64:128]
        z_refs[2][:, at] = z[128:192] * masks[1]
        z_refs[3][:, at] = z[192:256] * masks[2]

    half_sweep(first)

    def second(start, size, core):
        every = slice(None)
        even = lanes(z_refs[1], start, size) + from_left(z_refs[3], every, start, size, 1, HEXT)
        odd = lanes(z_refs[2], start, size) + from_right(z_refs[0], every, start, size, 1, HEXT)
        ehi, elo = split(even)
        ohi, olo = split(odd)
        for i in range(size // 128):
            cut = slice(i * 128, (i + 1) * 128)
            rows = jnp.concatenate(
                [
                    jnp.concatenate([ehi[:, cut], ohi[:, cut]], axis=1),
                    jnp.concatenate([elo[:, cut], olo[:, cut]], axis=1),
                ],
                axis=0,
            )
            out = dot_nt(rows, sel)
            out = out[:CH] + out[CH:]
            if bias_tile is not None:
                out = out + jnp.concatenate([bias_tile, bias_tile], axis=1)
            x_ref[:, pl.ds(aligned(2 * start + 256 * i), 256)] = out

    half_sweep(second)


def ring_fill(ref, core, hi, lo):
    if core is not None:
        ref[:, :CORE] = core
    ref[:, CORE : CORE + HALO] = hi
    ref[:, CORE + HALO :] = lo


def find_links(clip_ref, sel, mf, mb, mh, mhb):
    def links(start, size, core):
        at = pl.ds(aligned(start), size)
        here = lanes(clip_ref, start, size)

        def same(other):
            return jnp.where(other == here, 1.0, 0.0)

        for m, d in enumerate(DILATIONS):
            left = same(from_left(clip_ref, slice(None), start, size, d, EXT))
            right = same(from_right(clip_ref, slice(None), start, size, d, EXT))
            mf[16 * m : 16 * m + 8, at] = left
            mf[16 * m + 8 : 16 * m + 16, at] = right
            mb[32 * m : 32 * m + 16, at] = tile_rows(left, 2).astype(BF)
            mb[32 * m + 16 : 32 * m + 32, at] = tile_rows(right, 2).astype(BF)
            if m == 0:
                two = same(from_right(clip_ref, slice(None), start, size, 2, EXT))
                rows = jnp.concatenate([left, right, two, two], axis=0).astype(BF)
                half = start // 2
                for i in range(size // 256):
                    out = dot(rows[:, i * 256 : (i + 1) * 256], sel)[:, :128]
                    hat = pl.ds(aligned(half + 128 * i), 128)
                    mh[:, hat] = out[:24]
                    for n in range(3):
                        mhb[16 * n : 16 * n + 16, hat] = tile_rows(
                            out[8 * n : 8 * n + 8], 2
                        ).astype(BF)

    sweep(links)


def sum_refs():
    return [
        pltpu.VMEM((4, 3 * CH, 2 * CH), F32),
        pltpu.VMEM((4, 3 * CH, CH), F32),
        pltpu.VMEM((4, 2 * CH, 2 * CH), F32),
        pltpu.VMEM((4, CH, 128), F32),
        pltpu.VMEM((4, CH, 128), F32),
    ]


def state_refs():
    return [
        whole(),
        whole(rows=192),
        whole(rows=192),
        pltpu.VMEM((4, 128, EXT), BF),
        pltpu.VMEM((4, CH, EXT), F32),
        pltpu.VMEM((4, 128, EXT), BF),
        pltpu.VMEM((4, CH, EXT), F32),
        whole(),
        whole(BF, 128),
        whole(BF, 128),
        halves(),
        halves(),
        *sum_refs(),
    ]


def decode_kernel(
    cot, lo, hi, clip, chosen_in, cbt, weights, bias,
    rebuilt, quant_grad, grads, mf, mb, mh, mhb, chosen, chosen_hl, ids,
    up1, up2, usum, clip_ref, sems, x_ref, z0, z1, a_s, gx_s, u_s, gh_s, g_ref, g0, g1, e_ref, o_ref,
    *acc,
):
    ug = weights.at[PAIR_AT : PAIR_AT + 128]
    us = weights.at[PAIR_AT + 128 :]
    cot_in = pltpu.make_async_copy(cot, g_ref.at[:, :CORE], sems.at[0])
    cot_in.start()
    sel = selector()
    ring_fill(
        clip_ref,
        jnp.broadcast_to(clip[...].astype(F32), (8, CORE)),
        jnp.broadcast_to(hi[128:129], (8, HALO)),
        jnp.broadcast_to(lo[128:129], (8, HALO)),
    )
    apart(lambda: find_links(clip_ref, selector(), mf, mb, mh, mhb))
    chosen[:, :HCORE] = chosen_in[...]
    ids[...] = jnp.broadcast_to((hi[129:130] + lo[129:130]).astype(jnp.int32), (8, HALO))
    pick(ids, cbt, chosen, HCORE, HEXT, HALO)
    chi, clo = split(chosen[...])
    chosen_hl[:CH] = chi
    chosen_hl[CH:] = clo
    zu = [z0.at[:CH], z0.at[CH : 2 * CH], z0.at[2 * CH :], z1.at[:CH]]
    apart(lambda: spread(us[:, :192], chosen_hl, mh, zu, selector(), bias[17], x_ref))

    def keep(b):
        return a_s.at[b], gx_s.at[b], u_s.at[b], gh_s.at[b]

    def last(out, start, size, core):
        if core:
            x_ref[:, :CORE] = out[:, :CORE]

    order = DILATIONS[::-1]
    apart(lambda: stack_forward(x_ref, (z0, z1), 4, order, weights, bias, mf, keep, last))
    rebuilt_out = pltpu.make_async_copy(x_ref.at[:, :CORE], rebuilt, sems.at[1])
    rebuilt_out.start()
    cot_in.wait()
    ring_fill(g_ref, None, hi[CH : 2 * CH], lo[CH : 2 * CH])
    @apart
    def _():
        folded = []
        take = selector()

        def last_back(out, start, size, core):
            to_halves(out, take, e_ref, o_ref, start, size)
            if core:
                usum[...] = lane_fold(out[:, :CORE])

        stack_backward(
            g_ref, (g0, g1), 4, order, weights, mb, keep, acc, store_grads(grads, folded), last_back
        )
        store_columns(grads, folded + [usum[...]])

    def up(start, size, core):
        parts = pair_stack(e_ref, o_ref, mhb, start, size)
        quant_grad[:, pl.ds(aligned(start), size)] = pair_gather(ug, parts)
        if core:
            both = lanes(chosen_hl, 0, HCORE)
            up1[...] = dot_nt(parts[0][:, :HCORE], both)
            up2[...] = dot_nt(parts[1][:, :HCORE], both[:CH])

    half_sweep(up)
    total = up1[:, :CH] + up1[:, CH:] + up2[...]
    grads[GRAD_PAIR:GRAD_BIAS, :] = jnp.concatenate([total[: 2 * CH], total[2 * CH :]], axis=1)
    rebuilt_out.wait()


def encode_kernel(
    frames, lo, hi, codes, quant_grad, dec_grads, chosen, mf, mb, mh, mhb, weights, bias,
    frames_grad, all_sums,
    d_ref, l_ref, down1, down2, dsum, sems,
    x_ref, z0, z1, a_s, gx_s, u_s, gh_s, g_ref, g0, g1, e_ref, o_ref, *acc,
):
    dg = weights.at[PAIR_AT : PAIR_AT + 128]
    ds_ = weights.at[PAIR_AT + 128 :]
    ring_fill(x_ref, frames[...], hi[:CH], lo[:CH])
    sums, sums_b = all_sums.at[:SUM_ROWS], all_sums.at[SUM_ROWS:]
    grads = sums_b.at[GRAD_ROWS - DEC_CUT :]
    sums[CODE_ROWS:, :] = dec_grads[:DEC_CUT, :]
    sums_b[: GRAD_ROWS - DEC_CUT, :] = dec_grads[DEC_CUT:, :]

    def keep(b):
        return a_s.at[b], gx_s.at[b], u_s.at[b], gh_s.at[b]

    @apart
    def _():
        take = selector()

        def last(out, start, size, core):
            to_halves(out, take, e_ref, o_ref, start, size)

        stack_forward(x_ref, (z0, z1), 0, DILATIONS, weights, bias, mf, keep, last)

    folded = []

    def down(start, size, core):
        at = pl.ds(aligned(start), size)
        parts = pair_stack(e_ref, o_ref, mhb, start, size)
        value = pair_gather(dg, parts) + jnp.concatenate([bias[16]] * (size // 128), axis=1)
        gap = value - lanes(chosen, start, size)
        grad = quant_grad[:, at] + (2.0 * COMMIT) * gap
        hi, lo = split(grad)
        l_ref[:CH, at] = hi
        l_ref[CH:, at] = lo
        if core:
            dhi, dlo = split(-2.0 * gap[:, :HCORE])
            d_ref[:CH, :] = dhi
            d_ref[CH:, :] = dlo
            dsum[...] = lane_fold(grad[:, :HCORE])
            both = jnp.concatenate([hi, lo], axis=0)
            down1[...] = dot_nt(both[:, :HCORE], parts[0][:, :HCORE])
            down2[...] = dot_nt(hi[:, :HCORE], parts[1][:, :HCORE])

    apart(lambda: half_sweep(down))

    @apart
    def _():
        for i in range(CODES // 512):
            out = dot_nt(d_ref[...], one_hot(codes[...], i * 512, 512))
            out = out[:CH] + out[CH:]
            for n in range(4):
                at = i * 256 + CH * n
                sums[at : at + CH, :] = out[:, 128 * n : 128 * (n + 1)]

    zu = [z0.at[:CH], z0.at[CH : 2 * CH], z0.at[2 * CH :], z1.at[:CH]]
    apart(lambda: spread(ds_[:, :192], l_ref, mh, zu, selector(), None, g_ref))

    @apart
    def _():
        folded = []
        leaving = []

        def last_back(out, start, size, core):
            if core:
                at = slice(0, CORE)
                x_ref[:, at] = out[:, at]
                leaving.append(
                    pltpu.make_async_copy(
                        x_ref.at[:, at], frames_grad.at[:, at], sems.at[len(leaving)]
                    )
                )
                leaving[-1].start()

        stack_backward(
            g_ref, (g0, g1), 0, DILATIONS, weights, mb, keep, acc, store_grads(grads, folded), last_back
        )
        total = down1[:CH] + down1[CH:] + down2[...]
        grads[GRAD_PAIR : GRAD_PAIR + CH, :] = total[:, : 2 * CH]
        grads[GRAD_PAIR + CH : GRAD_BIAS, :] = total[:, 2 * CH :]
        store_columns(grads, folded + [dsum[...]])
        for copy in leaving:
            copy.wait()


def unpack_kernel(
    all_sums,
    cg, ec, ecb, ep, epb, dw, db, uw, ub, dc, dcb, dp, dpb,
):
    sums, sums_b = all_sums.at[:SUM_ROWS], all_sums.at[SUM_ROWS:]
    for i in range(CODES // 128):
        cg[:, i * 128 : (i + 1) * 128] = sums[i * CH : (i + 1) * CH, :]

    def enc(first, rows):
        at = GRAD_ROWS - DEC_CUT + first
        return sums_b[at : at + rows, :]

    def dec(first, rows):
        if first < DEC_CUT:
            return sums[CODE_ROWS + first : CODE_ROWS + first + rows, :]
        return sums_b[first - DEC_CUT : first - DEC_CUT + rows, :]

    for src, conv, cbias, proj, pbias, single in (
        (enc, ec, ecb, ep, epb, db),
        (dec, dc, dcb, dp, dpb, ub),
    ):
        rows = src(GRAD_BIAS, CH).T
        for b in range(4):
            at = slice((b % 2) * CH, (b % 2 + 1) * CH)
            p = b // 2
            conv[b] = src(p * 192, 192)[:, at].reshape(3, CH, CH)
            proj[b] = src(GRAD_PROJ + p * CH, CH)[:, at]
            cbias[b : b + 1, :] = rows[2 * b : 2 * b + 1]
            pbias[b : b + 1, :] = rows[2 * b + 1 : 2 * b + 2]
        single[...] = rows[8:9]
    for k in range(4):
        a, b = k // 2, k % 2
        dw[k] = enc(GRAD_PAIR + a * CH, CH)[:, b * CH : (b + 1) * CH]
        uw[k] = dec(GRAD_PAIR + b * CH, CH)[:, a * CH : (a + 1) * CH]


def shape(dims, kind=F32):
    return jax.ShapeDtypeStruct(dims, kind)


def call(kernel, outs, scratch=(), flops=0, limit=46, in_specs=None, out_specs=None):
    extra = {}
    if in_specs is not None:
        extra["in_specs"] = in_specs
    if out_specs is not None:
        extra["out_specs"] = out_specs
    return pl.pallas_call(
        kernel,
        out_shape=outs,
        scratch_shapes=list(scratch),
        compiler_params=pltpu.CompilerParams(vmem_limit_bytes=limit * MB),
        cost_estimate=pl.CostEstimate(flops=flops, bytes_accessed=2**20, transcendentals=0),
        **extra,
    )


def halves(kind=BF, rows=2 * CH):
    return pltpu.VMEM((rows, HEXT), kind)


def whole(kind=F32, rows=CH):
    return pltpu.VMEM((rows, EXT), kind)


FAR = pl.BlockSpec(memory_space=pltpu.HBM)


def far(*values):
    return [pltpu.with_memory_space_constraint(v, pltpu.HBM) for v in values]
LOCAL = pl.BlockSpec()


def local_pack(frames, cot, clip, codes):
    return call(
        pack_kernel,
        [shape((136, HALO)), shape((136, HALO))],
        [
            pltpu.VMEM((1, CORE), jnp.int32),
            pltpu.VMEM((1, HCORE), jnp.int32),
            pltpu.SemaphoreType.DMA((6,)),
        ],
        in_specs=[FAR] * 4,
    )(*far(frames, cot, clip, codes))


def local_prep(*args):
    return call(
        prep_kernel,
        [
            shape((WEIGHT_ROWS, 256), BF),
            shape((WEIGHT_ROWS, 256), BF),
            shape((18, CH, 128)),
            shape((128, CODES), BF),
            shape((CH, HCORE)),
        ],
        [pltpu.VMEM(a.shape, a.dtype) for a in args] + [pltpu.SemaphoreType.DMA((14,))],
        flops=10**7,
        limit=46,
        in_specs=[LOCAL if n in (6, 13) else FAR for n in range(14)],
    )(*[v if n in (6, 13) else far(v)[0] for n, v in enumerate(args)])


def local_decode(cot, *args):
    return call(
        decode_kernel,
        [
            shape((CH, CORE)),
            shape((CH, HEXT)),
            shape((GRAD_ROWS, 128)),
            shape((64, EXT)),
            shape((128, EXT), BF),
            shape((24, HEXT)),
            shape((48, HEXT), BF),
            shape((CH, HEXT)),
        ],
        [
            halves(),
            pltpu.VMEM((8, HALO), jnp.int32),
            pltpu.VMEM((256, 128), F32),
            pltpu.VMEM((256, CH), F32),
            pltpu.VMEM((CH, 128), F32),
            whole(rows=8),
            pltpu.SemaphoreType.DMA((2,)),
            *state_refs(),
        ],
        flops=2 * 10**10,
        limit=46,
        in_specs=[FAR] + [LOCAL] * 7,
        out_specs=[FAR] + [LOCAL] * 7,
    )(*far(cot), *args)


def local_encode(*args):
    return call(
        encode_kernel,
        [shape((CH, CORE)), shape((2 * SUM_ROWS, 128))],
        [
            pltpu.VMEM((2 * CH, HCORE), BF),
            halves(),
            pltpu.VMEM((128, 256), F32),
            pltpu.VMEM((CH, 256), F32),
            pltpu.VMEM((CH, 128), F32),
            pltpu.SemaphoreType.DMA((1,)),
            *state_refs(),
        ],
        flops=2 * 10**10,
        limit=46,
        in_specs=[LOCAL] * 13,
        out_specs=[FAR, LOCAL],
    )(*args)


def local_unpack(sums):
    block = [shape((4, 3, CH, CH)), shape((4, CH)), shape((4, CH, CH)), shape((4, CH))]
    return call(
        unpack_kernel,
        [
            shape((CH, CODES)),
            *block,
            shape((4, CH, CH)),
            shape((1, CH)),
            shape((4, CH, CH)),
            shape((1, CH)),
            *block,
        ],
    )(sums)


AXES = ("tm", "batch")
FIRST = (0, 1)
SCATTER = 1


def plan_of(first_of):
    tm, batch = lax.axis_size("tm"), lax.axis_size("batch")
    rings = []
    stride = 2
    while stride < tm:
        size = min(4, tm // stride)
        rings.append(("tm", stride, size))
        stride *= size
    rings.append(("batch", 1, batch))
    devices = [(t, b) for t in range(tm) for b in range(batch)]
    me = (lax.axis_index("tm"), lax.axis_index("batch"))

    def digit_of(ring, t, b):
        axis, stride, size = ring
        return (t if axis == "tm" else b) // stride % size

    def turned(ring, by, t, b):
        axis, stride, size = ring
        here = digit_of(ring, t, b)
        by = ((here + by) % size - here) * stride
        to = (t + by, b) if axis == "tm" else (t, b + by)
        return (t * batch + b, to[0] * batch + to[1])

    out = []
    for n in range(len(rings)):
        own = [rings[(n + f) % len(rings)] for f in first_of]
        size = own[0][2]
        turns = [[turned(own[t % 2], s, t, b) for t, b in devices] for s in range(1, size)]
        digit = jnp.where(me[0] % 2 == 0, digit_of(own[0], *me), digit_of(own[1], *me))
        out.append((turns, digit))
    return out


def piece(value, index, count):
    rows = value.shape[0] // count
    return lax.dynamic_slice_in_dim(value, lax.rem(index, count) * rows, rows, 0)


def added(mine, got):
    if len(got) == 1:
        return mine + got[0]
    return (mine + got[1]) + (got[0] + got[2])


def gathered(mine, got, digit):
    count, rows = len(got) + 1, mine.shape[0]
    out = jnp.zeros((count * rows, mine.shape[1]), mine.dtype)
    for s, part in enumerate([mine] + got):
        at = lax.rem(digit - s + count, count) * rows
        out = lax.dynamic_update_slice_in_dim(out, part, at, 0)
    return out


def sum_all(value):
    tm, batch = lax.axis_size("tm"), lax.axis_size("batch")
    core = lax.axis_index("tm") % 2
    swap = [(t * batch + b, (t ^ 1) * batch + b) for t in range(tm) for b in range(batch)]
    plan = plan_of(FIRST)
    value = piece(value, core, 2) + lax.ppermute(piece(value, core + 1, 2), AXES, swap)
    for n, (turns, digit) in enumerate(plan):
        count = len(turns) + 1
        if n < SCATTER:
            got = [
                lax.ppermute(piece(value, digit + s + 1, count), AXES, turn)
                for s, turn in enumerate(turns)
            ]
            value = added(piece(value, digit, count), got)
        else:
            value = added(value, [lax.ppermute(value, AXES, turn) for turn in turns])
    for turns, digit in plan[:SCATTER][::-1]:
        value = gathered(value, [lax.ppermute(value, AXES, turn) for turn in turns], digit)
    return gathered(value, [lax.ppermute(value, AXES, swap)], core)


def on_device(
    frames, clip_start, code_ids, cotangent,
    enc_conv, enc_conv_bias, enc_proj, enc_proj_bias, downscale_weight, downscale_bias,
    codebook, up_weight, up_bias, dec_conv, dec_conv_bias, dec_proj, dec_proj_bias,
):
    frames = frames.reshape(CH, CORE)
    cotangent = cotangent.reshape(CH, CORE)
    front, tail = local_pack(frames, cotangent, clip_start, code_ids)
    count = lax.axis_size("tm")
    ring = [(i, (i + 1) % count) for i in range(count)]
    lo = lax.ppermute(tail, "tm", ring)
    hi = lax.ppermute(front, "tm", [(j, i) for i, j in ring])
    enc_w, dec_w, bias, cbt, chosen = local_prep(
        enc_conv, enc_conv_bias, enc_proj, enc_proj_bias,
        downscale_weight, downscale_bias.reshape(1, CH),
        codebook.T, up_weight, up_bias.reshape(1, CH),
        dec_conv, dec_conv_bias, dec_proj, dec_proj_bias, code_ids,
    )
    rebuilt, quant_grad, dec_grads, mf, mb, mh, mhb, chosen = local_decode(
        cotangent, lo, hi, clip_start, chosen, cbt, dec_w, bias
    )
    frames_grad, sums = local_encode(
        frames, lo, hi, code_ids, quant_grad, dec_grads, chosen, mf, mb, mh, mhb,
        enc_w, bias,
    )
    out = list(local_unpack(sum_all(sums)))
    cg = out.pop(0).T
    out[5] = out[5].reshape(CH)
    out[7] = out[7].reshape(CH)
    out.insert(6, cg)
    return (rebuilt[None], frames_grad[None], *out)


def solution(mesh):
    split_spec = P("batch", None, "tm")
    row_spec = P("batch", "tm")
    return jax.shard_map(
        on_device,
        mesh=mesh,
        in_specs=(split_spec, row_spec, row_spec, split_spec) + (P(),) * 13,
        out_specs=(split_spec, split_spec) + (P(),) * 13,
        check_vma=False,
    )
```
